32 devices in a mesh: dp: 16 (over z, y, core), mp: 2 (over x).
Axes of the slice: x: 2, y: 2, z: 4, core: 2. Of those that a mesh axis runs over, the one named last changes fastest.
Arguments:
- tokens: bfloat16 [2048, 1024], P('dp'), may hold values from -6 to 6
- memory: bfloat16 [16384, 1024], P('dp'), may hold values from -6 to 6
- mem_len: int32 [16], P('dp'), may hold values from 128 to 1024, as said below
- dec_len: int32 [16], P('dp'), may hold values from 16 to 128, as said below
- cotangent: bfloat16 [2048, 1024], P('dp'), may hold values from -6 to 6
- self_qkv: bfloat16 [1024, 3, 1024], P(None, None, 'mp'), may hold values from -0.1875 to 0.1875
- self_qv_bias: float32 [2, 1024], P(None, 'mp'), may hold values from -3 to 3
- self_out: bfloat16 [1024, 1024], P('mp'), may hold values from -0.75 to 0.75
- cross_q: bfloat16 [1024, 1024], P(None, 'mp'), may hold values from -0.1875 to 0.1875
- cross_kv: bfloat16 [1024, 2, 1024], P(None, None, 'mp'), may hold values from -0.1875 to 0.1875
- cross_qv_bias: float32 [2, 1024], P(None, 'mp'), may hold values from -3 to 3
- cross_out: bfloat16 [1024, 1024], P('mp'), may hold values from -1 to 1
- fc_in: bfloat16 [1024, 4096], P(None, 'mp'), may hold values from -0.1875 to 0.1875
- fc_in_bias: float32 [4096], P('mp'), may hold values from -3 to 3
- fc_out: bfloat16 [4096, 1024], P('mp'), may hold values from -0.09375 to 0.09375
- out_bias: float32 [3, 1024], replicated, may hold values from -3 to 3
- norm_gain: float32 [3, 1024], replicated, may hold values from 0.5 to 1.5
- norm_bias: float32 [3, 1024], replicated, may hold values from -3 to 3
Outputs:
- layer_out: bfloat16 [2048, 1024], P('dp')
- grad_tokens: bfloat16 [2048, 1024], P('dp')
- grad_memory: bfloat16 [16384, 1024], P(('dp', 'mp'))
- grad_self_qkv: float32 [1024, 3, 1024], P('dp', None, 'mp')
- grad_self_qv_bias: float32 [2, 1024], P(None, 'mp')
- grad_self_out: float32 [1024, 1024], P('mp', 'dp')
- grad_cross_q: float32 [1024, 1024], P('dp', 'mp')
- grad_cross_kv: float32 [1024, 2, 1024], P('dp', None, 'mp')
- grad_cross_qv_bias: float32 [2, 1024], P(None, 'mp')
- grad_cross_out: float32 [1024, 1024], P('mp', 'dp')
- grad_fc_in: float32 [1024, 4096], P('dp', 'mp')
- grad_fc_in_bias: float32 [4096], P('mp')
- grad_fc_out: float32 [4096, 1024], P('mp', 'dp')
- grad_out_bias: float32 [3, 1024], replicated
- grad_norm_gain: float32 [3, 1024], replicated
- grad_norm_bias: float32 [3, 1024], replicated
The draws below stay inside these ranges and needn't reach their ends.
Inputs may be any that keep to these rules, and one draw needn't show every extreme that they name: `mem_len`: an item's memory rows past its length are padding; some item has exactly 1024. `dec_len`: an item's decoder rows past its length are padding; some item has exactly 128.
All inputs are finite; a program needn't handle non-finite values.
Results may differ from the reference program's by a relative error of at most 0.023.
The reference program's roundings to bfloat16 on the way count: a program that leaves them out, or rounds other values in their place, can miss the bound.
Values may be sent and summed in bfloat16 or wider, within the bound.
A program may use at most 192 MiB of HBM per device.

```python
import jax
import jax.numpy as jnp
from jax import lax

D = 1024
HEADS = 16
FF = 4096
HEAD = 64
TLEN = 128
MLEN = 1024
ITEMS = 16


def ragged_lengths(key, longest):
    chosen_key, length_key = jax.random.split(key)
    lengths = jax.random.randint(length_key, (ITEMS,), longest // 8, longest + 1)
    chosen = jax.random.randint(chosen_key, (), 0, ITEMS)
    slots = jnp.arange(ITEMS)
    lengths = jnp.where(slots == chosen, longest, lengths)
    lengths = jnp.where(slots == (chosen + 1) % ITEMS, longest // 8, lengths)
    return lengths.astype(jnp.int32)


def draw_mem_len(key, part):
    key = jax.random.fold_in(key, 11)
    return ragged_lengths(key, MLEN)


def draw_dec_len(key, part):
    key = jax.random.fold_in(key, 23)
    return ragged_lengths(key, TLEN)


def block_scale(rng, shape, pieces, least, high):
    loudness = 1.0
    for axis_at, blocks in pieces:
        draws = jax.random.uniform(jax.random.fold_in(jax.random.fold_in(rng, 6), axis_at), (blocks,), jnp.float32, least / len(pieces), high / len(pieces))
        loudness = loudness * jnp.repeat(jnp.exp(draws), shape[axis_at] // blocks).reshape((-1,) + (1,) * (len(shape) - 1 - axis_at))
    return loudness


def noise(stream_key, shape, deviation, most, cuts=(), kind=jnp.bfloat16):
    array = deviation * jax.random.normal(stream_key, shape, jnp.float32)
    if cuts:
        array = array * block_scale(stream_key, shape, cuts, -0.22, 0.18)
    return jnp.clip(array, -most, most).astype(kind)


def setup_inputs(seed: int = 0) -> dict:
    key_list = jax.random.split(jax.random.key(seed), 19)
    tokens = noise(key_list[0], (ITEMS * TLEN, D), 1.0, 6.0, ((0, 16),))
    memory = noise(key_list[1], (ITEMS * MLEN, D), 1.0, 6.0, ((0, 16),))
    mem_len = draw_mem_len(jax.random.fold_in(key_list[18], 71), 0)
    dec_len = draw_dec_len(jax.random.fold_in(key_list[18], 71), 0)
    cotangent = noise(key_list[4], (ITEMS * TLEN, D), 1.0, 6.0, ((0, 16),))
    self_qkv = noise(key_list[5], (D, 3, D), D ** -0.5, 0.1875, ((2, 2),))
    self_qv_bias = noise(key_list[6], (2, D), 0.5, 3.0, ((1, 2),), jnp.float32)
    self_out = noise(key_list[7], (D, D), (D // 16) ** -0.5, 0.75, ((0, 2),))
    cross_q = noise(key_list[8], (D, D), D ** -0.5, 0.1875, ((1, 2),))
    cross_kv = noise(key_list[9], (D, 2, D), D ** -0.5, 0.1875, ((2, 2),))
    cross_qv_bias = noise(key_list[10], (2, D), 0.5, 3.0, ((1, 2),), jnp.float32)
    cross_out = noise(key_list[11], (D, D), (D // 32) ** -0.5, 1.0, ((0, 2),))
    fc_in = noise(key_list[12], (D, FF), D ** -0.5, 0.1875, ((1, 2),))
    fc_in_bias = noise(key_list[13], (FF,), 0.5, 3.0, ((0, 2),), jnp.float32)
    fc_out = noise(key_list[14], (FF, D), FF ** -0.5, 0.09375, ((0, 2),))
    out_bias = noise(key_list[15], (3, D), 0.5, 3.0, (), jnp.float32)
    norm_gain = jnp.clip(1.0 + 0.1 * jax.random.normal(key_list[16], (3, D), jnp.float32), 0.5, 1.5)
    norm_bias = noise(key_list[17], (3, D), 0.5, 3.0, (), jnp.float32)
    return dict(tokens=tokens, memory=memory, mem_len=mem_len, dec_len=dec_len, cotangent=cotangent, self_qkv=self_qkv, self_qv_bias=self_qv_bias, self_out=self_out, cross_q=cross_q, cross_kv=cross_kv, cross_qv_bias=cross_qv_bias, cross_out=cross_out, fc_in=fc_in, fc_in_bias=fc_in_bias, fc_out=fc_out, out_bias=out_bias, norm_gain=norm_gain, norm_bias=norm_bias)


@jax.custom_vjp
def low(v):
    return lax.optimization_barrier(v.astype(jnp.bfloat16)).astype(jnp.float32)

@jax.custom_vjp
def low_back(v):
    return v

def low_keep(v):
    return (low(v), None)

def low_pass(kept, grad):
    return (grad,)

def back_keep(v):
    return (v, None)

def back_low(kept, grad):
    return (low(grad),)
low.defvjp(low_keep, low_pass)
low_back.defvjp(back_keep, back_low)
highest = lax.Precision.HIGHEST
epsilon = 1e-05

def product(operand, weight):
    return jnp.dot(operand, weight, precision=highest, preferred_element_type=jnp.float32)

def normalize(inputs, gain_row, shift_row):
    row_mean = lax.optimization_barrier(jnp.mean(inputs, axis=-1, keepdims=True))
    centred = inputs - row_mean
    variance = lax.optimization_barrier(jnp.mean(centred * centred, axis=-1, keepdims=True))
    return centred * lax.rsqrt(variance + epsilon) * gain_row + shift_row

def gelu(inputs):
    return 0.5 * inputs * (1.0 + lax.erf(inputs * 0.7071067811865476))

def attend(query_in, key_in, value_in, allowed):
    query_rows = query_in.shape[0]
    key_rows = key_in.shape[0]
    heads_q = query_in.reshape(query_rows, HEADS, HEAD)
    heads_k = key_in.reshape(key_rows, HEADS, HEAD)
    heads_v = value_in.reshape(key_rows, HEADS, HEAD)
    scores = jnp.einsum('qhd,khd->hqk', heads_q, heads_k, precision=highest) * HEAD ** (-0.5)
    scores = jnp.where(allowed[None], low_back(scores), -1e+30)
    row_top = lax.optimization_barrier(jnp.max(scores, axis=-1, keepdims=True))
    weights = jnp.exp(scores - row_top)
    softmax_low = low(weights / lax.optimization_barrier(jnp.sum(weights, axis=-1, keepdims=True)))
    mixed = jnp.einsum('hqk,khd->qhd', softmax_low, heads_v, precision=highest)
    return mixed.reshape(query_rows, HEADS * HEAD)

def self_item(packed_args):
    query_in, key_in, value_in, length = packed_args
    position = jnp.arange(TLEN, dtype=jnp.int32)
    allowed = (position[None, :] <= position[:, None]) & (position[None, :] < length)
    return attend(query_in, key_in, value_in, allowed)

def cross_item(packed_args):
    query_in, key_in, value_in, length = packed_args
    position = jnp.arange(MLEN, dtype=jnp.int32)
    allowed = jnp.broadcast_to(position[None, :] < length, (TLEN, MLEN))
    return attend(query_in, key_in, value_in, allowed)

def forward(tokens, memory, self_qkv, self_qv_bias, self_out, cross_q, cross_kv, cross_qv_bias, cross_out, fc_in, fc_in_bias, fc_out, out_bias, norm_gain, norm_bias, mem_len, dec_len):
    zero_row = jnp.zeros((1, D), jnp.float32)
    packed = jnp.einsum('td,dcf->tcf', tokens, self_qkv, precision=highest)
    packed = packed + jnp.concatenate([self_qv_bias[:1], zero_row, self_qv_bias[1:]], axis=0)[None]
    packed = low(low_back(packed))
    item_shape = (ITEMS, TLEN, D)
    self_mixed = lax.map(jax.checkpoint(self_item), (packed[:, 0].reshape(item_shape), packed[:, 1].reshape(item_shape), packed[:, 2].reshape(item_shape), dec_len))
    self_mixed = low(low_back(self_mixed.reshape(ITEMS * TLEN, D)))
    branch = low_back(product(self_mixed, self_out) + out_bias[0])
    first_norm = normalize(tokens + branch, norm_gain[0], norm_bias[0])
    cross_query = low(low_back(product(low(first_norm), cross_q) + cross_qv_bias[0]))
    cross_pair = jnp.einsum('md,dcf->mcf', memory, cross_kv, precision=highest)
    cross_pair = low(low_back(cross_pair + jnp.concatenate([zero_row, cross_qv_bias[1:]], axis=0)[None]))
    memory_shape = (ITEMS, MLEN, D)
    cross_mixed = lax.map(jax.checkpoint(cross_item), (cross_query.reshape(item_shape), cross_pair[:, 0].reshape(memory_shape), cross_pair[:, 1].reshape(memory_shape), mem_len))
    cross_mixed = low(low_back(cross_mixed.reshape(ITEMS * TLEN, D)))
    branch = low_back(product(cross_mixed, cross_out) + out_bias[1])
    second_norm = normalize(first_norm + branch, norm_gain[1], norm_bias[1])
    hidden = low_back(product(low(second_norm), fc_in) + fc_in_bias)
    active = low(gelu(hidden))
    branch = low_back(product(active, fc_out) + out_bias[2])
    return normalize(second_norm + branch, norm_gain[2], norm_bias[2])

def reference(tokens, memory, mem_len, dec_len, cotangent, self_qkv, self_qv_bias, self_out, cross_q, cross_kv, cross_qv_bias, cross_out, fc_in, fc_in_bias, fc_out, out_bias, norm_gain, norm_bias):
    floats = [arr.astype(jnp.float32) for arr in (tokens, memory, self_qkv, self_qv_bias, self_out, cross_q, cross_kv, cross_qv_bias, cross_out, fc_in, fc_in_bias, fc_out, out_bias, norm_gain, norm_bias)]

    def layer(*inputs):
        return forward(*inputs, mem_len, dec_len)
    output, pull = jax.vjp(layer, *floats)
    position = jnp.arange(TLEN, dtype=jnp.int32)
    live_rows = (position[None, :] < dec_len[:, None]).reshape(ITEMS * TLEN, 1)
    grads = pull(jnp.where(live_rows, cotangent.astype(jnp.float32), 0.0))
    return (output.astype(jnp.bfloat16), grads[0].astype(jnp.bfloat16), grads[1].astype(jnp.bfloat16), grads[2], grads[3], grads[4], grads[5], grads[6], grads[7], grads[8], grads[9], grads[10], grads[11], grads[12], grads[13], grads[14])
```

```python
import functools
import types

import jax
import jax.numpy as jnp
from jax import lax
from jax.experimental import pallas as pl
from jax.experimental.pallas import tpu as pltpu
from jax.sharding import PartitionSpec as P

HEAD = 64
GROUP = 16
epsilon = 1e-05
MESH = pl.DeviceIdType.MESH
f32, bf16 = jnp.float32, jnp.bfloat16

FC_OUT, FC_IN, CROSS_OUT, CROSS_Q, SELF_OUT, QKV, KV = 0, 4, 8, 9, 10, 11, 14
UNITS = 16
X_TOKENS, X_FIRST, X_SECOND, X_FFN, X_CROSS, X_SELF = range(6)


def nn(a, b):
    return lax.dot_general(a, b, (((1,), (0,)), ((), ())), preferred_element_type=f32)


def nt(a, b):
    return lax.dot_general(a, b, (((1,), (1,)), ((), ())), preferred_element_type=f32)


def loop(count, body):
    def step(i, carry):
        body(i)
        return carry

    lax.fori_loop(0, count, step, 0)


def at(index, size):
    return pl.ds(pl.multiple_of(index * size, size), size)


def kernel(names, refs_at, *refs):
    r = types.SimpleNamespace(**dict(zip(names, refs)))
    T, D = r.tokens.shape
    ML = r.memory.shape[0]
    HL = r.self_out.shape[0]
    FL = r.fc_out.shape[0]
    W = 512
    PAIRS = HL // 128
    CH = 128
    scale = HEAD**-0.5

    d, m = lax.axis_index("dp"), lax.axis_index("mp")
    c, y = lax.rem(d, 2), lax.rem(d // 2, 2)
    zl, zh = lax.rem(d // 4, 2), lax.rem(d // 8, 2)
    to_mp = (d, 1 - m)
    to_c = (d + 1 - 2 * c, m)
    to_y = (d + 2 - 4 * y, m)
    to_z1 = (d + 4 - 8 * zl, m)
    to_z2 = (d + 8 - 16 * zh, m)

    barrier = pltpu.get_barrier_semaphore()
    for partner in (to_mp, to_c, to_y, to_z1, to_z2):
        pl.semaphore_signal(barrier, inc=1, device_id=partner, device_id_type=MESH)

    given = {}
    local_given = {}

    def slot(key, count=1):
        if key not in given:
            given[key] = sum(n for _, n in given.values()), count
        return given[key][0]

    def remote(key, index, count, src, dst, partner):
        base = slot(key, count) + index
        return pltpu.make_async_remote_copy(
            src_ref=src,
            dst_ref=dst,
            send_sem=r.send_sem.at[base],
            recv_sem=r.recv_sem.at[base],
            device_id=partner,
            device_id_type=MESH,
        )

    def local(key, src, dst, index=0, count=1):
        if key not in local_given:
            local_given[key] = sum(n for _, n in local_given.values()), count
        return pltpu.make_async_copy(src, dst, r.local_sem.at[local_given[key][0] + index])

    def load(src):
        name = next(k for k, v in vars(r).items() if v is src)
        return local(name, src, getattr(r, name + "_v"))

    for src in (r.tokens, r.wqkv, r.self_out, r.memory, r.wkv, r.cross_q, r.cross_out, r.fc_in, r.fc_out, r.cotangent):
        load(src).start()
    pl.semaphore_wait(barrier, 5)

    dec_len = r.dec_len[0]
    mem_len = r.mem_len[0]
    gain, shift, out_bias = r.norm_gain, r.norm_bias, r.out_bias
    sm = r.sm
    ycat, xcat, xsend = r.ycat, r.xcat, r.xsend
    low = r.low
    lane_low = lax.broadcasted_iota(jnp.int32, (T, 128), 1) < HEAD

    def stacked(pair):
        wide = pair.astype(f32)
        return jnp.concatenate(
            [jnp.where(lane_low, wide, 0.0).astype(bf16), jnp.where(lane_low, 0.0, wide).astype(bf16)], axis=0
        )

    def unstacked(wide):
        return jnp.concatenate([wide[:HEAD, :T], wide[HEAD:, T:]], axis=0).T

    def col_sum(x):
        return jnp.sum(x, axis=0, keepdims=True)

    def send_x(w, src):
        def block(q):
            row = lax.rem(q, 2) * 128 + (q // 2) * 64
            for own in (True, False):
                side = y if own else 1 - y
                t = src[:, at(q * 2 + side, 128)].astype(f32).T.astype(bf16)
                for half in range(2):
                    rows = pl.ds(pl.multiple_of(half * 256 + row, 64), 64)
                    piece = t[half * 64 : (half + 1) * 64]
                    if own:
                        xcat[w, rows, 0:128] = piece
                    else:
                        xsend[w, rows, :] = piece

        loop(4, block)
        copy_x(w).start()

    def copy_x(w):
        return remote(("x", w), 0, 1, xsend.at[w], xcat.at[w, :, pl.ds(128, 128)], to_y)

    def copy_y(u):
        return remote("yunit", u, KV, ycat.at[u, pl.ds(0, T), :], ycat.at[u, pl.ds(T, T), :], to_y)

    def exchange_copy(k, j):
        s = k % 2
        return remote(("ex", k), j, 4, r.ex_out.at[s, j], r.ex_in.at[s, j], to_mp)

    def exchange_start(k, term):
        def step(j):
            r.ex_out[k % 2, j] = term(j).astype(bf16)
            exchange_copy(k, j).start()

        loop(4, step)

    def exchange_wait(k):
        def step(j):
            exchange_copy(k, j).wait()

        loop(4, step)

    def exchanged(k, rows):
        s = k % 2
        return jnp.concatenate(
            [r.ex_out[s, j, rows, :].astype(f32) + r.ex_in[s, j, rows, :].astype(f32) for j in range(4)], axis=1
        )

    def kept(u):
        return r.fc_out_v.at[at(lax.rem(u, 8), 256), at(u // 8, W)]

    def core_out(u):
        return r.fc_in_v.at[at(lax.rem(u, 4), 256), at(u // 4, W)]

    def copy_core(u):
        return remote("core", u, KV, core_out(u), r.core_in.at[u], to_c)

    def stage_a(w, u0, count):
        def step(i):
            u = u0 + i
            if w >= 0:
                copy_y(u).wait_recv()
            out = core_out(u)
            keep = kept(u)
            for h in range(2):
                cols = pl.ds(h * 256, 256)
                rhs = ycat[u, :, cols]
                out[:, cols] = nn(xcat[w, at(1 - c, 256), :], rhs).astype(bf16)
                keep[:, cols] = nn(xcat[w, at(c, 256), :], rhs).astype(bf16)
            copy_core(u).start()

        copy_x_once(w)
        loop(count, step)

    x_waited = set()

    def copy_x_once(w):
        if w not in x_waited:
            x_waited.add(w)
            copy_x(w).wait_recv()

    def copy_z1(u):
        return remote("z1", u, UNITS, r.z1_out.at[u], r.z1_in.at[u], to_z1)

    def copy_z2(u):
        return remote("z2", u, UNITS, r.z2_out.at[u], r.z2_in.at[u], to_z2)

    def chunk_sum(u, rows):
        return kept(u)[rows, :].astype(f32) + r.core_in[u, rows, :].astype(f32)

    def kv_sum(v, rows):
        low_rows = pl.ds(pl.multiple_of(y * 256 + rows.start, 64), rows.size)
        return (
            r.memory_v[pl.ds(pl.multiple_of(y * 256 + rows.start, 64), rows.size), at(v, W)].astype(f32)
            + r.kvc_in[v, low_rows, :].astype(f32)
            + r.kvy_in[v, rows, :].astype(f32)
        )

    def stage_b(u0, count, total=chunk_sum, shift_u=0, before=None):
        def step(i):
            u = u0 + i
            if before is None:
                copy_core(u).wait_recv()
            else:
                before(i)
            r.z1_out[u] = total(u - shift_u, at(1 - zl, 128)).astype(bf16)
            copy_z1(u).start()

        loop(count, step)

    def stage_c(u0, count, total=chunk_sum, shift_u=0):
        def step(i):
            u = u0 + i
            copy_z1(u).wait_recv()
            rows = pl.ds(pl.multiple_of(zl * 128 + (1 - zh) * 64, 64), 64)
            got = r.z1_in[u, at(1 - zh, 64), :].astype(f32)
            r.z2_out[u] = (total(u - shift_u, rows) + got).astype(bf16)
            copy_z2(u).start()

        loop(count, step)

    def out_copy(u0, i):
        u = u0 + i
        fin = r.fin.at[u]
        if u0 == FC_OUT:
            return local(u0, fin, r.g_fc_out.at[:, at(i, W)], i, 4)
        if u0 == FC_IN:
            return local(u0, fin, r.g_fc_in.at[:, at(i, W)], i, 4)
        if u0 == QKV:
            return local(u0, fin, r.g_qkv.at[i], i, 3)
        if u0 == KV:
            return local(u0, fin, r.g_kv.at[i], i, 2)
        return local(u0, fin, {CROSS_OUT: r.g_cross_out, CROSS_Q: r.g_cross_q, SELF_OUT: r.g_self_out}[u0])

    def stage_d(u0, count, total=chunk_sum, shift_u=0):
        def step(i):
            u = u0 + i
            copy_z2(u).wait_recv()
            rows = pl.ds(pl.multiple_of(zl * 128 + zh * 64, 64), 64)
            got = r.z1_in[u, at(zh, 64), :].astype(f32) + r.z2_in[u].astype(f32)
            r.fin[u] = total(u - shift_u, rows) + got
            out_copy(u0, i).start()

        loop(count, step)

    load(r.tokens).wait()
    load(r.wqkv).wait()
    for part in range(3):

        def packed(j, part=part):
            cols = at(j, 256)
            x = nn(r.tokens_v[...], r.wqkv_v[part, :, cols])
            if part == 0:
                x = x + r.self_qv_bias[0:1, cols]
            if part == 2:
                x = x + r.self_qv_bias[1:2, cols]
            r.packed[part, :, cols] = x.astype(bf16)

        loop(HL // 256, packed)

    key_row = lax.broadcasted_iota(jnp.int32, (T, 2 * T), 0)
    query_row = lax.rem(lax.broadcasted_iota(jnp.int32, (T, 2 * T), 1), T)

    def self_pair(p):
        cols = at(p, 128)
        q, k, v = (r.packed[i, :, cols] for i in range(3))
        s = nt(k, stacked(q)) * scale
        s = jnp.where((key_row <= query_row) & (key_row < dec_len), s, -1e30)
        w = jnp.exp(s - jnp.max(s, axis=0, keepdims=True))
        probs = w / jnp.sum(w, axis=0, keepdims=True)
        r.self_probs[p] = probs
        mixed = nn(v.astype(f32).T.astype(bf16), probs.astype(bf16))
        ycat[SELF_OUT, 0:T, cols] = unstacked(mixed).astype(bf16)

    loop(PAIRS, self_pair)
    load(r.self_out).wait()
    exchange_start(0, lambda j: nn(ycat[SELF_OUT, 0:T, :], r.self_out_v[:, at(j, 256)]))
    copy_y(SELF_OUT).start()
    send_x(X_TOKENS, r.tokens_v)

    load(r.memory).wait()
    load(r.wkv).wait()
    key, value, turned = r.key, r.value, r.turned

    def pair_rows(i):
        rows = at(i, CH)
        x = r.memory_v[rows, :]
        for j in range(HL // 256):
            cols = pl.ds(j * 256, 256)
            key[rows, cols] = nn(x, r.wkv_v[0, :, cols]).astype(bf16)
            val = (nn(x, r.wkv_v[1, :, cols]) + r.cross_qv_bias[1:2, cols]).astype(bf16)
            value[rows, cols] = val

    loop(ML // CH, pair_rows)

    def turn(src):
        def step(i):
            rows = at(i, CH)
            for j in range(HL // 128):
                turned[pl.ds(j * 128, 128), rows] = src[rows, pl.ds(j * 128, 128)].astype(f32).T.astype(bf16)

        loop(ML // CH, step)

    turn(value)

    def normalize(v, k):
        mean = jnp.mean(v, axis=-1, keepdims=True)
        centred = v - mean
        inv = lax.rsqrt(jnp.mean(centred * centred, axis=-1, keepdims=True) + epsilon)
        unit = centred * inv
        return unit * gain[k : k + 1, :] + shift[k : k + 1, :], unit, inv

    def norm_back(g, unit, inv, k):
        w = g * gain[k : k + 1, :]
        return inv * (w - jnp.mean(w, axis=-1, keepdims=True) - unit * jnp.mean(w * unit, axis=-1, keepdims=True))

    exchange_wait(0)

    def first_rows(i):
        rows = at(i, 16)
        v = r.tokens_v[rows, :].astype(f32) + (exchanged(0, rows) + out_bias[0:1, :])
        norm, unit, inv = normalize(v, 0)
        r.norm[rows, :] = norm
        r.unit0[rows, :] = unit
        r.inv[0, rows, :] = jnp.broadcast_to(inv, (16, 128))
        low[rows, :] = norm.astype(bf16)

    loop(T // 16, first_rows)

    load(r.cross_q).wait()

    def cross_query(j):
        cols = at(j, 256)
        x = nn(low[...], r.cross_q_v[:, cols]) + r.cross_qv_bias[0:1, cols]
        r.query[:, cols] = x.astype(bf16)

    loop(HL // 256, cross_query)

    probs_ref = r.probs
    low_probs = r.low_probs
    mem_row = lax.broadcasted_iota(jnp.int32, (CH, 2 * T), 0)
    chunks = ML // CH

    def fold(x, op):
        total = x[0:8]
        for i in range(1, x.shape[0] // 8):
            total = op(total, x[8 * i : 8 * i + 8])
        return total

    def cross_pair(p):
        cols = at(p, 128)
        q = stacked(r.query[:, cols])

        def scores(i, top):
            rows = at(i, CH)
            s = nt(key[rows, cols], q) * scale
            s = jnp.where(mem_row + i * CH < mem_len, s, -1e30)
            probs_ref[p, rows, :] = s
            return jnp.maximum(top, fold(s, jnp.maximum))

        top = lax.fori_loop(0, chunks, scores, jnp.full((8, 2 * T), -1e30, f32))
        top = jnp.max(top, axis=0, keepdims=True)

        def weigh(i, total):
            rows = at(i, CH)
            w = jnp.exp(probs_ref[p, rows, :] - top)
            probs_ref[p, rows, :] = w
            return total + fold(w, jnp.add)

        total = lax.fori_loop(0, chunks, weigh, jnp.zeros((8, 2 * T), f32))
        part = 1.0 / jnp.sum(total, axis=0, keepdims=True)

        def share(i):
            rows = at(i, CH)
            w = probs_ref[p, rows, :] * part
            probs_ref[p, rows, :] = w
            low_probs[rows, :] = w.astype(bf16)

        loop(chunks, share)
        mixed = nn(turned[cols, :], low_probs[...])
        ycat[CROSS_OUT, 0:T, cols] = unstacked(mixed).astype(bf16)

    loop(PAIRS, cross_pair)
    load(r.cross_out).wait()
    exchange_start(1, lambda j: nn(ycat[CROSS_OUT, 0:T, :], r.cross_out_v[:, at(j, 256)]))
    copy_y(CROSS_OUT).start()
    send_x(X_FIRST, low)
    turn(key)

    def turn_memory(i):
        rows = at(i, CH)

        def block(b):
            t = r.memory_v[rows, at(b, 128)].astype(f32).T.astype(bf16)
            side, zlow, zhigh = lax.rem(b, 2), lax.rem(b // 2, 2), b // 4
            for half in range(2):
                to = half * 512 + side * 256 + zlow * 128 + zhigh * 64
                r.memory_t[pl.ds(pl.multiple_of(to, 64), 64), rows] = t[half * 64 : (half + 1) * 64]

        loop(D // 128, block)

    exchange_wait(1)

    def second_rows(i):
        rows = at(i, 16)
        v = r.norm[rows, :] + (exchanged(1, rows) + out_bias[1:2, :])
        norm, unit, inv = normalize(v, 1)
        r.norm[rows, :] = norm
        r.unit1[rows, :] = unit
        r.inv[1, rows, :] = jnp.broadcast_to(inv, (16, 128))
        low[rows, :] = norm.astype(bf16)

    loop(T // 16, second_rows)
    load(r.fc_in).wait()

    def ffn(j):
        cols = at(j, 256)
        h = nn(low[...], r.fc_in_v[:, cols]) + r.fc_in_bias[:, cols]
        phi = 0.5 * (1.0 + lax.erf(h * 0.7071067811865476))
        slope = phi + h * jnp.exp(-0.5 * h * h) * 0.3989422804014327
        r.slope[:, cols] = slope
        ycat[FC_OUT + j // 2, 0:T, at(lax.rem(j, 2), 256)] = (h * phi).astype(bf16)

    loop(FL // 256, ffn)
    load(r.fc_out).wait()

    def ffn_term(j):
        cols = at(j, 256)
        total = nn(ycat[FC_OUT, 0:T, :], r.fc_out_v[pl.ds(0, W), cols])
        for b in range(1, FL // W):
            total = total + nn(ycat[FC_OUT + b, 0:T, :], r.fc_out_v[pl.ds(b * W, W), cols])
        return total

    exchange_start(2, ffn_term)
    for b in range(4):
        copy_y(FC_OUT + b).start()
    send_x(X_SECOND, low)
    loop(ML // CH, turn_memory)
    load(r.cotangent).wait()
    exchange_wait(2)

    row16 = lax.broadcasted_iota(jnp.int32, (16, D), 0)
    zero8 = jnp.zeros((8, D), f32)

    def sums_of(body, k):
        def step(i, carry):
            g, unit, rounded = body(i)
            return (
                carry[0] + fold(rounded, jnp.add),
                carry[1] + fold(g * unit, jnp.add),
                carry[2] + fold(g, jnp.add),
            )

        bias, gains, shifts = lax.fori_loop(0, T // 16, step, (zero8, zero8, zero8))
        sm[0, k : k + 1, :] = col_sum(bias)
        sm[0, 3 + k : 4 + k, :] = col_sum(gains)
        sm[0, 6 + k : 7 + k, :] = col_sum(shifts)

    def output_rows(i):
        rows = at(i, 16)
        v = r.norm[rows, :] + (exchanged(2, rows) + out_bias[2:3, :])
        norm, unit, inv = normalize(v, 2)
        r.layer_v[rows, :] = norm.astype(bf16)
        g = jnp.where(row16 + i * 16 < dec_len, r.cotangent_v[rows, :].astype(f32), 0.0)
        grad = norm_back(g, unit, inv, 2)
        r.grad[rows, :] = grad
        rounded = grad.astype(bf16)
        low[rows, :] = rounded
        return g, unit, rounded.astype(f32)

    copy_x(X_SECOND).wait_send()
    sums_of(output_rows, 2)
    layer_copy = local("layer", r.layer_v, r.layer_out)
    layer_copy.start()
    send_x(X_FFN, low)

    def hidden_grad(j):
        cols = at(j, 256)
        g = nt(low[...], r.fc_out_v[at(j, 256), :]) * r.slope[:, cols]
        rounded = g.astype(bf16)
        ycat[FC_IN + j // 2, 0:T, at(lax.rem(j, 2), 256)] = rounded
        sm[0, pl.ds(11 + j // 4, 1), at(lax.rem(j, 4), 256)] = col_sum(rounded.astype(f32))

    loop(FL // 256, hidden_grad)

    def hidden_term(j):
        rows = at(j, 256)
        total = nt(ycat[FC_IN, 0:T, :], r.fc_in_v[rows, pl.ds(0, W)])
        for b in range(1, FL // W):
            total = total + nt(ycat[FC_IN + b, 0:T, :], r.fc_in_v[rows, pl.ds(b * W, W)])
        return total

    exchange_start(3, hidden_term)
    for b in range(4):
        copy_y(FC_IN + b).start()
    stage_a(X_FFN, FC_OUT, 4)
    stage_b(FC_OUT, 4)
    exchange_wait(3)

    def grad_rows(k, e, unit_ref):
        def body(i):
            rows = at(i, 16)
            g = r.grad[rows, :] + exchanged(e, rows)
            unit = unit_ref[rows, :]
            grad = norm_back(g, unit, r.inv[k, rows, 0:1], k)
            r.grad[rows, :] = grad
            rounded = grad.astype(bf16)
            low[rows, :] = rounded
            return g, unit, rounded.astype(f32)

        sums_of(body, k)

    grad_rows(1, 3, r.unit1)
    send_x(X_CROSS, low)

    load_mixed = r.mixed_grad

    def cross_mixed_grad(j):
        load_mixed[:, at(j, 256)] = nt(low[...], r.cross_out_v[at(j, 256), :]).astype(bf16)

    loop(HL // 256, cross_mixed_grad)

    dp_ref = r.dp

    def cross_back(p):
        cols = at(p, 128)
        q = stacked(r.query[:, cols])
        g = stacked(load_mixed[:, cols])

        def first(i, total):
            rows = at(i, CH)
            probs = probs_ref[p, rows, :]
            dprobs = nt(value[rows, cols], g)
            dp_ref[rows, :] = dprobs
            value[rows, cols] = nn(probs.astype(bf16), g).astype(bf16)
            return total + fold(probs * dprobs, jnp.add)

        total = lax.fori_loop(0, chunks, first, jnp.zeros((8, 2 * T), f32))
        total = jnp.sum(total, axis=0, keepdims=True)

        def second(i):
            rows = at(i, CH)
            ds = (probs_ref[p, rows, :] * (dp_ref[rows, :] - total)).astype(bf16)
            low_probs[rows, :] = ds
            key[rows, cols] = (nn(ds, q) * scale).astype(bf16)

        loop(chunks, second)
        dq = nn(turned[cols, :], low_probs[...])
        ycat[CROSS_Q, 0:T, cols] = (unstacked(dq) * scale).astype(bf16)

    loop(PAIRS, cross_back)
    exchange_start(4, lambda j: nt(ycat[CROSS_Q, 0:T, :], r.cross_q_v[at(j, 256), :]))
    copy_y(CROSS_Q).start()
    sm[0, 10:11, 0:HL] = col_sum(ycat[CROSS_Q, 0:T, :].astype(f32))

    def memory_term(i):
        other = at((1 - m) * 4 + i, CH)
        own = at(m * 4 + i, CH)
        for j in range(D // 256):
            cols = pl.ds(j * 256, 256)
            for half, to in ((other, r.gm_out), (own, r.gm_own)):
                x = nt(key[half, :], r.wkv_v[0, cols, :]) + nt(value[half, :], r.wkv_v[1, cols, :])
                to[i, :, cols] = x.astype(bf16)
        gm_copy(i).start()

    def gm_copy(i):
        return remote("gm", i, 4, r.gm_out.at[i], r.gm_in.at[i], to_mp)

    def copy_kvc(v):
        return remote("kvc", v, 2, r.kvc_out.at[v], r.kvc_in.at[v], to_c)

    def copy_kvy(v):
        return remote("kvy", v, 2, r.kvy_out.at[v], r.kvy_in.at[v], to_y)

    def kv_stage_a(v):
        pair = key if v == 0 else value
        for h in range(2):
            cols = pl.ds(h * 256, 256)

            def step(b, cols=cols, h=h):
                r.kvc_out[v, at(b, 128), cols] = nn(r.memory_t[at((1 - c) * 4 + b, 128), :], pair[:, cols]).astype(bf16)
                r.memory_v[at(b, 128), pl.ds(v * W + h * 256, 256)] = nn(
                    r.memory_t[at(c * 4 + b, 128), :], pair[:, cols]
                ).astype(bf16)

            loop(4, step)
        copy_kvc(v).start()

    def kv_stage_y(v):
        copy_kvc(v).wait_recv()
        rows = at(1 - y, 256)
        r.kvy_out[v] = (r.memory_v[rows, pl.ds(v * W, W)].astype(f32) + r.kvc_in[v, rows, :].astype(f32)).astype(bf16)
        copy_kvy(v).start()

    stage_a(X_SECOND, FC_IN, 4)
    stage_a(X_CROSS, CROSS_OUT, 1)
    stage_b(FC_IN, 4)
    stage_b(CROSS_OUT, 1)
    stage_c(FC_OUT, 4)
    exchange_wait(4)
    copy_x(X_CROSS).wait_send()
    grad_rows(0, 4, r.unit0)
    send_x(X_SELF, low)

    def self_mixed_grad(j):
        load_mixed[:, at(j, 256)] = nt(low[...], r.self_out_v[at(j, 256), :]).astype(bf16)

    loop(HL // 256, self_mixed_grad)

    def self_back(p):
        cols = at(p, 128)
        q, k, v = (r.packed[i, :, cols] for i in range(3))
        probs = r.self_probs[p]
        g = stacked(load_mixed[:, cols])
        dprobs = nt(v, g)
        ycat[QKV + 2, 0:T, cols] = nn(probs.astype(bf16), g).astype(bf16)
        ds = (probs * (dprobs - jnp.sum(probs * dprobs, axis=0, keepdims=True))).astype(bf16)
        ycat[QKV + 1, 0:T, cols] = (nn(ds, stacked(q)) * scale).astype(bf16)
        dq = nn(k.astype(f32).T.astype(bf16), ds)
        ycat[QKV, 0:T, cols] = (unstacked(dq) * scale).astype(bf16)

    loop(PAIRS, self_back)

    def packed_term(j):
        rows = at(j, 256)
        total = nt(ycat[QKV, 0:T, :], r.wqkv_v[0, rows, :])
        for b in range(1, 3):
            total = total + nt(ycat[QKV + b, 0:T, :], r.wqkv_v[b, rows, :])
        return total

    for b in range(3):
        copy_y(QKV + b).start()
    exchange_start(5, packed_term)
    sm[0, 9:10, 0:HL] = col_sum(ycat[QKV, 0:T, :].astype(f32))
    sm[0, 9:10, HL : 2 * HL] = col_sum(ycat[QKV + 2, 0:T, :].astype(f32))
    sm[0, 10:11, HL : 2 * HL] = col_sum(value[...].astype(f32))
    sm[0, 13:16, :] = jnp.zeros((3, D), f32)

    partners = (to_c, to_y, to_z1, to_z2)

    def small_copy(k):
        return remote(("small", k), 0, 1, sm.at[k], r.sm_in.at[k], partners[k])

    def small_step(k):
        small_copy(k).wait_recv()
        sm[k + 1] = sm[k] + r.sm_in[k]

    small_copy(0).start()
    stage_a(X_FIRST, CROSS_Q, 1)
    stage_a(X_SELF, SELF_OUT, 1)
    kv_stage_a(0)
    small_step(0)
    small_copy(1).start()
    kv_stage_a(1)
    stage_b(CROSS_Q, 2)
    kv_stage_y(0)
    kv_stage_y(1)
    stage_a(X_TOKENS, QKV, 3)
    small_step(1)
    small_copy(2).start()
    loop(4, memory_term)
    stage_b(QKV, 3)
    stage_b(KV, 2, kv_sum, KV, lambda i: copy_kvy(i).wait_recv())
    small_step(2)
    small_copy(3).start()
    exchange_wait(5)

    def token_rows(i):
        rows = at(i, 16)
        r.tokens_g[rows, :] = (r.grad[rows, :] + exchanged(5, rows)).astype(bf16)

    loop(T // 16, token_rows)
    token_copy = local("tokens_g", r.tokens_g, r.grad_tokens)
    token_copy.start()
    stage_d(FC_OUT, 4)
    stage_c(FC_IN, 4)
    stage_c(CROSS_OUT, 3)
    stage_c(QKV, 3)
    stage_c(KV, 2, kv_sum, KV)

    def memory_sum(i):
        gm_copy(i).wait()
        r.gm_own[i] = (r.gm_own[i].astype(f32) + r.gm_in[i].astype(f32)).astype(bf16)
        gm_store(i).start()

    def gm_store(i):
        return local("gm_store", r.gm_own.at[i], r.grad_memory.at[at(i, CH), :], i, 4)

    loop(4, memory_sum)
    stage_d(FC_IN, 4)
    stage_d(CROSS_OUT, 1)
    stage_d(CROSS_Q, 1)
    stage_d(SELF_OUT, 1)
    stage_d(QKV, 3)
    stage_d(KV, 2, kv_sum, KV)
    small_step(3)
    sm_copy = local("sm", sm.at[4], r.sums)
    sm_copy.start()

    for w in (X_TOKENS, X_FIRST, X_FFN, X_SELF):
        copy_x(w).wait_send()
    loop(KV, lambda u: copy_y(u).wait_send())
    loop(KV, lambda u: copy_core(u).wait_send())
    loop(2, lambda v: copy_kvc(v).wait_send())
    loop(2, lambda v: copy_kvy(v).wait_send())
    loop(UNITS, lambda u: copy_z1(u).wait_send())
    loop(UNITS, lambda u: copy_z2(u).wait_send())
    for k in range(4):
        small_copy(k).wait_send()
    for u0, count in ((FC_OUT, 4), (FC_IN, 4), (CROSS_OUT, 1), (CROSS_Q, 1), (SELF_OUT, 1), (QKV, 3), (KV, 2)):
        loop(count, lambda i, u0=u0: out_copy(u0, i).wait())
    loop(4, lambda i: gm_store(i).wait())
    layer_copy.wait()
    token_copy.wait()
    sm_copy.wait()
    refs_at.update(remote=sum(n for _, n in given.values()), local=sum(n for _, n in local_given.values()))


REMOTE_SEMS = 140
LOCAL_SEMS = 40


def layer(tokens, memory, mem_len, dec_len, cotangent, wqkv, self_qv_bias, self_out, cross_q, wkv, cross_qv_bias, cross_out, fc_in, fc_in_bias, fc_out, out_bias, norm_gain, norm_bias):
    T, D = tokens.shape
    ML = memory.shape[0]
    HL = self_out.shape[0]
    FL = fc_out.shape[0]
    R = D // GROUP
    W = 512
    PAIRS = HL // 128
    anywhere = pl.BlockSpec(memory_space=pl.ANY)
    in_vmem = pl.BlockSpec(memory_space=pltpu.VMEM)
    in_smem = pl.BlockSpec(memory_space=pltpu.SMEM)
    big = dict(tokens=tokens, memory=memory, cotangent=cotangent, wqkv=wqkv, self_out=self_out, cross_q=cross_q, wkv=wkv,
               cross_out=cross_out, fc_in=fc_in, fc_out=fc_out)
    small = dict(self_qv_bias=self_qv_bias, cross_qv_bias=cross_qv_bias, fc_in_bias=fc_in_bias, out_bias=out_bias,
                 norm_gain=norm_gain, norm_bias=norm_bias)
    scalars = dict(mem_len=mem_len, dec_len=dec_len)
    outs = dict(
        layer_out=((T, D), bf16),
        grad_tokens=((T, D), bf16),
        grad_memory=((ML // 2, D), bf16),
        g_qkv=((3, R, HL), f32),
        g_self_out=((R, HL), f32),
        g_cross_q=((R, HL), f32),
        g_kv=((2, R, HL), f32),
        g_cross_out=((R, HL), f32),
        g_fc_in=((R, FL), f32),
        g_fc_out=((R, FL), f32),
        sums=((16, D), f32),
    )
    scratch = {name + "_v": (x.shape, x.dtype) for name, x in big.items()}
    scratch |= dict(
        packed=((3, T, HL), bf16),
        self_probs=((PAIRS, T, 2 * T), f32),
        low=((T, D), bf16),
        ycat=((KV, 2 * T, W), bf16),
        xcat=((6, 512, 256), bf16),
        xsend=((6, 512, 128), bf16),
        ex_out=((2, 4, T, 256), bf16),
        ex_in=((2, 4, T, 256), bf16),
        norm=((T, D), f32),
        unit0=((T, D), f32),
        unit1=((T, D), f32),
        inv=((2, T, 128), f32),
        grad=((T, D), f32),
        key=((ML, HL), bf16),
        value=((ML, HL), bf16),
        turned=((HL, ML), bf16),
        query=((T, HL), bf16),
        mixed_grad=((T, HL), bf16),
        probs=((PAIRS, ML, 2 * T), f32),
        low_probs=((ML, 2 * T), bf16),
        dp=((ML, 2 * T), f32),
        slope=((T, FL), f32),
        memory_t=((D, ML), bf16),
        layer_v=((T, D), bf16),
        tokens_g=((T, D), bf16),
        gm_out=((4, 128, D), bf16),
        gm_own=((4, 128, D), bf16),
        gm_in=((4, 128, D), bf16),
        core_in=((KV, 256, W), bf16),
        kvc_out=((2, 512, W), bf16),
        kvc_in=((2, 512, W), bf16),
        kvy_out=((2, 256, W), bf16),
        kvy_in=((2, 256, W), bf16),
        z1_out=((UNITS, 128, W), bf16),
        z1_in=((UNITS, 128, W), bf16),
        z2_out=((UNITS, 64, W), bf16),
        z2_in=((UNITS, 64, W), bf16),
        fin=((UNITS, 64, W), f32),
        sm=((5, 16, D), f32),
        sm_in=((4, 16, D), f32),
    )
    sems = dict(send_sem=REMOTE_SEMS, recv_sem=REMOTE_SEMS, local_sem=LOCAL_SEMS)
    names = [*big, *small, *scalars, *outs, *scratch, *sems]
    got = {}
    out = pl.pallas_call(
        functools.partial(kernel, names, got),
        out_shape=[jax.ShapeDtypeStruct(s, t) for s, t in outs.values()],
        in_specs=[anywhere] * len(big) + [in_vmem] * len(small) + [in_smem] * len(scalars),
        out_specs=[anywhere] * len(outs),
        scratch_shapes=[pltpu.VMEM(s, t) for s, t in scratch.values()]
        + [pltpu.SemaphoreType.DMA((count,)) for count in sems.values()],
        compiler_params=pltpu.CompilerParams(
            collective_id=0, has_side_effects=True, vmem_limit_bytes=63 * 2**20
        ),
        name="layer",
    )(*big.values(), *small.values(), *scalars.values())
    assert got["remote"] <= REMOTE_SEMS and got["local"] <= LOCAL_SEMS, got
    return types.SimpleNamespace(**dict(zip(outs, out)))


def per_device(tokens, memory, mem_len, dec_len, cotangent, self_qkv, self_qv_bias, self_out, cross_q, cross_kv, cross_qv_bias, cross_out, fc_in, fc_in_bias, fc_out, out_bias, norm_gain, norm_bias):
    D = tokens.shape[1]
    HL = self_out.shape[0]
    devices = lax.axis_size("dp")
    outer = devices // GROUP

    def regroup(x, axis, there):
        if outer == 1:
            return x
        sizes = (outer, GROUP) if there else (GROUP, outer)
        shape = x.shape
        x = x.reshape(shape[:axis] + sizes + (D // devices,) + shape[axis + 1 :])
        return jnp.swapaxes(x, axis, axis + 1).reshape(shape)

    tokens, memory, cotangent, self_out, cross_out, fc_out, out_bias, norm_gain, norm_bias = (
        regroup(x, 1, True)
        for x in (tokens, memory, cotangent, self_out, cross_out, fc_out, out_bias, norm_gain, norm_bias)
    )
    self_qkv, cross_q, cross_kv, fc_in = (regroup(x, 0, True) for x in (self_qkv, cross_q, cross_kv, fc_in))
    got = layer(
        tokens, memory, mem_len, dec_len, cotangent, self_qkv.transpose(1, 0, 2), self_qv_bias, self_out, cross_q,
        cross_kv.transpose(1, 0, 2), cross_qv_bias, cross_out, fc_in, fc_in_bias.reshape(1, -1), fc_out, out_bias,
        norm_gain, norm_bias,
    )
    groups = [[o * GROUP + i for o in range(outer)] for i in range(GROUP)]

    def spread(x, axis):
        if outer == 1:
            return x
        return lax.psum_scatter(x, "dp", scatter_dimension=axis, axis_index_groups=groups, tiled=True)

    sums = got.sums
    if outer > 1:
        sums = lax.psum(sums, "dp", axis_index_groups=groups)
    layer_out, grad_tokens, grad_memory = (
        regroup(x, 1, False) for x in (got.layer_out, got.grad_tokens, got.grad_memory)
    )
    return (
        layer_out,
        grad_tokens,
        grad_memory,
        spread(got.g_qkv, 1).transpose(1, 0, 2),
        sums[9].reshape(2, HL),
        spread(got.g_self_out, 0).T,
        spread(got.g_cross_q, 0),
        spread(got.g_kv, 1).transpose(1, 0, 2),
        sums[10].reshape(2, HL),
        spread(got.g_cross_out, 0).T,
        spread(got.g_fc_in, 0),
        sums[11:13].reshape(-1),
        spread(got.g_fc_out, 0).T,
        regroup(sums[0:3], 1, False),
        regroup(sums[3:6], 1, False),
        regroup(sums[6:9], 1, False),
    )


def solution(mesh):
    placed = (
        P("dp", None),
        P("dp", None),
        P("dp"),
        P("dp"),
        P("dp", None),
        P(None, None, "mp"),
        P(None, "mp"),
        P("mp", None),
        P(None, "mp"),
        P(None, None, "mp"),
        P(None, "mp"),
        P("mp", None),
        P(None, "mp"),
        P("mp"),
        P("mp", None),
        P(),
        P(),
        P(),
    )
    return jax.shard_map(
        per_device,
        mesh=mesh,
        in_specs=placed,
        out_specs=(
            P("dp", None),
            P("dp", None),
            P(("dp", "mp"), None),
            P("dp", None, "mp"),
            P(None, "mp"),
            P("mp", "dp"),
            P("dp", "mp"),
            P("dp", None, "mp"),
            P(None, "mp"),
            P("mp", "dp"),
            P("dp", "mp"),
            P("mp"),
            P("mp", "dp"),
            P(),
            P(),
            P(),
        ),
        check_vma=False,
    )
```

```python
import functools
import types

import jax
import jax.numpy as jnp
from jax import lax
from jax.experimental import pallas as pl
from jax.experimental.pallas import tpu as pltpu
from jax.sharding import PartitionSpec as P

HEAD = 64
LOG2E = 1.4426950408889634
GROUP = 16
epsilon = 1e-05
MESH = pl.DeviceIdType.MESH
f32, bf16 = jnp.float32, jnp.bfloat16

FC_OUT, FC_IN, CROSS_OUT, CROSS_Q, SELF_OUT, QKV, KV = 0, 4, 8, 9, 10, 11, 14
UNITS = 16
X_TOKENS, X_FIRST, X_SECOND, X_FFN, X_CROSS, X_SELF = range(6)


AXIS_Y, AXIS_Z = 0, 1


def axis_of(unit):
    return AXIS_Z if unit < FC_IN or unit == CROSS_OUT else AXIS_Y


def x_axis(x):
    return AXIS_Z if x in (X_FFN, X_CROSS) else AXIS_Y


def x_of(unit):
    return ((X_FFN,) * 4 + (X_SECOND,) * 4 + (X_CROSS, X_FIRST, X_SELF) + (X_TOKENS,) * 3)[unit]


def nn(a, b):
    return lax.dot_general(a, b, (((1,), (0,)), ((), ())), preferred_element_type=f32)


def nt(a, b):
    return lax.dot_general(a, b, (((1,), (1,)), ((), ())), preferred_element_type=f32)


def loop(count, body, unroll=1):
    def step(i, carry):
        for j in range(unroll):
            body(i * unroll + j)
        return carry

    if unroll == count:
        step(0, 0)
    else:
        lax.fori_loop(0, count // unroll, step, 0)


def at(index, size):
    return pl.ds(index * size if isinstance(index, int) else pl.multiple_of(index * size, size), size)


def kernel(names, refs_at, *refs):
    r = types.SimpleNamespace(**dict(zip(names, refs)))
    T, D = r.tokens.shape
    ML = r.memory.shape[0]
    HL = r.self_out.shape[0]
    FL = r.fc_out.shape[0]
    W = 512
    PAIRS = HL // 128
    CH = 128
    scale = HEAD**-0.5

    d, m = lax.axis_index("dp"), lax.axis_index("mp")
    c, y = lax.rem(d, 2), lax.rem(d // 2, 2)
    zl, zh = lax.rem(d // 4, 2), lax.rem(d // 8, 2)
    to_mp = (d, 1 - m)
    to_c = (d + 1 - 2 * c, m)
    to_y = (d + 2 - 4 * y, m)
    to_z1 = (d + 4 - 8 * zl, m)
    to_z2 = (d + 8 - 16 * zh, m)

    bits, partners_of = (y, zl), (to_y, to_z1)

    barrier = pltpu.get_barrier_semaphore()
    for partner in (to_mp, to_c, to_y, to_z1, to_z2):
        pl.semaphore_signal(barrier, inc=1, device_id=partner, device_id_type=MESH)

    given = {}
    local_given = {}

    def slot(key, count=1):
        if key not in given:
            given[key] = sum(n for _, n in given.values()), count
        return given[key][0]

    def remote(key, index, count, src, dst, partner):
        base = slot(key, count) + index
        return pltpu.make_async_remote_copy(
            src_ref=src,
            dst_ref=dst,
            send_sem=r.send_sem.at[base],
            recv_sem=r.recv_sem.at[base],
            device_id=partner,
            device_id_type=MESH,
        )

    def local(key, src, dst, index=0, count=1):
        if key not in local_given:
            local_given[key] = sum(n for _, n in local_given.values()), count
        return pltpu.make_async_copy(src, dst, r.local_sem.at[local_given[key][0] + index])

    def load(src):
        name = next(k for k, v in vars(r).items() if v is src)
        return local(name, src, getattr(r, name + "_v"))

    def load_qkv(part):
        return local("qkv", r.wqkv.at[part], r.wqkv_v.at[part], part, 3)

    load(r.tokens).start()
    for part in range(3):
        load_qkv(part).start()
    for src in (r.self_out, r.memory, r.cross_kv, r.cross_q, r.cross_out, r.fc_in, r.fc_out, r.cotangent):
        load(src).start()

    dec_len = r.dec_len[0]
    mem_len = r.mem_len[0]
    gain, shift, out_bias = r.norm_gain, r.norm_bias, r.out_bias
    sm = r.sm
    ycat, xcat, xsend = r.ycat, r.xcat, r.xsend
    low = r.low
    lane_low = lax.broadcasted_iota(jnp.int32, (T, 128), 1) < HEAD

    def stacked(pair):
        wide = pair.astype(f32)
        return jnp.concatenate(
            [jnp.where(lane_low, wide, 0.0).astype(bf16), jnp.where(lane_low, 0.0, wide).astype(bf16)], axis=0
        )

    def unstacked(wide):
        return jnp.concatenate([wide[:HEAD, :T], wide[HEAD:, T:]], axis=0).T

    def col_sum(x):
        return jnp.sum(x, axis=0, keepdims=True)

    def send_x(w, src):
        g = x_axis(w)

        def block(q):
            high, o = q // 2, lax.rem(q, 2)
            row = o * 128 + high * 64
            for own in (True, False):
                side = bits[g] if own else 1 - bits[g]
                from_block = high * 4 + (o * 2 + side if g == AXIS_Y else side * 2 + o)
                t = src[:, at(from_block, 128)].astype(f32).T.astype(bf16)
                for half in range(2):
                    rows = pl.ds(pl.multiple_of(half * 256 + row, 64), 64)
                    piece = t[half * 64 : (half + 1) * 64]
                    if own:
                        xcat[w, rows, 0:128] = piece
                    else:
                        xsend[w, rows, :] = piece

        loop(4, block, 2)
        copy_x(w).start()

    def copy_x(w):
        return remote(("x", w), 0, 1, xsend.at[w], xcat.at[w, :, pl.ds(128, 128)], partners_of[x_axis(w)])

    def copy_y(u):
        to = partners_of[axis_of(u)]
        return remote("gather", u, KV, ycat.at[u, pl.ds(0, T), :], ycat.at[u, pl.ds(T, T), :], to)

    def exchange_copy(k, j):
        s = k % 2
        return remote(("ex", k), j, 4, r.ex_out.at[s, j], r.ex_in.at[s, j], to_mp)

    def exchange_start(k, term):
        def step(j):
            r.ex_out[k % 2, j] = term(j).astype(bf16)
            exchange_copy(k, j).start()

        loop(4, step, 4)

    def exchange_wait(k):
        def step(j):
            exchange_copy(k, j).wait()

        loop(4, step)

    def exchanged(k, rows):
        s = k % 2
        return jnp.concatenate(
            [r.ex_out[s, j, rows, :].astype(f32) + r.ex_in[s, j, rows, :].astype(f32) for j in range(4)], axis=1
        )

    def kept(u):
        return r.fc_out_v.at[at(u % 8, 256), at(u // 8, W)]

    def core_out(u):
        return r.fc_in_v.at[at(u % 4, 256), at(u // 4, W)]

    def copy_core(u):
        return remote("core", u, KV, core_out(u), r.core_in.at[u], to_c)

    def copy_half(u):
        return remote("half", u, UNITS, r.half_out.at[u], r.half_in.at[u], partners_of[1 - axis_of(u)])

    def copy_last(u):
        return remote("last", u, UNITS, r.last_out.at[u], r.last_in.at[u], to_z2)

    def kvc_copy(v):
        return remote("kvc", v, 2, r.kvc_out.at[v], r.kvc_in.at[v], to_c)

    def kvy_copy(v):
        return remote("kvy", v, 2, r.kvy_out.at[v], r.kvy_in.at[v], to_y)

    arrived = set()

    def product(u):
        w = x_of(u)
        if w not in arrived:
            arrived.add(w)
            copy_x(w).wait_recv()
        copy_y(u).wait_recv()
        for h in range(W // 256):
            cols = pl.ds(h * 256, 256)
            rhs = ycat[u, :, cols]
            core_out(u)[:, cols] = nn(xcat[w, at(1 - c, 256), :], rhs).astype(bf16)
            kept(u)[:, cols] = nn(xcat[w, at(c, 256), :], rhs).astype(bf16)
        copy_core(u).start()

    def local_sum(u, rows):
        if u < KV:
            return kept(u)[rows, :].astype(f32) + r.core_in[u, rows, :].astype(f32)
        v = u - KV
        wide = pl.ds(pl.multiple_of(y * 256 + rows.start, 64), rows.size)
        mine = r.memory_v[wide, pl.ds(v * W, W)].astype(f32) + r.kvc_in[v, wide, :].astype(f32)
        return mine + r.kvy_in[v, rows, :].astype(f32)

    def halve(u):
        if u < KV:
            copy_core(u).wait_recv()
        else:
            kvy_copy(u - KV).wait_recv()
        r.half_out[u] = local_sum(u, at(1 - bits[1 - axis_of(u)], 128)).astype(bf16)
        copy_half(u).start()

    def part_rows(u, high):
        return pl.ds(pl.multiple_of(bits[1 - axis_of(u)] * 128 + high * 64, 64), 64)

    def halve_last(u):
        copy_half(u).wait_recv()
        got = r.half_in[u, at(1 - zh, 64), :].astype(f32)
        r.last_out[u] = (local_sum(u, part_rows(u, 1 - zh)) + got).astype(bf16)
        copy_last(u).start()

    def out_copy(u):
        if u < FC_IN:
            to = r.g_fc_out.at[:, at(u, W)]
        elif u < CROSS_OUT:
            to = r.g_fc_in.at[:, at(u - FC_IN, W)]
        elif u < QKV:
            to = (r.g_cross_out, r.g_cross_q, r.g_self_out)[u - CROSS_OUT]
        elif u < KV:
            to = r.g_qkv.at[u - QKV]
        else:
            to = r.g_kv.at[u - KV]
        return local("unit", r.fin.at[u], to, u, UNITS)

    def total(u):
        copy_last(u).wait_recv()
        got = r.half_in[u, at(zh, 64), :].astype(f32) + r.last_in[u].astype(f32)
        r.fin[u] = local_sum(u, part_rows(u, zh)) + got
        out_copy(u).start()

    def project():
        load(r.tokens).wait()
        for part in range(3):
            load_qkv(part).wait()

            def packed(j, part=part):
                cols = at(j, 256)
                x = nn(r.tokens_v[...], r.wqkv_v[part, :, cols])
                if part == 0:
                    x = x + r.self_qv_bias[0:1, cols]
                if part == 2:
                    x = x + r.self_qv_bias[1:2, cols]
                r.packed[part, :, cols] = x.astype(bf16)

            loop(HL // 256, packed, 2)

    key_row = lax.broadcasted_iota(jnp.int32, (T, 2 * T), 0)
    query_row = lax.rem(lax.broadcasted_iota(jnp.int32, (T, 2 * T), 1), T)

    def self_pair(p):
        cols = at(p, 128)
        q, k, v = (r.packed[i, :, cols] for i in range(3))
        s = nt(k, stacked(q)) * scale
        s = jnp.where((key_row <= query_row) & (key_row < dec_len), s, -1e30)
        w = jnp.exp(s - jnp.max(s, axis=0, keepdims=True))
        probs = w / jnp.sum(w, axis=0, keepdims=True)
        r.self_probs[p] = probs
        mixed = nn(v.astype(f32).T.astype(bf16), probs.astype(bf16))
        ycat[SELF_OUT, 0:T, cols] = unstacked(mixed).astype(bf16)

    def self_attention():
        loop(PAIRS, self_pair, 4)

    def send_first():
        load(r.self_out).wait()
        pl.semaphore_wait(barrier, 5)
        exchange_start(0, lambda j: nn(ycat[SELF_OUT, 0:T, :], r.self_out_v[:, at(j, 256)]))
        copy_y(SELF_OUT).start()

    key, value, turned = r.key, r.value, r.turned
    odd = lax.broadcasted_iota(jnp.int32, (256, 256), 0)
    odd = jnp.where(odd < 128, 2 * odd, 2 * odd - 255)
    select = (lax.broadcasted_iota(jnp.int32, (256, 256), 1) == odd).astype(f32).astype(bf16)

    def part_weights(i):
        rows = at(i, CH)
        x = nn(select, r.cross_kv_v[rows].reshape(2 * CH, HL)).astype(bf16)
        r.wkv_v[0, rows, :] = x[:CH]
        r.wkv_v[1, rows, :] = x[CH:]

    def pair_rows(i):
        rows = at(i, CH)
        x = r.memory_v[rows, :]
        for j in range(HL // 256):
            cols = pl.ds(j * 256, 256)
            key[rows, cols] = nn(x, r.wkv_v[0, :, cols]).astype(bf16)
            val = (nn(x, r.wkv_v[1, :, cols]) + r.cross_qv_bias[1:2, cols]).astype(bf16)
            value[rows, cols] = val

    def turn(src):
        def step(i):
            rows = at(i, CH)
            for j in range(HL // 128):
                turned[pl.ds(j * 128, 128), rows] = src[rows, pl.ds(j * 128, 128)].astype(f32).T.astype(bf16)

        loop(ML // CH, step, 2)

    def memory_pair():
        load(r.cross_kv).wait()
        loop(D // CH, part_weights, 2)
        load(r.memory).wait()
        loop(ML // CH, pair_rows, 2)
        turn(value)

    def turn_memory(i):
        rows = at(i, CH)

        def block(b):
            t = r.memory_v[rows, at(b, 128)].astype(f32).T.astype(bf16)
            side, zlow, zhigh = lax.rem(b, 2), lax.rem(b // 2, 2), b // 4
            for half in range(2):
                to = half * 512 + side * 256 + zlow * 128 + zhigh * 64
                r.memory_t[pl.ds(pl.multiple_of(to, 64), 64), rows] = t[half * 64 : (half + 1) * 64]

        loop(D // 128, block, 4)

    def normalize(v, k):
        mean = jnp.mean(v, axis=-1, keepdims=True)
        centred = v - mean
        inv = lax.rsqrt(jnp.mean(centred * centred, axis=-1, keepdims=True) + epsilon)
        unit = centred * inv
        return unit * gain[k : k + 1, :] + shift[k : k + 1, :], unit, inv

    def norm_back(g, unit, inv, k):
        w = g * gain[k : k + 1, :]
        return inv * (w - jnp.mean(w, axis=-1, keepdims=True) - unit * jnp.mean(w * unit, axis=-1, keepdims=True))

    def norm_rows(k, base, unit_ref):
        def body(i):
            rows = at(i, 16)
            v = base[rows, :].astype(f32) + (exchanged(k, rows) + out_bias[k : k + 1, :])
            norm, unit, inv = normalize(v, k)
            r.norm[rows, :] = norm
            unit_ref[rows, :] = unit
            r.inv[k, rows, :] = jnp.broadcast_to(inv, (16, 128))
            low[rows, :] = norm.astype(bf16)

        exchange_wait(k)
        loop(T // 16, body, T // 16)

    def first_norm():
        norm_rows(0, r.tokens_v, r.unit0)

    def cross_query(j):
        cols = at(j, 256)
        x = nn(low[...], r.cross_q_v[:, cols]) + r.cross_qv_bias[0:1, cols]
        r.query[:, cols] = x.astype(bf16)

    probs_ref = r.probs
    low_probs = r.low_probs
    mem_row = lax.broadcasted_iota(jnp.int32, (CH, 2 * T), 0)
    chunks = ML // CH

    def fold(x, op):
        total = x[0:8]
        for i in range(1, x.shape[0] // 8):
            total = op(total, x[8 * i : 8 * i + 8])
        return total

    def cross_pair(p):
        cols = at(p, 128)
        q = stacked(r.query[:, cols])
        top = jnp.full((8, 2 * T), -1e30, f32)
        for i in range(chunks):
            rows = at(i, CH)
            s = nt(key[rows, cols], q) * (scale * LOG2E)
            s = jnp.where(mem_row < mem_len - i * CH, s, -1e30)
            probs_ref[p, rows, :] = s
            top = jnp.maximum(top, fold(s, jnp.maximum))
        top = jnp.max(top, axis=0, keepdims=True)
        total = jnp.zeros((8, 2 * T), f32)
        for i in range(chunks):
            rows = at(i, CH)
            w = jnp.exp2(probs_ref[p, rows, :] - top)
            probs_ref[p, rows, :] = w
            low_probs[rows, :] = w.astype(bf16)
            total = total + fold(w, jnp.add)
        part = 1.0 / jnp.sum(total, axis=0, keepdims=True)
        r.part[p] = jnp.broadcast_to(part, (8, 2 * T))
        mixed = nn(turned[cols, :], low_probs[...]) * part
        ycat[CROSS_OUT, 0:T, cols] = unstacked(mixed).astype(bf16)

    def cross_attention():
        load(r.cross_q).wait()
        loop(HL // 256, cross_query, 2)
        loop(PAIRS, cross_pair)

    def send_second():
        load(r.cross_out).wait()
        exchange_start(1, lambda j: nn(ycat[CROSS_OUT, 0:T, :], r.cross_out_v[:, at(j, 256)]))
        copy_y(CROSS_OUT).start()

    def second_norm():
        norm_rows(1, r.norm, r.unit1)

    def ffn(j):
        cols = at(j, 256)
        h = nn(low[...], r.fc_in_v[:, cols]) + r.fc_in_bias[:, cols]
        phi = 0.5 * (1.0 + lax.erf(h * 0.7071067811865476))
        slope = phi + h * jnp.exp(-0.5 * h * h) * 0.3989422804014327
        r.slope[:, cols] = slope
        ycat[FC_OUT + j // 2, 0:T, at(lax.rem(j, 2), 256)] = (h * phi).astype(bf16)

    def hidden_units():
        load(r.fc_in).wait()
        for b in range(FL // W):
            ffn(2 * b)
            ffn(2 * b + 1)
            copy_y(FC_OUT + b).start()

    def ffn_term(j):
        cols = at(j, 256)
        total = nn(ycat[FC_OUT, 0:T, :], r.fc_out_v[pl.ds(0, W), cols])
        for b in range(1, FL // W):
            total = total + nn(ycat[FC_OUT + b, 0:T, :], r.fc_out_v[pl.ds(b * W, W), cols])
        return total

    def send_third():
        load(r.fc_out).wait()
        exchange_start(2, ffn_term)

    row16 = lax.broadcasted_iota(jnp.int32, (16, D), 0)
    zero8 = jnp.zeros((8, D), f32)

    def sums_of(body, k):
        def step(i, carry):
            g, unit, rounded = body(i)
            return (
                carry[0] + fold(rounded, jnp.add),
                carry[1] + fold(g * unit, jnp.add),
                carry[2] + fold(g, jnp.add),
            )

        carry = (zero8, zero8, zero8)
        for i in range(T // 16):
            carry = step(i, carry)
        bias, gains, shifts = carry
        sm[k : k + 1, :] = col_sum(bias)
        sm[3 + k : 4 + k, :] = col_sum(gains)
        sm[6 + k : 7 + k, :] = col_sum(shifts)

    def output_rows(i):
        rows = at(i, 16)
        v = r.norm[rows, :] + (exchanged(2, rows) + out_bias[2:3, :])
        norm, unit, inv = normalize(v, 2)
        r.layer_v[rows, :] = norm.astype(bf16)
        g = jnp.where(row16 + i * 16 < dec_len, r.cotangent_v[rows, :].astype(f32), 0.0)
        grad = norm_back(g, unit, inv, 2)
        r.grad[rows, :] = grad
        rounded = grad.astype(bf16)
        low[rows, :] = rounded
        return g, unit, rounded.astype(f32)

    def layer_copy():
        return local("layer", r.layer_v, r.layer_out)

    def output_norm():
        load(r.cotangent).wait()
        exchange_wait(2)
        sums_of(output_rows, 2)
        layer_copy().start()

    def hidden_grad(j):
        cols = at(j, 256)
        g = nt(low[...], r.fc_out_v[at(j, 256), :]) * r.slope[:, cols]
        rounded = g.astype(bf16)
        ycat[FC_IN + j // 2, 0:T, at(j % 2, 256)] = rounded
        sm[pl.ds(11 + j // 4, 1), at(j % 4, 256)] = col_sum(rounded.astype(f32))

    def hidden_grads():
        for b in range(FL // W):
            hidden_grad(2 * b)
            hidden_grad(2 * b + 1)
            copy_y(FC_IN + b).start()

    def hidden_term(j):
        rows = at(j, 256)
        total = nt(ycat[FC_IN, 0:T, :], r.fc_in_v[rows, pl.ds(0, W)])
        for b in range(1, FL // W):
            total = total + nt(ycat[FC_IN + b, 0:T, :], r.fc_in_v[rows, pl.ds(b * W, W)])
        return total

    def send_fourth():
        exchange_start(3, hidden_term)

    def grad_rows(k, e, unit_ref):
        def body(i):
            rows = at(i, 16)
            g = r.grad[rows, :] + exchanged(e, rows)
            unit = unit_ref[rows, :]
            grad = norm_back(g, unit, r.inv[k, rows, 0:1], k)
            r.grad[rows, :] = grad
            rounded = grad.astype(bf16)
            low[rows, :] = rounded
            return g, unit, rounded.astype(f32)

        exchange_wait(e)
        sums_of(body, k)

    mixed_grad = r.mixed_grad

    def second_back():
        grad_rows(1, 3, r.unit1)

    def mixed_from(weights):
        for j in range(HL // 256):
            mixed_grad[:, at(j, 256)] = nt(low[...], weights[at(j, 256), :]).astype(bf16)

    def cross_mixed_grad():
        mixed_from(r.cross_out_v)

    dp_ref = r.dp

    def cross_back(p):
        cols = at(p, 128)
        q = stacked(r.query[:, cols])
        g = stacked(mixed_grad[:, cols])
        part = r.part[p, 0:1, :]
        total = jnp.zeros((8, 2 * T), f32)
        for i in range(chunks):
            rows = at(i, CH)
            probs = probs_ref[p, rows, :] * part
            dprobs = nt(value[rows, cols], g)
            dp_ref[rows, :] = dprobs
            probs_ref[p, rows, :] = probs
            value[rows, cols] = nn(probs.astype(bf16), g).astype(bf16)
            total = total + fold(probs * dprobs, jnp.add)
        total = jnp.sum(total, axis=0, keepdims=True)
        for i in range(chunks):
            rows = at(i, CH)
            ds = (probs_ref[p, rows, :] * (dp_ref[rows, :] - total)).astype(bf16)
            low_probs[rows, :] = ds
            key[rows, cols] = (nn(ds, q) * scale).astype(bf16)
        dq = nn(turned[cols, :], low_probs[...])
        ycat[CROSS_Q, 0:T, cols] = (unstacked(dq) * scale).astype(bf16)

    def send_fifth():
        exchange_start(4, lambda j: nt(ycat[CROSS_Q, 0:T, :], r.cross_q_v[at(j, 256), :]))
        copy_y(CROSS_Q).start()
        sm[10:11, 0:HL] = col_sum(ycat[CROSS_Q, 0:T, :].astype(f32))
        sm[10:11, HL : 2 * HL] = col_sum(value[...].astype(f32))

    def gm_copy(i):
        return remote("gm", i, 4, r.gm_out.at[i], r.gm_in.at[i], to_mp)

    def memory_term(i):
        for half, to in (((1 - m) * 4 + i, r.gm_out), (m * 4 + i, r.gm_own)):
            rows = at(half, CH)
            for j in range(D // 256):
                cols = pl.ds(j * 256, 256)
                x = nt(key[rows, :], r.wkv_v[0, cols, :]) + nt(value[rows, :], r.wkv_v[1, cols, :])
                to[i, :, cols] = x.astype(bf16)
        gm_copy(i).start()

    def gm_store(i):
        return local("gm_store", r.gm_own.at[i], r.grad_memory.at[at(i, CH), :], i, 4)

    def memory_sum(i):
        gm_copy(i).wait()
        r.gm_own[i] = (r.gm_own[i].astype(f32) + r.gm_in[i].astype(f32)).astype(bf16)
        gm_store(i).start()

    def pair_product(v):
        pair = key if v == 0 else value
        for h in range(2):
            cols = pl.ds(h * 256, 256)

            def step(b, cols=cols, h=h):
                rows = at(b, 128)
                other, own = r.memory_t[at((1 - c) * 4 + b, 128), :], r.memory_t[at(c * 4 + b, 128), :]
                r.kvc_out[v, rows, cols] = nn(other, pair[:, cols]).astype(bf16)
                r.memory_v[rows, pl.ds(v * W + h * 256, 256)] = nn(own, pair[:, cols]).astype(bf16)

            loop(4, step)
        kvc_copy(v).start()

    def pair_halve(v):
        kvc_copy(v).wait_recv()
        rows = at(1 - y, 256)
        mine = r.memory_v[rows, pl.ds(v * W, W)].astype(f32)
        r.kvy_out[v] = (mine + r.kvc_in[v, rows, :].astype(f32)).astype(bf16)
        kvy_copy(v).start()

    def first_back():
        grad_rows(0, 4, r.unit0)

    def self_back(p):
        cols = at(p, 128)
        q, k, v = (r.packed[i, :, cols] for i in range(3))
        probs = r.self_probs[p]
        g = stacked(mixed_grad[:, cols])
        dprobs = nt(v, g)
        ycat[QKV + 2, 0:T, cols] = nn(probs.astype(bf16), g).astype(bf16)
        ds = (probs * (dprobs - jnp.sum(probs * dprobs, axis=0, keepdims=True))).astype(bf16)
        ycat[QKV + 1, 0:T, cols] = (nn(ds, stacked(q)) * scale).astype(bf16)
        dq = nn(k.astype(f32).T.astype(bf16), ds)
        ycat[QKV, 0:T, cols] = (unstacked(dq) * scale).astype(bf16)

    def self_grads():
        mixed_from(r.self_out_v)
        loop(PAIRS, self_back, 4)
        for b in range(3):
            copy_y(QKV + b).start()
        sm[9:10, 0:HL] = col_sum(ycat[QKV, 0:T, :].astype(f32))
        sm[9:10, HL : 2 * HL] = col_sum(ycat[QKV + 2, 0:T, :].astype(f32))
        sm[13:16, :] = jnp.zeros((3, D), f32)

    def packed_term(j):
        rows = at(j, 256)
        total = nt(ycat[QKV, 0:T, :], r.wqkv_v[0, rows, :])
        for b in range(1, 3):
            total = total + nt(ycat[QKV + b, 0:T, :], r.wqkv_v[b, rows, :])
        return total

    def send_sixth():
        exchange_start(5, packed_term)

    def token_copy():
        return local("tokens_g", r.tokens_g, r.grad_tokens)

    def token_grads():
        def body(i):
            rows = at(i, 16)
            r.tokens_g[rows, :] = (r.grad[rows, :] + exchanged(5, rows)).astype(bf16)

        exchange_wait(5)
        loop(T // 16, body, 2)
        token_copy().start()

    doubling = (to_c, to_y, to_z1, to_z2)

    def small_copy(k):
        return remote("small", k, 4, r.sm_out.at[k], r.sm_in.at[k], doubling[k])

    def sums_copy():
        return local("sums", sm, r.sums)

    def small_step(k):
        if k > 0:
            small_copy(k - 1).wait()
            sm[...] = r.sm_out[k - 1].astype(f32) + r.sm_in[k - 1].astype(f32)
        if k < 4:
            r.sm_out[k] = sm[...].astype(bf16)
            small_copy(k).start()
        else:
            sums_copy().start()

    def each(step, *indices):
        for i in indices:
            step(i)

    project()
    self_attention()
    send_first()
    memory_pair()
    send_x(X_TOKENS, r.tokens_v)
    each(turn_memory, 4, 3, 1)
    first_norm()
    cross_attention()
    send_second()
    send_x(X_FIRST, low)
    turn(key)
    each(turn_memory, 0, 6, 2, 5, 7)
    second_norm()
    send_x(X_SECOND, low)
    hidden_units()
    send_third()
    output_norm()
    send_x(X_FFN, low)
    hidden_grads()
    send_fourth()
    each(product, 4)
    each(halve, 4)
    each(product, 0, 3, 2, 1, 5)
    each(halve, 0)
    second_back()
    send_x(X_CROSS, low)
    cross_mixed_grad()
    each(halve, 3, 2, 1)
    each(cross_back, 0)
    each(halve_last, 4)
    each(product, 6)
    each(cross_back, 1, 2)
    each(halve, 6)
    each(product, 7)
    each(halve, 5)
    each(cross_back, 3)
    each(product, 8)
    send_fifth()
    each(halve_last, 0)
    each(halve, 7)
    each(memory_term, 0)
    each(halve, 8)
    each(memory_term, 3)
    each(halve_last, 3, 6)
    each(pair_product, 1)
    each(halve_last, 2)
    first_back()
    each(halve_last, 5)
    each(memory_term, 1)
    each(total, 4)
    send_x(X_SELF, low)
    self_grads()
    each(halve_last, 7, 1)
    send_sixth()
    each(memory_sum, 0)
    each(small_step, 0)
    each(product, 9)
    each(total, 3, 0)
    each(pair_product, 0)
    each(halve_last, 8)
    each(small_step, 1)
    each(total, 6)
    each(halve, 9)
    each(pair_halve, 1)
    each(memory_term, 2)
    each(memory_sum, 3)
    each(product, 10)
    each(pair_halve, 0)
    each(total, 2)
    each(halve, 10)
    each(product, 11)
    each(total, 5)
    each(memory_sum, 1)
    each(halve, 11)
    each(halve_last, 9)
    each(product, 12)
    each(total, 7)
    each(halve, 12)
    each(halve_last, 10)
    each(product, 13)
    each(small_step, 2)
    each(total, 1)
    token_grads()
    each(halve, 13)
    each(halve_last, 11)
    each(total, 8)
    each(halve_last, 12)
    each(memory_sum, 2)
    each(halve, 15)
    each(total, 9)
    each(small_step, 3)
    each(total, 10)
    each(halve_last, 13)
    each(halve, 14)
    each(total, 11)
    each(halve_last, 15)
    each(total, 12)
    each(small_step, 4)
    each(total, 13)
    each(halve_last, 14)
    each(total, 15, 14)
    for w in range(6):
        copy_x(w).wait_send()
    for u in range(UNITS):
        if u < KV:
            copy_y(u).wait_send()
            copy_core(u).wait_send()
        copy_half(u).wait_send()
        copy_last(u).wait_send()
        out_copy(u).wait()
    for v in range(2):
        kvc_copy(v).wait_send()
        kvy_copy(v).wait_send()
    for i in range(4):
        gm_store(i).wait()
    layer_copy().wait()
    token_copy().wait()
    sums_copy().wait()
    refs_at.update(remote=sum(n for _, n in given.values()), local=sum(n for _, n in local_given.values()))


REMOTE_SEMS = 144
LOCAL_SEMS = 40


def layer(tokens, memory, mem_len, dec_len, cotangent, wqkv, self_qv_bias, self_out, cross_q, cross_kv, cross_qv_bias, cross_out, fc_in, fc_in_bias, fc_out, out_bias, norm_gain, norm_bias):
    T, D = tokens.shape
    ML = memory.shape[0]
    HL = self_out.shape[0]
    FL = fc_out.shape[0]
    R = D // GROUP
    W = 512
    PAIRS = HL // 128
    anywhere = pl.BlockSpec(memory_space=pl.ANY)
    in_vmem = pl.BlockSpec(memory_space=pltpu.VMEM)
    in_smem = pl.BlockSpec(memory_space=pltpu.SMEM)
    big = dict(tokens=tokens, memory=memory, cotangent=cotangent, wqkv=wqkv, self_out=self_out, cross_q=cross_q, cross_kv=cross_kv,
               cross_out=cross_out, fc_in=fc_in, fc_out=fc_out)
    small = dict(self_qv_bias=self_qv_bias, cross_qv_bias=cross_qv_bias, fc_in_bias=fc_in_bias, out_bias=out_bias,
                 norm_gain=norm_gain, norm_bias=norm_bias)
    scalars = dict(mem_len=mem_len, dec_len=dec_len)
    outs = dict(
        layer_out=((T, D), bf16),
        grad_tokens=((T, D), bf16),
        grad_memory=((ML // 2, D), bf16),
        g_qkv=((3, R, HL), f32),
        g_self_out=((R, HL), f32),
        g_cross_q=((R, HL), f32),
        g_kv=((2, R, HL), f32),
        g_cross_out=((R, HL), f32),
        g_fc_in=((R, FL), f32),
        g_fc_out=((R, FL), f32),
        sums=((16, D), f32),
    )
    scratch = {name + "_v": (x.shape, x.dtype) for name, x in big.items()}
    scratch |= dict(
        wkv_v=((2, D, HL), bf16),
        packed=((3, T, HL), bf16),
        self_probs=((PAIRS, T, 2 * T), f32),
        low=((T, D), bf16),
        ycat=((KV, 2 * T, W), bf16),
        xcat=((6, 512, 256), bf16),
        xsend=((6, 512, 128), bf16),
        ex_out=((2, 4, T, 256), bf16),
        ex_in=((2, 4, T, 256), bf16),
        norm=((T, D), f32),
        unit0=((T, D), f32),
        unit1=((T, D), f32),
        inv=((2, T, 128), f32),
        grad=((T, D), f32),
        key=((ML, HL), bf16),
        value=((ML, HL), bf16),
        turned=((HL, ML), bf16),
        query=((T, HL), bf16),
        mixed_grad=((T, HL), bf16),
        probs=((PAIRS, ML, 2 * T), f32),
        part=((PAIRS, 8, 2 * T), f32),
        low_probs=((ML, 2 * T), bf16),
        dp=((ML, 2 * T), f32),
        slope=((T, FL), f32),
        memory_t=((D, ML), bf16),
        layer_v=((T, D), bf16),
        tokens_g=((T, D), bf16),
        gm_out=((4, 128, D), bf16),
        gm_own=((4, 128, D), bf16),
        gm_in=((4, 128, D), bf16),
        core_in=((KV, 256, W), bf16),
        kvc_out=((2, 512, W), bf16),
        kvc_in=((2, 512, W), bf16),
        kvy_out=((2, 256, W), bf16),
        kvy_in=((2, 256, W), bf16),
        half_out=((UNITS, 128, W), bf16),
        half_in=((UNITS, 128, W), bf16),
        last_out=((UNITS, 64, W), bf16),
        last_in=((UNITS, 64, W), bf16),
        fin=((UNITS, 64, W), f32),
        sm=((16, D), f32),
        sm_out=((4, 16, D), bf16),
        sm_in=((4, 16, D), bf16),
    )
    sems = dict(send_sem=REMOTE_SEMS, recv_sem=REMOTE_SEMS, local_sem=LOCAL_SEMS)
    names = [*big, *small, *scalars, *outs, *scratch, *sems]
    got = {}
    out = pl.pallas_call(
        functools.partial(kernel, names, got),
        out_shape=[jax.ShapeDtypeStruct(s, t) for s, t in outs.values()],
        in_specs=[anywhere] * len(big) + [in_vmem] * len(small) + [in_smem] * len(scalars),
        out_specs=[anywhere] * len(outs),
        scratch_shapes=[pltpu.VMEM(s, t) for s, t in scratch.values()]
        + [pltpu.SemaphoreType.DMA((count,)) for count in sems.values()],
        compiler_params=pltpu.CompilerParams(
            collective_id=0, has_side_effects=True, vmem_limit_bytes=63 * 2**20
        ),
        name="layer",
    )(*big.values(), *small.values(), *scalars.values())
    assert got["remote"] <= REMOTE_SEMS and got["local"] <= LOCAL_SEMS, got
    return types.SimpleNamespace(**dict(zip(outs, out)))


def finish_kernel(count, *refs):
    ins, outs, scratch = refs[: count + 2], refs[count + 2 : 2 * count + 9], refs[2 * count + 9 :]
    held, turned, in_sem, out_sem = scratch[: count + 1], *scratch[count + 1 :]
    loads = [pltpu.make_async_copy(a, b, in_sem.at[i]) for i, (a, b) in enumerate(zip(ins, held))]
    stores = [
        pltpu.make_async_copy(a, b, out_sem.at[i]) for i, (a, b) in enumerate(zip((*held[:count], turned), outs))
    ]
    for load in loads:
        load.start()
    sums = ins[count + 1]
    self_bias, cross_bias, hidden_bias, out_bias, gains, shifts = outs[count + 1 :]
    width = self_bias.shape[1]
    for row, to in ((9, self_bias), (10, cross_bias)):
        for part in range(2):
            to[part : part + 1, :] = sums[row : row + 1, part * width : (part + 1) * width]
    features = sums.shape[1]
    for part in range(hidden_bias.shape[1] // features):
        hidden_bias[:, part * features : (part + 1) * features] = sums[11 + part : 12 + part, :]
    for first, to in ((0, out_bias), (3, gains), (6, shifts)):
        to[...] = sums[first : first + 3, :]
    for i in range(count):
        loads[i].wait()
        stores[i].start()
    loads[count].wait()
    for part in range(2):
        turned[:, part, :] = held[count][part]
    stores[count].start()
    for store in stores:
        store.wait()


def finish(whole, kv, sums):
    R, HL = kv.shape[1:]
    D = sums.shape[1]
    anywhere = pl.BlockSpec(memory_space=pl.ANY)
    in_vmem = pl.BlockSpec(memory_space=pltpu.VMEM)
    small = [(2, HL), (2, HL), (1, 4 * HL), (3, D), (3, D), (3, D)]
    return pl.pallas_call(
        functools.partial(finish_kernel, len(whole)),
        out_shape=[jax.ShapeDtypeStruct(x.shape, x.dtype) for x in whole]
        + [jax.ShapeDtypeStruct((R, 2, HL), f32)]
        + [jax.ShapeDtypeStruct(shape, f32) for shape in small],
        in_specs=[anywhere] * (len(whole) + 1) + [in_vmem],
        out_specs=[anywhere] * (len(whole) + 1) + [in_vmem] * len(small),
        scratch_shapes=[pltpu.VMEM(x.shape, x.dtype) for x in (*whole, kv)]
        + [pltpu.VMEM((R, 2, HL), f32)]
        + [pltpu.SemaphoreType.DMA((len(whole) + 1,))] * 2,
        compiler_params=pltpu.CompilerParams(vmem_limit_bytes=63 * 2**20),
        name="finish",
    )(*whole, kv, sums)


def per_device(tokens, memory, mem_len, dec_len, cotangent, self_qkv, self_qv_bias, self_out, cross_q, cross_kv, cross_qv_bias, cross_out, fc_in, fc_in_bias, fc_out, out_bias, norm_gain, norm_bias):
    D = tokens.shape[1]
    devices = lax.axis_size("dp")
    outer = devices // GROUP

    def regroup(x, axis, there):
        if outer == 1:
            return x
        sizes = (outer, GROUP) if there else (GROUP, outer)
        shape = x.shape
        x = x.reshape(shape[:axis] + sizes + (D // devices,) + shape[axis + 1 :])
        return jnp.swapaxes(x, axis, axis + 1).reshape(shape)

    tokens, memory, cotangent, self_out, cross_out, fc_out, out_bias, norm_gain, norm_bias = (
        regroup(x, 1, True)
        for x in (tokens, memory, cotangent, self_out, cross_out, fc_out, out_bias, norm_gain, norm_bias)
    )
    self_qkv, cross_q, cross_kv, fc_in = (regroup(x, 0, True) for x in (self_qkv, cross_q, cross_kv, fc_in))
    got = layer(
        tokens, memory, mem_len, dec_len, cotangent, self_qkv.transpose(1, 0, 2), self_qv_bias, self_out, cross_q,
        cross_kv, cross_qv_bias, cross_out, fc_in, fc_in_bias.reshape(1, -1), fc_out, out_bias,
        norm_gain, norm_bias,
    )
    groups = [[o * GROUP + i for o in range(outer)] for i in range(GROUP)]

    def spread(x, axis):
        if outer == 1:
            return x
        return lax.psum_scatter(x, "dp", scatter_dimension=axis, axis_index_groups=groups, tiled=True)

    sums = got.sums
    if outer > 1:
        sums = lax.psum(sums, "dp", axis_index_groups=groups)
    (
        layer_out, grad_tokens, grad_memory, qkv, self_out, cross_q, cross_out, fc_in, fc_out, kv,
        self_bias, cross_bias, hidden_bias, out_bias, gains, shifts,
    ) = finish(
        (
            got.layer_out, got.grad_tokens, got.grad_memory, got.g_qkv, got.g_self_out, got.g_cross_q, got.g_cross_out,
            got.g_fc_in, got.g_fc_out,
        ),
        got.g_kv,
        sums,
    )
    return (
        regroup(layer_out, 1, False),
        regroup(grad_tokens, 1, False),
        regroup(grad_memory, 1, False),
        spread(qkv, 1).transpose(1, 0, 2),
        self_bias,
        spread(self_out, 0).T,
        spread(cross_q, 0),
        spread(kv, 0),
        cross_bias,
        spread(cross_out, 0).T,
        spread(fc_in, 0),
        hidden_bias.reshape(-1),
        spread(fc_out, 0).T,
        regroup(out_bias, 1, False),
        regroup(gains, 1, False),
        regroup(shifts, 1, False),
    )


def solution(mesh):
    placed = (
        P("dp", None),
        P("dp", None),
        P("dp"),
        P("dp"),
        P("dp", None),
        P(None, None, "mp"),
        P(None, "mp"),
        P("mp", None),
        P(None, "mp"),
        P(None, None, "mp"),
        P(None, "mp"),
        P("mp", None),
        P(None, "mp"),
        P("mp"),
        P("mp", None),
        P(),
        P(),
        P(),
    )
    return jax.shard_map(
        per_device,
        mesh=mesh,
        in_specs=placed,
        out_specs=(
            P("dp", None),
            P("dp", None),
            P(("dp", "mp"), None),
            P("dp", None, "mp"),
            P(None, "mp"),
            P("mp", "dp"),
            P("dp", "mp"),
            P("dp", None, "mp"),
            P(None, "mp"),
            P("mp", "dp"),
            P("dp", "mp"),
            P("mp"),
            P("mp", "dp"),
            P(),
            P(),
            P(),
        ),
        check_vma=False,
    )
```

```python
import functools
import types

import jax
import jax.numpy as jnp
from jax import lax
from jax.experimental import pallas as pl
from jax.experimental.pallas import tpu as pltpu
from jax.sharding import PartitionSpec as P

HEAD = 64
LOG2E = 1.4426950408889634
GROUP = 16
epsilon = 1e-05
MESH = pl.DeviceIdType.MESH
f32, bf16 = jnp.float32, jnp.bfloat16

FC_OUT, FC_IN, CROSS_OUT, CROSS_Q, SELF_OUT, QKV, KV = 0, 4, 8, 9, 10, 11, 14
UNITS = 16
X_TOKENS, X_FIRST, X_SECOND, X_FFN, X_CROSS, X_SELF = range(6)


AXIS_Y, AXIS_Z = 0, 1


def axis_of(unit):
    return AXIS_Z if unit < FC_IN or unit in (CROSS_OUT, SELF_OUT) else AXIS_Y


def x_axis(x):
    return AXIS_Z if x in (X_FFN, X_CROSS, X_SELF) else AXIS_Y


def x_of(unit):
    return ((X_FFN,) * 4 + (X_SECOND,) * 4 + (X_CROSS, X_FIRST, X_SELF) + (X_TOKENS,) * 3)[unit]


def nn(a, b):
    return lax.dot_general(a, b, (((1,), (0,)), ((), ())), preferred_element_type=f32)


def nt(a, b):
    return lax.dot_general(a, b, (((1,), (1,)), ((), ())), preferred_element_type=f32)


def loop(count, body, unroll=1):
    def step(i, carry):
        for j in range(unroll):
            body(i * unroll + j)
        return carry

    if unroll == count:
        step(0, 0)
    else:
        lax.fori_loop(0, count // unroll, step, 0)


def at(index, size):
    return pl.ds(index * size if isinstance(index, int) else pl.multiple_of(index * size, size), size)


def kernel(names, refs_at, *refs):
    r = types.SimpleNamespace(**dict(zip(names, refs)))
    T, D = r.tokens.shape
    ML = r.memory.shape[0]
    HL = r.self_out.shape[0]
    FL = r.fc_out.shape[0]
    W = 512
    PAIRS = HL // 128
    CH = 128
    scale = HEAD**-0.5

    d, m = lax.axis_index("dp"), lax.axis_index("mp")
    c, y = lax.rem(d, 2), lax.rem(d // 2, 2)
    zl, zh = lax.rem(d // 4, 2), lax.rem(d // 8, 2)
    to_mp = (d, 1 - m)
    to_c = (d + 1 - 2 * c, m)
    to_y = (d + 2 - 4 * y, m)
    to_z1 = (d + 4 - 8 * zl, m)
    to_z2 = (d + 8 - 16 * zh, m)

    bits, partners_of = (y, zl), (to_y, to_z1)

    barrier = pltpu.get_barrier_semaphore()
    for partner in (to_mp, to_c, to_y, to_z1, to_z2):
        pl.semaphore_signal(barrier, inc=1, device_id=partner, device_id_type=MESH)

    given = {}
    local_given = {}

    def slot(key, count=1):
        if key not in given:
            given[key] = sum(n for _, n in given.values()), count
        return given[key][0]

    def remote(key, index, count, src, dst, partner):
        base = slot(key, count) + index
        return pltpu.make_async_remote_copy(
            src_ref=src,
            dst_ref=dst,
            send_sem=r.send_sem.at[base],
            recv_sem=r.recv_sem.at[base],
            device_id=partner,
            device_id_type=MESH,
        )

    def local(key, src, dst, index=0, count=1):
        if key not in local_given:
            local_given[key] = sum(n for _, n in local_given.values()), count
        return pltpu.make_async_copy(src, dst, r.local_sem.at[local_given[key][0] + index])

    def load(src):
        name = next(k for k, v in vars(r).items() if v is src)
        return local(name, src, getattr(r, name + "_v"))

    def load_qkv(part):
        return local("qkv", r.wqkv.at[part], r.wqkv_v.at[part], part, 3)

    first = (r.dec_len, r.mem_len, r.self_qv_bias, r.cross_qv_bias, r.fc_in_bias, r.out_bias, r.norm_gain, r.norm_bias)
    load(r.tokens).start()
    load_qkv(0).start()
    for src in first:
        load(src).start()
    load_qkv(1).start()
    load_qkv(2).start()
    for src in (r.self_out, r.memory, r.cross_kv, r.cross_q, r.cross_out, r.fc_in, r.fc_out, r.cotangent):
        load(src).start()

    gain, shift, out_bias = r.norm_gain_v, r.norm_bias_v, r.out_bias_v
    sm = r.sm
    ycat, xcat, xsend = r.ycat, r.xcat, r.xsend
    low = r.low
    lane_low = lax.broadcasted_iota(jnp.int32, (T, 128), 1) < HEAD

    def stacked(pair):
        wide = pair.astype(f32)
        return jnp.concatenate(
            [jnp.where(lane_low, wide, 0.0).astype(bf16), jnp.where(lane_low, 0.0, wide).astype(bf16)], axis=0
        )

    def unstacked(wide):
        return jnp.concatenate([wide[:HEAD, :T], wide[HEAD:, T:]], axis=0).T

    def col_sum(x):
        return jnp.sum(x, axis=0, keepdims=True)

    def send_x(w, src):
        g = x_axis(w)

        def block(q):
            high, o = q // 2, lax.rem(q, 2)
            row = o * 128 + high * 64
            for own in (True, False):
                side = bits[g] if own else 1 - bits[g]
                from_block = high * 4 + (o * 2 + side if g == AXIS_Y else side * 2 + o)
                t = src[:, at(from_block, 128)].astype(f32).T.astype(bf16)
                for half in range(2):
                    rows = pl.ds(pl.multiple_of(half * 256 + row, 64), 64)
                    piece = t[half * 64 : (half + 1) * 64]
                    if own:
                        xcat[w, rows, 0:128] = piece
                    else:
                        xsend[w, rows, :] = piece

        loop(4, block, 2)
        copy_x(w).start()

    def copy_x(w):
        rows = pl.ds(0, 512) if x_axis(w) == AXIS_Y else at(m, 256)
        return remote(
            ("x", w), 0, 1, xsend.at[w, rows, :], xcat.at[w, rows, pl.ds(128, 128)], partners_of[x_axis(w)]
        )

    def copy_shared(w, side):
        held = xcat.at[w, at(side, 256), pl.ds(128, 128)]
        return remote(("shared", w), 0, 1, held, held, to_mp)

    def share_x(w):
        copy_x(w).wait_recv()
        copy_shared(w, m).start()

    def copy_y(u):
        to = partners_of[axis_of(u)]
        return remote("gather", u, KV, ycat.at[u, pl.ds(0, T), :], ycat.at[u, pl.ds(T, T), :], to)

    def exchange_copy(k, j):
        s = k % 2
        return remote(("ex", k), j, 4, r.ex_out.at[s, j], r.ex_in.at[s, j], to_mp)

    def exchange_start(k, term):
        def step(j):
            r.ex_out[k % 2, j] = term(j).astype(bf16)
            exchange_copy(k, j).start()

        loop(4, step, 4)

    def exchange_wait(k):
        def step(j):
            exchange_copy(k, j).wait()

        loop(4, step)

    def exchanged(k, rows):
        s = k % 2
        return jnp.concatenate(
            [r.ex_out[s, j, rows, :].astype(f32) + r.ex_in[s, j, rows, :].astype(f32) for j in range(4)], axis=1
        )

    def kept(u):
        return r.fc_out_v.at[at(u % 8, 256), at(u // 8, W)]

    def core_out(u):
        return r.fc_in_v.at[at(u % 4, 256), at(u // 4, W)]

    def copy_core(u):
        return remote("core", u, KV, core_out(u), r.core_in.at[u], to_c)

    def copy_half(u):
        return remote("half", u, UNITS, r.half_out.at[u], r.half_in.at[u], partners_of[1 - axis_of(u)])

    def copy_last(u):
        return remote("last", u, UNITS, r.last_out.at[u], r.last_in.at[u], to_z2)

    def kvc_copy(v):
        return remote("kvc", v, 2, r.kvc_out.at[v], r.kvc_in.at[v], to_c)

    def kvy_copy(v):
        return remote("kvy", v, 2, r.kvy_out.at[v], r.kvy_in.at[v], to_y)

    arrived = set()

    def product(u):
        w = x_of(u)
        if w not in arrived:
            arrived.add(w)
            (copy_x(w) if x_axis(w) == AXIS_Y else copy_shared(w, 1 - m)).wait_recv()
        copy_y(u).wait_recv()
        for h in range(W // 256):
            cols = pl.ds(h * 256, 256)
            rhs = ycat[u, :, cols]
            core_out(u)[:, cols] = nn(xcat[w, at(1 - c, 256), :], rhs).astype(bf16)
            kept(u)[:, cols] = nn(xcat[w, at(c, 256), :], rhs).astype(bf16)
        copy_core(u).start()

    def local_sum(u, rows):
        if u < KV:
            return kept(u)[rows, :].astype(f32) + r.core_in[u, rows, :].astype(f32)
        v = u - KV
        wide = pl.ds(pl.multiple_of(y * 256 + rows.start, 64), rows.size)
        mine = r.memory_v[wide, pl.ds(v * W, W)].astype(f32) + r.kvc_in[v, wide, :].astype(f32)
        return mine + r.kvy_in[v, rows, :].astype(f32)

    def halve(u):
        if u < KV:
            copy_core(u).wait_recv()
        else:
            kvy_copy(u - KV).wait_recv()
        r.half_out[u] = local_sum(u, at(1 - bits[1 - axis_of(u)], 128)).astype(bf16)
        copy_half(u).start()

    def part_rows(u, high):
        return pl.ds(pl.multiple_of(bits[1 - axis_of(u)] * 128 + high * 64, 64), 64)

    def halve_last(u):
        copy_half(u).wait_recv()
        got = r.half_in[u, at(1 - zh, 64), :].astype(f32)
        r.last_out[u] = (local_sum(u, part_rows(u, 1 - zh)) + got).astype(bf16)
        copy_last(u).start()

    def out_copy(u):
        if u < FC_IN:
            to = r.g_fc_out.at[:, at(u, W)]
        elif u < CROSS_OUT:
            to = r.g_fc_in.at[:, at(u - FC_IN, W)]
        elif u < QKV:
            to = (r.g_cross_out, r.g_cross_q, r.g_self_out)[u - CROSS_OUT]
        elif u < KV:
            to = r.g_qkv.at[u - QKV]
        else:
            to = r.g_kv.at[u - KV]
        return local("unit", r.fin.at[u], to, u, UNITS)

    def total(u):
        copy_last(u).wait_recv()
        got = r.half_in[u, at(zh, 64), :].astype(f32) + r.last_in[u].astype(f32)
        r.fin[u] = local_sum(u, part_rows(u, zh)) + got
        out_copy(u).start()

    def project():
        load(r.tokens).wait()
        for part in range(3):
            load_qkv(part).wait()
            if part == 0:
                for src in first:
                    load(src).wait()

            def packed(j, part=part):
                cols = at(j, 256)
                x = nn(r.tokens_v[...], r.wqkv_v[part, :, cols])
                if part == 0:
                    x = x + r.self_qv_bias_v[0:1, cols]
                if part == 2:
                    x = x + r.self_qv_bias_v[1:2, cols]
                r.packed[part, :, cols] = x.astype(bf16)

            loop(HL // 256, packed, 2)

    key_row = lax.broadcasted_iota(jnp.int32, (T, 2 * T), 0)
    query_row = lax.rem(lax.broadcasted_iota(jnp.int32, (T, 2 * T), 1), T)

    def self_pair(p):
        cols = at(p, 128)
        q, k, v = (r.packed[i, :, cols] for i in range(3))
        s = nt(k, stacked(q)) * scale
        s = jnp.where((key_row <= query_row) & (key_row < r.dec_len_v[0]), s, -1e30)
        w = jnp.exp(s - jnp.max(s, axis=0, keepdims=True))
        probs = w / jnp.sum(w, axis=0, keepdims=True)
        r.self_probs[p] = probs
        mixed = nn(v.astype(f32).T.astype(bf16), probs.astype(bf16))
        ycat[SELF_OUT, 0:T, cols] = unstacked(mixed).astype(bf16)

    def self_attention():
        loop(PAIRS, self_pair, 4)

    def send_first():
        load(r.self_out).wait()
        pl.semaphore_wait(barrier, 5)
        exchange_start(0, lambda j: nn(ycat[SELF_OUT, 0:T, :], r.self_out_v[:, at(j, 256)]))
        copy_y(SELF_OUT).start()
        load(r.memory).wait()

    key, value, turned = r.key, r.value, r.turned
    odd = lax.broadcasted_iota(jnp.int32, (256, 256), 0)
    odd = jnp.where(odd < 128, 2 * odd, 2 * odd - 255)
    select = (lax.broadcasted_iota(jnp.int32, (256, 256), 1) == odd).astype(f32).astype(bf16)

    def part_weights(i):
        rows = at(i, CH)
        x = nn(select, r.cross_kv_v[rows].reshape(2 * CH, HL)).astype(bf16)
        r.wkv_v[0, rows, :] = x[:CH]
        r.wkv_v[1, rows, :] = x[CH:]

    def pair_rows(i):
        rows = at(i, CH)
        x = r.memory_v[rows, :]
        for j in range(HL // 256):
            cols = pl.ds(j * 256, 256)
            key[rows, cols] = nn(x, r.wkv_v[0, :, cols]).astype(bf16)
            val = (nn(x, r.wkv_v[1, :, cols]) + r.cross_qv_bias_v[1:2, cols]).astype(bf16)
            value[rows, cols] = val

    def turn(src):
        def step(i):
            rows = at(i, CH)
            for j in range(HL // 128):
                turned[pl.ds(j * 128, 128), rows] = src[rows, pl.ds(j * 128, 128)].astype(f32).T.astype(bf16)

        loop(ML // CH, step, 2)

    def memory_pair():
        load(r.cross_kv).wait()
        loop(D // CH, part_weights, 2)
        loop(ML // CH, pair_rows, 2)
        turn(value)

    def turn_memory(i):
        rows = at(i, CH)

        def block(b):
            t = r.memory_v[rows, at(b, 128)].astype(f32).T.astype(bf16)
            side, zlow, zhigh = lax.rem(b, 2), lax.rem(b // 2, 2), b // 4
            for half in range(2):
                to = half * 512 + side * 256 + zlow * 128 + zhigh * 64
                r.memory_t[pl.ds(pl.multiple_of(to, 64), 64), rows] = t[half * 64 : (half + 1) * 64]

        loop(D // 128, block, 4)

    def normalize(v, k):
        mean = jnp.mean(v, axis=-1, keepdims=True)
        centred = v - mean
        inv = lax.rsqrt(jnp.mean(centred * centred, axis=-1, keepdims=True) + epsilon)
        unit = centred * inv
        return unit * gain[k : k + 1, :] + shift[k : k + 1, :], unit, inv

    def norm_back(g, unit, inv, k):
        w = g * gain[k : k + 1, :]
        return inv * (w - jnp.mean(w, axis=-1, keepdims=True) - unit * jnp.mean(w * unit, axis=-1, keepdims=True))

    def norm_rows(k, base, unit_ref):
        def body(i):
            rows = at(i, 16)
            v = base[rows, :].astype(f32) + (exchanged(k, rows) + out_bias[k : k + 1, :])
            norm, unit, inv = normalize(v, k)
            r.norm[rows, :] = norm
            unit_ref[rows, :] = unit
            r.inv[k, rows, :] = jnp.broadcast_to(inv, (16, 128))
            low[rows, :] = norm.astype(bf16)

        exchange_wait(k)
        loop(T // 16, body, T // 16)

    def first_norm():
        norm_rows(0, r.tokens_v, r.unit0)

    def cross_query(j):
        cols = at(j, 256)
        x = nn(low[...], r.cross_q_v[:, cols]) + r.cross_qv_bias_v[0:1, cols]
        r.query[:, cols] = x.astype(bf16)

    probs_ref = r.probs
    low_probs = r.low_probs
    mem_row = lax.broadcasted_iota(jnp.int32, (CH, 2 * T), 0)
    chunks = ML // CH

    def fold(x, op):
        total = x[0:8]
        for i in range(1, x.shape[0] // 8):
            total = op(total, x[8 * i : 8 * i + 8])
        return total

    def cross_pair(p):
        cols = at(p, 128)
        q = stacked(r.query[:, cols])
        top = jnp.full((8, 2 * T), -1e30, f32)
        for i in range(chunks):
            rows = at(i, CH)
            s = nt(key[rows, cols], q) * (scale * LOG2E)
            s = jnp.where(mem_row < r.mem_len_v[0] - i * CH, s, -1e30)
            probs_ref[p, rows, :] = s
            top = jnp.maximum(top, fold(s, jnp.maximum))
        top = jnp.max(top, axis=0, keepdims=True)
        total = jnp.zeros((8, 2 * T), f32)
        for i in range(chunks):
            rows = at(i, CH)
            w = jnp.exp2(probs_ref[p, rows, :] - top)
            probs_ref[p, rows, :] = w
            low_probs[rows, :] = w.astype(bf16)
            total = total + fold(w, jnp.add)
        part = 1.0 / jnp.sum(total, axis=0, keepdims=True)
        r.part[p] = jnp.broadcast_to(part, (8, 2 * T))
        mixed = nn(turned[cols, :], low_probs[...]) * part
        ycat[CROSS_OUT, 0:T, cols] = unstacked(mixed).astype(bf16)

    def cross_attention():
        load(r.cross_q).wait()
        loop(HL // 256, cross_query, 2)
        loop(PAIRS, cross_pair)

    def send_second():
        load(r.cross_out).wait()
        exchange_start(1, lambda j: nn(ycat[CROSS_OUT, 0:T, :], r.cross_out_v[:, at(j, 256)]))
        copy_y(CROSS_OUT).start()

    def second_norm():
        norm_rows(1, r.norm, r.unit1)

    def ffn(j):
        cols = at(j, 256)
        h = nn(low[...], r.fc_in_v[:, cols]) + r.fc_in_bias_v[:, cols]
        phi = 0.5 * (1.0 + lax.erf(h * 0.7071067811865476))
        slope = phi + h * jnp.exp(-0.5 * h * h) * 0.3989422804014327
        r.slope[:, cols] = slope
        ycat[FC_OUT + j // 2, 0:T, at(lax.rem(j, 2), 256)] = (h * phi).astype(bf16)

    def hidden_units():
        load(r.fc_in).wait()
        for b in range(FL // W):
            ffn(2 * b)
            ffn(2 * b + 1)
            copy_y(FC_OUT + b).start()

    def ffn_term(j):
        cols = at(j, 256)
        total = nn(ycat[FC_OUT, 0:T, :], r.fc_out_v[pl.ds(0, W), cols])
        for b in range(1, FL // W):
            total = total + nn(ycat[FC_OUT + b, 0:T, :], r.fc_out_v[pl.ds(b * W, W), cols])
        return total

    def send_third():
        load(r.fc_out).wait()
        exchange_start(2, ffn_term)

    row16 = lax.broadcasted_iota(jnp.int32, (16, D), 0)
    zero8 = jnp.zeros((8, D), f32)

    def sums_of(body, k):
        def step(i, carry):
            g, unit, rounded = body(i)
            return (
                carry[0] + fold(rounded, jnp.add),
                carry[1] + fold(g * unit, jnp.add),
                carry[2] + fold(g, jnp.add),
            )

        carry = (zero8, zero8, zero8)
        for i in range(T // 16):
            carry = step(i, carry)
        bias, gains, shifts = carry
        sm[k : k + 1, :] = col_sum(bias)
        sm[3 + k : 4 + k, :] = col_sum(gains)
        sm[6 + k : 7 + k, :] = col_sum(shifts)

    def output_rows(i):
        rows = at(i, 16)
        v = r.norm[rows, :] + (exchanged(2, rows) + out_bias[2:3, :])
        norm, unit, inv = normalize(v, 2)
        r.layer_v[rows, :] = norm.astype(bf16)
        g = jnp.where(row16 + i * 16 < r.dec_len_v[0], r.cotangent_v[rows, :].astype(f32), 0.0)
        grad = norm_back(g, unit, inv, 2)
        r.grad[rows, :] = grad
        rounded = grad.astype(bf16)
        low[rows, :] = rounded
        return g, unit, rounded.astype(f32)

    def layer_copy():
        return local("layer", r.layer_v, r.layer_out)

    def output_norm():
        load(r.cotangent).wait()
        exchange_wait(2)
        sums_of(output_rows, 2)
        layer_copy().start()

    def hidden_grad(j):
        cols = at(j, 256)
        g = nt(low[...], r.fc_out_v[at(j, 256), :]) * r.slope[:, cols]
        rounded = g.astype(bf16)
        ycat[FC_IN + j // 2, 0:T, at(j % 2, 256)] = rounded
        sm[pl.ds(11 + j // 4, 1), at(j % 4, 256)] = col_sum(rounded.astype(f32))

    def hidden_grads():
        for b in range(FL // W):
            hidden_grad(2 * b)
            hidden_grad(2 * b + 1)
            copy_y(FC_IN + b).start()

    def hidden_term(j):
        rows = at(j, 256)
        total = nt(ycat[FC_IN, 0:T, :], r.fc_in_v[rows, pl.ds(0, W)])
        for b in range(1, FL // W):
            total = total + nt(ycat[FC_IN + b, 0:T, :], r.fc_in_v[rows, pl.ds(b * W, W)])
        return total

    def send_fourth():
        exchange_start(3, hidden_term)

    def grad_rows(k, e, unit_ref):
        def body(i):
            rows = at(i, 16)
            g = r.grad[rows, :] + exchanged(e, rows)
            unit = unit_ref[rows, :]
            grad = norm_back(g, unit, r.inv[k, rows, 0:1], k)
            r.grad[rows, :] = grad
            rounded = grad.astype(bf16)
            low[rows, :] = rounded
            return g, unit, rounded.astype(f32)

        exchange_wait(e)
        sums_of(body, k)

    mixed_grad = r.mixed_grad

    def second_back():
        grad_rows(1, 3, r.unit1)

    def mixed_from(weights):
        for j in range(HL // 256):
            mixed_grad[:, at(j, 256)] = nt(low[...], weights[at(j, 256), :]).astype(bf16)

    def cross_mixed_grad():
        mixed_from(r.cross_out_v)

    dp_ref = r.dp

    def cross_back(p):
        cols = at(p, 128)
        q = stacked(r.query[:, cols])
        g = stacked(mixed_grad[:, cols])
        part = r.part[p, 0:1, :]
        total = jnp.zeros((8, 2 * T), f32)
        for i in range(chunks):
            rows = at(i, CH)
            probs = probs_ref[p, rows, :] * part
            dprobs = nt(value[rows, cols], g)
            dp_ref[rows, :] = dprobs
            probs_ref[p, rows, :] = probs
            value[rows, cols] = nn(probs.astype(bf16), g).astype(bf16)
            total = total + fold(probs * dprobs, jnp.add)
        total = jnp.sum(total, axis=0, keepdims=True)
        for i in range(chunks):
            rows = at(i, CH)
            ds = (probs_ref[p, rows, :] * (dp_ref[rows, :] - total)).astype(bf16)
            low_probs[rows, :] = ds
            key[rows, cols] = (nn(ds, q) * scale).astype(bf16)
        dq = nn(turned[cols, :], low_probs[...])
        ycat[CROSS_Q, 0:T, cols] = (unstacked(dq) * scale).astype(bf16)

    def send_fifth():
        exchange_start(4, lambda j: nt(ycat[CROSS_Q, 0:T, :], r.cross_q_v[at(j, 256), :]))
        copy_y(CROSS_Q).start()
        sm[10:11, 0:HL] = col_sum(ycat[CROSS_Q, 0:T, :].astype(f32))
        sm[10:11, HL : 2 * HL] = col_sum(value[...].astype(f32))

    def gm_copy(i):
        return remote("gm", i, 4, r.gm_out.at[i], r.gm_in.at[i], to_mp)

    def memory_term(i):
        for half, to in (((1 - m) * 4 + i, r.gm_out), (m * 4 + i, r.gm_own)):
            rows = at(half, CH)
            for j in range(D // 256):
                cols = pl.ds(j * 256, 256)
                x = nt(key[rows, :], r.wkv_v[0, cols, :]) + nt(value[rows, :], r.wkv_v[1, cols, :])
                to[i, :, cols] = x.astype(bf16)
        gm_copy(i).start()

    def gm_store(i):
        return local("gm_store", r.gm_own.at[i], r.grad_memory.at[at(i, CH), :], i, 4)

    def memory_sum(i):
        gm_copy(i).wait()
        r.gm_own[i] = (r.gm_own[i].astype(f32) + r.gm_in[i].astype(f32)).astype(bf16)
        gm_store(i).start()

    def pair_product(v):
        pair = key if v == 0 else value
        for h in range(2):
            cols = pl.ds(h * 256, 256)

            def step(b, cols=cols, h=h):
                rows = at(b, 128)
                other, own = r.memory_t[at((1 - c) * 4 + b, 128), :], r.memory_t[at(c * 4 + b, 128), :]
                r.kvc_out[v, rows, cols] = nn(other, pair[:, cols]).astype(bf16)
                r.memory_v[rows, pl.ds(v * W + h * 256, 256)] = nn(own, pair[:, cols]).astype(bf16)

            loop(4, step)
        kvc_copy(v).start()

    def pair_halve(v):
        kvc_copy(v).wait_recv()
        rows = at(1 - y, 256)
        mine = r.memory_v[rows, pl.ds(v * W, W)].astype(f32)
        r.kvy_out[v] = (mine + r.kvc_in[v, rows, :].astype(f32)).astype(bf16)
        kvy_copy(v).start()

    def first_back():
        grad_rows(0, 4, r.unit0)

    def self_back(p):
        cols = at(p, 128)
        q, k, v = (r.packed[i, :, cols] for i in range(3))
        probs = r.self_probs[p]
        g = stacked(mixed_grad[:, cols])
        dprobs = nt(v, g)
        ycat[QKV + 2, 0:T, cols] = nn(probs.astype(bf16), g).astype(bf16)
        ds = (probs * (dprobs - jnp.sum(probs * dprobs, axis=0, keepdims=True))).astype(bf16)
        ycat[QKV + 1, 0:T, cols] = (nn(ds, stacked(q)) * scale).astype(bf16)
        dq = nn(k.astype(f32).T.astype(bf16), ds)
        ycat[QKV, 0:T, cols] = (unstacked(dq) * scale).astype(bf16)

    def self_grads():
        mixed_from(r.self_out_v)
        loop(PAIRS, self_back, 4)
        for b in range(3):
            copy_y(QKV + b).start()
        sm[9:10, 0:HL] = col_sum(ycat[QKV, 0:T, :].astype(f32))
        sm[9:10, HL : 2 * HL] = col_sum(ycat[QKV + 2, 0:T, :].astype(f32))
        sm[13:16, :] = jnp.zeros((3, D), f32)

    def packed_term(j):
        rows = at(j, 256)
        total = nt(ycat[QKV, 0:T, :], r.wqkv_v[0, rows, :])
        for b in range(1, 3):
            total = total + nt(ycat[QKV + b, 0:T, :], r.wqkv_v[b, rows, :])
        return total

    def send_sixth():
        exchange_start(5, packed_term)

    def token_copy():
        return local("tokens_g", r.tokens_g, r.grad_tokens)

    def token_grads():
        def body(i):
            rows = at(i, 16)
            r.tokens_g[rows, :] = (r.grad[rows, :] + exchanged(5, rows)).astype(bf16)

        exchange_wait(5)
        loop(T // 16, body, 2)
        token_copy().start()

    doubling = (to_c, to_y, to_z1, to_z2)

    def small_copy(k):
        return remote("small", k, 4, r.sm_out.at[k], r.sm_in.at[k], doubling[k])

    def sums_copy():
        return local("sums", sm, r.sums)

    def small_step(k):
        if k > 0:
            small_copy(k - 1).wait()
            sm[...] = r.sm_out[k - 1].astype(f32) + r.sm_in[k - 1].astype(f32)
        if k < 4:
            r.sm_out[k] = sm[...].astype(bf16)
            small_copy(k).start()
        else:
            sums_copy().start()

    def each(step, *indices):
        for i in indices:
            step(i)

    project()
    self_attention()
    send_first()
    each(turn_memory, 6, 0)
    memory_pair()
    each(turn_memory, 5)
    send_x(X_TOKENS, r.tokens_v)
    each(turn_memory, 7)
    first_norm()
    cross_attention()
    send_second()
    send_x(X_FIRST, low)
    turn(key)
    each(turn_memory, 4, 1, 2, 3)
    second_norm()
    hidden_units()
    send_third()
    send_x(X_SECOND, low)
    output_norm()
    send_x(X_FFN, low)
    hidden_grads()
    send_fourth()
    each(product, 4)
    share_x(X_FFN)
    each(halve, 4)
    each(product, 5)
    second_back()
    each(halve, 5)
    send_x(X_CROSS, low)
    cross_mixed_grad()
    each(cross_back, 0, 1)
    each(product, 3, 1, 6, 7)
    each(halve_last, 4)
    each(cross_back, 2)
    each(halve, 3, 6, 1)
    each(halve_last, 5)
    each(product, 0)
    each(halve, 7)
    each(product, 2)
    share_x(X_CROSS)
    each(cross_back, 3)
    send_fifth()
    each(halve, 0, 2)
    each(memory_term, 3)
    each(total, 4)
    each(product, 8)
    each(halve_last, 3)
    each(memory_term, 0)
    each(halve_last, 6)
    each(pair_product, 0)
    first_back()
    send_x(X_SELF, low)
    each(halve_last, 1, 7)
    each(halve, 8)
    self_grads()
    each(small_step, 0)
    each(product, 9)
    each(pair_halve, 0)
    send_sixth()
    each(small_step, 1)
    each(total, 3)
    share_x(X_SELF)
    each(halve, 9)
    each(memory_sum, 3)
    each(halve_last, 0)
    each(total, 5)
    each(memory_term, 1)
    each(total, 6)
    each(halve_last, 2)
    each(memory_term, 2)
    each(pair_product, 1)
    each(halve_last, 8, 9)
    each(memory_sum, 0)
    each(total, 1, 7)
    each(product, 11)
    each(pair_halve, 1)
    each(halve, 11)
    each(total, 0)
    each(product, 12)
    token_grads()
    each(halve, 12)
    each(product, 10)
    each(total, 2)
    each(product, 13)
    each(halve_last, 11)
    each(halve, 10, 13)
    each(total, 8)
    each(halve_last, 12)
    each(memory_sum, 1)
    each(total, 9)
    each(halve, 14)
    each(small_step, 2)
    each(halve_last, 13)
    each(total, 11)
    each(memory_sum, 2)
    each(total, 12)
    each(halve_last, 14)
    each(halve, 15)
    each(small_step, 3)
    each(halve_last, 10)
    each(total, 13)
    each(halve_last, 15)
    each(total, 14)
    each(small_step, 4)
    each(total, 10, 15)
    for w in range(6):
        copy_x(w).wait_send()
        if x_axis(w) == AXIS_Z:
            copy_shared(w, m).wait_send()
    for u in range(UNITS):
        if u < KV:
            copy_y(u).wait_send()
            copy_core(u).wait_send()
        copy_half(u).wait_send()
        copy_last(u).wait_send()
        out_copy(u).wait()
    for v in range(2):
        kvc_copy(v).wait_send()
        kvy_copy(v).wait_send()
    for i in range(4):
        gm_store(i).wait()
    layer_copy().wait()
    token_copy().wait()
    sums_copy().wait()
    refs_at.update(remote=sum(n for _, n in given.values()), local=sum(n for _, n in local_given.values()))


REMOTE_SEMS = 144
LOCAL_SEMS = 64


def layer(tokens, memory, mem_len, dec_len, cotangent, wqkv, self_qv_bias, self_out, cross_q, cross_kv, cross_qv_bias, cross_out, fc_in, fc_in_bias, fc_out, out_bias, norm_gain, norm_bias):
    T, D = tokens.shape
    ML = memory.shape[0]
    HL = self_out.shape[0]
    FL = fc_out.shape[0]
    R = D // GROUP
    W = 512
    PAIRS = HL // 128
    anywhere = pl.BlockSpec(memory_space=pl.ANY)
    big = dict(tokens=tokens, memory=memory, cotangent=cotangent, wqkv=wqkv, self_out=self_out, cross_q=cross_q, cross_kv=cross_kv,
               cross_out=cross_out, fc_in=fc_in, fc_out=fc_out)
    small = dict(self_qv_bias=self_qv_bias, cross_qv_bias=cross_qv_bias, fc_in_bias=fc_in_bias, out_bias=out_bias,
                 norm_gain=norm_gain, norm_bias=norm_bias)
    scalars = dict(mem_len=mem_len, dec_len=dec_len)
    outs = dict(
        layer_out=((T, D), bf16),
        grad_tokens=((T, D), bf16),
        grad_memory=((ML // 2, D), bf16),
        g_qkv=((3, R, HL), f32),
        g_self_out=((R, HL), f32),
        g_cross_q=((R, HL), f32),
        g_kv=((2, R, HL), f32),
        g_cross_out=((R, HL), f32),
        g_fc_in=((R, FL), f32),
        g_fc_out=((R, FL), f32),
        sums=((16, D), f32),
    )
    scratch = {name + "_v": (x.shape, x.dtype) for name, x in (big | small).items()}
    scratch |= dict(
        wkv_v=((2, D, HL), bf16),
        packed=((3, T, HL), bf16),
        self_probs=((PAIRS, T, 2 * T), f32),
        low=((T, D), bf16),
        ycat=((KV, 2 * T, W), bf16),
        xcat=((6, 512, 256), bf16),
        xsend=((6, 512, 128), bf16),
        ex_out=((2, 4, T, 256), bf16),
        ex_in=((2, 4, T, 256), bf16),
        norm=((T, D), f32),
        unit0=((T, D), f32),
        unit1=((T, D), f32),
        inv=((2, T, 128), f32),
        grad=((T, D), f32),
        key=((ML, HL), bf16),
        value=((ML, HL), bf16),
        turned=((HL, ML), bf16),
        query=((T, HL), bf16),
        mixed_grad=((T, HL), bf16),
        probs=((PAIRS, ML, 2 * T), f32),
        part=((PAIRS, 8, 2 * T), f32),
        low_probs=((ML, 2 * T), bf16),
        dp=((ML, 2 * T), f32),
        slope=((T, FL), f32),
        memory_t=((D, ML), bf16),
        layer_v=((T, D), bf16),
        tokens_g=((T, D), bf16),
        gm_out=((4, 128, D), bf16),
        gm_own=((4, 128, D), bf16),
        gm_in=((4, 128, D), bf16),
        core_in=((KV, 256, W), bf16),
        kvc_out=((2, 512, W), bf16),
        kvc_in=((2, 512, W), bf16),
        kvy_out=((2, 256, W), bf16),
        kvy_in=((2, 256, W), bf16),
        half_out=((UNITS, 128, W), bf16),
        half_in=((UNITS, 128, W), bf16),
        last_out=((UNITS, 64, W), bf16),
        last_in=((UNITS, 64, W), bf16),
        fin=((UNITS, 64, W), f32),
        sm=((16, D), f32),
        sm_out=((4, 16, D), bf16),
        sm_in=((4, 16, D), bf16),
    )
    sems = dict(send_sem=REMOTE_SEMS, recv_sem=REMOTE_SEMS, local_sem=LOCAL_SEMS)
    lengths = {name + "_v": pltpu.SMEM((1,), jnp.int32) for name in scalars}
    names = [*big, *small, *scalars, *outs, *scratch, *lengths, *sems]
    got = {}
    out = pl.pallas_call(
        functools.partial(kernel, names, got),
        out_shape=[jax.ShapeDtypeStruct(s, t) for s, t in outs.values()],
        in_specs=[anywhere] * (len(big) + len(small) + len(scalars)),
        out_specs=[anywhere] * len(outs),
        scratch_shapes=[pltpu.VMEM(s, t) for s, t in scratch.values()]
        + [*lengths.values()]
        + [pltpu.SemaphoreType.DMA((count,)) for count in sems.values()],
        compiler_params=pltpu.CompilerParams(
            collective_id=0, has_side_effects=True, vmem_limit_bytes=63 * 2**20
        ),
        name="layer",
    )(*big.values(), *small.values(), *scalars.values())
    assert got["remote"] <= REMOTE_SEMS and got["local"] <= LOCAL_SEMS, got
    return types.SimpleNamespace(**dict(zip(outs, out)))


def finish_kernel(count, small, *refs):
    ins, outs, scratch = refs[: count + 2], refs[count + 2 : 2 * count + 3 + small], refs[2 * count + 3 + small :]
    held, turned, made, (in_sem, out_sem) = scratch[: count + 2], scratch[count + 2], scratch[count + 3 : -2], scratch[-2:]
    loads = [pltpu.make_async_copy(a, b, in_sem.at[i]) for i, (a, b) in enumerate(zip(ins, held))]
    stores = [
        pltpu.make_async_copy(a, b, out_sem.at[i]) for i, (a, b) in enumerate(zip((*held[:count], turned, *made), outs))
    ]
    for load in loads[::-1]:
        load.start()
    loads[count + 1].wait()
    sums = held[count + 1]
    self_bias, cross_bias, hidden_bias, out_bias, gains, shifts = made
    width = self_bias.shape[1]
    for row, to in ((9, self_bias), (10, cross_bias)):
        for part in range(2):
            to[part : part + 1, :] = sums[row : row + 1, part * width : (part + 1) * width]
    features = sums.shape[1]
    for part in range(hidden_bias.shape[1] // features):
        hidden_bias[:, part * features : (part + 1) * features] = sums[11 + part : 12 + part, :]
    for first, to in ((0, out_bias), (3, gains), (6, shifts)):
        to[...] = sums[first : first + 3, :]
    for i in range(small):
        stores[count + 1 + i].start()
    loads[count].wait()
    for part in range(2):
        turned[:, part, :] = held[count][part]
    stores[count].start()
    for i in range(count):
        loads[i].wait()
        stores[i].start()
    for store in stores:
        store.wait()


def finish(whole, kv, sums):
    R, HL = kv.shape[1:]
    D = sums.shape[1]
    anywhere = pl.BlockSpec(memory_space=pl.ANY)
    small = [(2, HL), (2, HL), (1, 4 * HL), (3, D), (3, D), (3, D)]
    return pl.pallas_call(
        functools.partial(finish_kernel, len(whole), len(small)),
        out_shape=[jax.ShapeDtypeStruct(x.shape, x.dtype) for x in whole]
        + [jax.ShapeDtypeStruct((R, 2, HL), f32)]
        + [jax.ShapeDtypeStruct(shape, f32) for shape in small],
        in_specs=[anywhere] * (len(whole) + 2),
        out_specs=[anywhere] * (len(whole) + 1 + len(small)),
        scratch_shapes=[pltpu.VMEM(x.shape, x.dtype) for x in (*whole, kv, sums)]
        + [pltpu.VMEM(shape, f32) for shape in [(R, 2, HL), *small]]
        + [pltpu.SemaphoreType.DMA((len(whole) + 2,)), pltpu.SemaphoreType.DMA((len(whole) + 1 + len(small),))],
        compiler_params=pltpu.CompilerParams(vmem_limit_bytes=63 * 2**20),
        name="finish",
    )(*whole, kv, sums)


def per_device(tokens, memory, mem_len, dec_len, cotangent, self_qkv, self_qv_bias, self_out, cross_q, cross_kv, cross_qv_bias, cross_out, fc_in, fc_in_bias, fc_out, out_bias, norm_gain, norm_bias):
    D = tokens.shape[1]
    devices = lax.axis_size("dp")
    outer = devices // GROUP

    def regroup(x, axis, there):
        if outer == 1:
            return x
        sizes = (outer, GROUP) if there else (GROUP, outer)
        shape = x.shape
        x = x.reshape(shape[:axis] + sizes + (D // devices,) + shape[axis + 1 :])
        return jnp.swapaxes(x, axis, axis + 1).reshape(shape)

    tokens, memory, cotangent, self_out, cross_out, fc_out, out_bias, norm_gain, norm_bias = (
        regroup(x, 1, True)
        for x in (tokens, memory, cotangent, self_out, cross_out, fc_out, out_bias, norm_gain, norm_bias)
    )
    self_qkv, cross_q, cross_kv, fc_in = (regroup(x, 0, True) for x in (self_qkv, cross_q, cross_kv, fc_in))
    got = layer(
        tokens, memory, mem_len, dec_len, cotangent, self_qkv.transpose(1, 0, 2), self_qv_bias, self_out, cross_q,
        cross_kv, cross_qv_bias, cross_out, fc_in, fc_in_bias.reshape(1, -1), fc_out, out_bias,
        norm_gain, norm_bias,
    )
    groups = [[o * GROUP + i for o in range(outer)] for i in range(GROUP)]

    def spread(x, axis):
        if outer == 1:
            return x
        return lax.psum_scatter(x, "dp", scatter_dimension=axis, axis_index_groups=groups, tiled=True)

    sums = got.sums
    if outer > 1:
        sums = lax.psum(sums, "dp", axis_index_groups=groups)
    (
        layer_out, grad_tokens, grad_memory, qkv, self_out, cross_q, cross_out, fc_in, fc_out, kv,
        self_bias, cross_bias, hidden_bias, out_bias, gains, shifts,
    ) = finish(
        (
            got.layer_out, got.grad_tokens, got.grad_memory, got.g_qkv, got.g_self_out, got.g_cross_q, got.g_cross_out,
            got.g_fc_in, got.g_fc_out,
        ),
        got.g_kv,
        sums,
    )
    return (
        regroup(layer_out, 1, False),
        regroup(grad_tokens, 1, False),
        regroup(grad_memory, 1, False),
        spread(qkv, 1).transpose(1, 0, 2),
        self_bias,
        spread(self_out, 0).T,
        spread(cross_q, 0),
        spread(kv, 0),
        cross_bias,
        spread(cross_out, 0).T,
        spread(fc_in, 0),
        hidden_bias.reshape(-1),
        spread(fc_out, 0).T,
        regroup(out_bias, 1, False),
        regroup(gains, 1, False),
        regroup(shifts, 1, False),
    )


def solution(mesh):
    placed = (
        P("dp", None),
        P("dp", None),
        P("dp"),
        P("dp"),
        P("dp", None),
        P(None, None, "mp"),
        P(None, "mp"),
        P("mp", None),
        P(None, "mp"),
        P(None, None, "mp"),
        P(None, "mp"),
        P("mp", None),
        P(None, "mp"),
        P("mp"),
        P("mp", None),
        P(),
        P(),
        P(),
    )
    return jax.shard_map(
        per_device,
        mesh=mesh,
        in_specs=placed,
        out_specs=(
            P("dp", None),
            P("dp", None),
            P(("dp", "mp"), None),
            P("dp", None, "mp"),
            P(None, "mp"),
            P("mp", "dp"),
            P("dp", "mp"),
            P("dp", None, "mp"),
            P(None, "mp"),
            P("mp", "dp"),
            P("dp", "mp"),
            P("mp"),
            P("mp", "dp"),
            P(),
            P(),
            P(),
        ),
        check_vma=False,
    )
```

```python
import functools
import types

import jax
import jax.numpy as jnp
from jax import lax
from jax.experimental import pallas as pl
from jax.experimental.pallas import tpu as pltpu
from jax.sharding import PartitionSpec as P

HEAD = 64
LOG2E = 1.4426950408889634
GROUP = 16
epsilon = 1e-05
MESH = pl.DeviceIdType.MESH
f32, bf16 = jnp.float32, jnp.bfloat16

FC_OUT, FC_IN, CROSS_OUT, CROSS_Q, SELF_OUT, QKV, KV = 0, 4, 8, 9, 10, 11, 14
UNITS = 16
X_TOKENS, X_FIRST, X_SECOND, X_FFN, X_CROSS, X_SELF = range(6)


AXIS_Y, AXIS_Z = 0, 1


def axis_of(unit):
    return AXIS_Z if unit < FC_IN or unit in (CROSS_OUT, SELF_OUT) else AXIS_Y


def x_axis(x):
    return AXIS_Z if x in (X_FFN, X_CROSS, X_SELF) else AXIS_Y


def x_of(unit):
    return ((X_FFN,) * 4 + (X_SECOND,) * 4 + (X_CROSS, X_FIRST, X_SELF) + (X_TOKENS,) * 3)[unit]


def nn(a, b):
    return lax.dot_general(a, b, (((1,), (0,)), ((), ())), preferred_element_type=f32)


def nt(a, b):
    return lax.dot_general(a, b, (((1,), (1,)), ((), ())), preferred_element_type=f32)


def loop(count, body, unroll=1):
    def step(i, carry):
        for j in range(unroll):
            body(i * unroll + j)
        return carry

    if unroll == count:
        step(0, 0)
    else:
        lax.fori_loop(0, count // unroll, step, 0)


def at(index, size):
    return pl.ds(index * size if isinstance(index, int) else pl.multiple_of(index * size, size), size)


def kernel(names, refs_at, *refs):
    r = types.SimpleNamespace(**dict(zip(names, refs)))
    T, D = r.tokens.shape
    ML = r.memory.shape[0]
    HL = r.self_out.shape[0]
    FL = r.fc_out.shape[0]
    W = 512
    PAIRS = HL // 128
    CH = 128
    scale = HEAD**-0.5

    d, m = lax.axis_index("dp"), lax.axis_index("mp")
    c, y = lax.rem(d, 2), lax.rem(d // 2, 2)
    zl, zh = lax.rem(d // 4, 2), lax.rem(d // 8, 2)
    to_mp = (d, 1 - m)
    to_c = (d + 1 - 2 * c, m)
    to_y = (d + 2 - 4 * y, m)
    to_z1 = (d + 4 - 8 * zl, m)
    to_z2 = (d + 8 - 16 * zh, m)

    bits, partners_of = (y, zl), (to_y, to_z1)

    barrier = pltpu.get_barrier_semaphore()
    for partner in (to_mp, to_c, to_y, to_z1, to_z2):
        pl.semaphore_signal(barrier, inc=1, device_id=partner, device_id_type=MESH)

    given = {}
    local_given = {}

    def slot(key, count=1):
        if key not in given:
            given[key] = sum(n for _, n in given.values()), count
        return given[key][0]

    def remote(key, index, count, src, dst, partner):
        base = slot(key, count) + index
        return pltpu.make_async_remote_copy(
            src_ref=src,
            dst_ref=dst,
            send_sem=r.send_sem.at[base],
            recv_sem=r.recv_sem.at[base],
            device_id=partner,
            device_id_type=MESH,
        )

    def local(key, src, dst, index=0, count=1):
        if key not in local_given:
            local_given[key] = sum(n for _, n in local_given.values()), count
        return pltpu.make_async_copy(src, dst, r.local_sem.at[local_given[key][0] + index])

    def load(src):
        name = next(k for k, v in vars(r).items() if v is src)
        return local(name, src, getattr(r, name + "_v"))

    def load_qkv(part):
        return local("qkv", r.wqkv.at[part], r.wqkv_v.at[part], part, 3)

    first = (r.dec_len, r.mem_len, r.self_qv_bias, r.cross_qv_bias, r.fc_in_bias, r.out_bias, r.norm_gain, r.norm_bias)
    load(r.tokens).start()
    load_qkv(0).start()
    for src in first:
        load(src).start()
    load_qkv(1).start()
    load_qkv(2).start()
    for src in (r.self_out, r.memory, r.cross_kv, r.cross_q, r.cross_out, r.fc_in, r.fc_out, r.cotangent):
        load(src).start()

    gain, shift, out_bias = r.norm_gain_v, r.norm_bias_v, r.out_bias_v
    sm = r.sm
    ycat, xcat, xsend = r.ycat, r.xcat, r.xsend
    low = r.low
    lane_low = lax.broadcasted_iota(jnp.int32, (T, 128), 1) < HEAD

    def stacked(pair):
        wide = pair.astype(f32)
        return jnp.concatenate(
            [jnp.where(lane_low, wide, 0.0).astype(bf16), jnp.where(lane_low, 0.0, wide).astype(bf16)], axis=0
        )

    def unstacked(wide):
        return jnp.concatenate([wide[:HEAD, :T], wide[HEAD:, T:]], axis=0).T

    quad_lane = lax.broadcasted_iota(jnp.int32, (T // 2, 256), 1) // HEAD

    def stacked_quad(quad):
        wide = quad.astype(f32)
        return jnp.concatenate([jnp.where(quad_lane == h, wide, 0.0).astype(bf16) for h in range(4)], axis=0)

    def unstacked_quad(wide):
        parts = []
        for b in range(2):
            span = slice(b * 128, (b + 1) * 128)
            t = wide[span, span].T
            parts.append(jnp.where(lane_low[: T // 2], t[: T // 2], t[T // 2 :]))
        return jnp.concatenate(parts, axis=1)

    def col_sum(x):
        return jnp.sum(x, axis=0, keepdims=True)

    def send_x(w, src):
        g = x_axis(w)

        def block(q):
            high, o = q // 2, lax.rem(q, 2)
            row = o * 128 + high * 64
            for own in (True, False):
                side = bits[g] if own else 1 - bits[g]
                from_block = high * 4 + (o * 2 + side if g == AXIS_Y else side * 2 + o)
                t = src[:, at(from_block, 128)].astype(f32).T.astype(bf16)
                for half in range(2):
                    rows = pl.ds(pl.multiple_of(half * 256 + row, 64), 64)
                    piece = t[half * 64 : (half + 1) * 64]
                    if own:
                        xcat[w, rows, 0:128] = piece
                    else:
                        xsend[w, rows, :] = piece

        loop(4, block, 2)
        copy_x(w).start()

    def copy_x(w):
        rows = pl.ds(0, 512) if x_axis(w) == AXIS_Y else at(m, 256)
        return remote(
            ("x", w), 0, 1, xsend.at[w, rows, :], xcat.at[w, rows, pl.ds(128, 128)], partners_of[x_axis(w)]
        )

    def copy_shared(w, side):
        held = xcat.at[w, at(side, 256), pl.ds(128, 128)]
        return remote(("shared", w), 0, 1, held, held, to_mp)

    def share_x(w):
        copy_x(w).wait_recv()
        copy_shared(w, m).start()

    def copy_y_half(u, half):
        rows, there = pl.ds(half * (T // 2), T // 2), pl.ds(T + half * (T // 2), T // 2)
        return remote(("half", half), u, 4, ycat.at[u, rows, :], ycat.at[u, there, :], partners_of[axis_of(FC_OUT)])

    def gathers(u):
        return [copy_y_half(u, half) for half in range(2)] if u < FC_IN else [copy_y(u)]

    def copy_y(u):
        to = partners_of[axis_of(u)]
        return remote("gather", u, KV, ycat.at[u, pl.ds(0, T), :], ycat.at[u, pl.ds(T, T), :], to)

    HALF = T // 2

    def exchange_part(k, j):
        return (at(j, HALF), pl.ds(0, D)) if k < 3 else (pl.ds(0, T), at(j, 256))

    def exchange_copy(k, j):
        rows, cols = exchange_part(k, j)
        return remote(
            ("ex", k), j, 4, r.ex_out.at[k % 2, rows, cols], r.ex_in.at[k % 2, rows, cols], to_mp
        )

    def exchange_half(k, half, term):
        for j in range(D // 256):
            cols = pl.ds(j * 256, 256)
            r.ex_out[k % 2, at(half, HALF), cols] = term(at(half, HALF), cols).astype(bf16)
        exchange_copy(k, half).start()

    def exchange_start(k, term):
        for j in range(D // 256):
            r.ex_out[k % 2, :, pl.ds(j * 256, 256)] = term(j).astype(bf16)
            exchange_copy(k, j).start()

    def exchange_wait(k):
        for j in range(4):
            exchange_copy(k, j).wait()

    def exchanged(k, rows):
        return r.ex_out[k % 2, rows, :].astype(f32) + r.ex_in[k % 2, rows, :].astype(f32)

    def kept(u):
        return r.fc_out_v.at[at(u % 8, 256), at(u // 8, W)]

    def core_out(u):
        return r.fc_in_v.at[at(u % 4, 256), at(u // 4, W)]

    def copy_core(u):
        return remote("core", u, KV, core_out(u), r.core_in.at[u], to_c)

    def copy_half(u):
        return remote("half", u, UNITS, r.half_out.at[u], r.half_in.at[u], partners_of[1 - axis_of(u)])

    def copy_last(u):
        return remote("last", u, UNITS, r.last_out.at[u], r.last_in.at[u], to_z2)

    def kvc_copy(v):
        return remote("kvc", v, 2, r.kvc_out.at[v], r.kvc_in.at[v], to_c)

    def kvy_copy(v):
        return remote("kvy", v, 2, r.kvy_out.at[v], r.kvy_in.at[v], to_y)

    arrived = set()

    def product(u):
        w = x_of(u)
        if w not in arrived:
            arrived.add(w)
            (copy_x(w) if x_axis(w) == AXIS_Y else copy_shared(w, 1 - m)).wait_recv()
        for copy in gathers(u):
            copy.wait_recv()
        for h in range(W // 256):
            cols = pl.ds(h * 256, 256)
            rhs = ycat[u, :, cols]
            core_out(u)[:, cols] = nn(xcat[w, at(1 - c, 256), :], rhs).astype(bf16)
            kept(u)[:, cols] = nn(xcat[w, at(c, 256), :], rhs).astype(bf16)
        copy_core(u).start()

    def local_sum(u, rows):
        if u < KV:
            return kept(u)[rows, :].astype(f32) + r.core_in[u, rows, :].astype(f32)
        v = u - KV
        wide = pl.ds(pl.multiple_of(y * 256 + rows.start, 64), rows.size)
        mine = r.memory_v[wide, pl.ds(v * W, W)].astype(f32) + r.kvc_in[v, wide, :].astype(f32)
        return mine + r.kvy_in[v, rows, :].astype(f32)

    def halve(u):
        if u < KV:
            copy_core(u).wait_recv()
        else:
            kvy_copy(u - KV).wait_recv()
        r.half_out[u] = local_sum(u, at(1 - bits[1 - axis_of(u)], 128)).astype(bf16)
        copy_half(u).start()

    def part_rows(u, high):
        return pl.ds(pl.multiple_of(bits[1 - axis_of(u)] * 128 + high * 64, 64), 64)

    def halve_last(u):
        copy_half(u).wait_recv()
        got = r.half_in[u, at(1 - zh, 64), :].astype(f32)
        r.last_out[u] = (local_sum(u, part_rows(u, 1 - zh)) + got).astype(bf16)
        copy_last(u).start()

    def out_copy(u):
        if u < FC_IN:
            to = r.g_fc_out.at[:, at(u, W)]
        elif u < CROSS_OUT:
            to = r.g_fc_in.at[:, at(u - FC_IN, W)]
        elif u < QKV:
            to = (r.g_cross_out, r.g_cross_q, r.g_self_out)[u - CROSS_OUT]
        elif u < KV:
            to = r.g_qkv.at[u - QKV]
        else:
            to = r.g_kv.at[u - KV]
        return local("unit", r.fin.at[u], to, u, UNITS)

    def total(u):
        copy_last(u).wait_recv()
        got = r.half_in[u, at(zh, 64), :].astype(f32) + r.last_in[u].astype(f32)
        r.fin[u] = local_sum(u, part_rows(u, zh)) + got
        out_copy(u).start()

    def project():
        load(r.tokens).wait()
        for part in range(3):
            load_qkv(part).wait()
            if part == 0:
                for src in first:
                    load(src).wait()

            def packed(j, part=part):
                cols = at(j, 256)
                x = nn(r.tokens_v[...], r.wqkv_v[part, :, cols])
                if part == 0:
                    x = x + r.self_qv_bias_v[0:1, cols]
                if part == 2:
                    x = x + r.self_qv_bias_v[1:2, cols]
                r.packed[part, :, cols] = x.astype(bf16)

            loop(HL // 256, packed, 2)

    key_row = lax.broadcasted_iota(jnp.int32, (T, 2 * T), 0)
    query_row = lax.rem(lax.broadcasted_iota(jnp.int32, (T, 2 * T), 1), T)

    def self_pair(p):
        cols = at(p, 128)
        q, k, v = (r.packed[i, :, cols] for i in range(3))
        s = nt(k, stacked(q)) * scale
        s = jnp.where((key_row <= query_row) & (key_row < r.dec_len_v[0]), s, -1e30)
        w = jnp.exp(s - jnp.max(s, axis=0, keepdims=True))
        probs = w / jnp.sum(w, axis=0, keepdims=True)
        r.self_probs[p] = probs
        mixed = nn(v.astype(f32).T.astype(bf16), probs.astype(bf16))
        ycat[SELF_OUT, 0:T, cols] = unstacked(mixed).astype(bf16)

    def self_attention():
        loop(PAIRS, self_pair, 4)

    def send_first():
        load(r.self_out).wait()
        pl.semaphore_wait(barrier, 5)
        for half in range(2):
            exchange_half(0, half, lambda rows, cols: nn(ycat[SELF_OUT, rows, :], r.self_out_v[:, cols]))
        copy_y(SELF_OUT).start()
        load(r.memory).wait()

    key, value, turned = r.key, r.value, r.turned
    odd = lax.broadcasted_iota(jnp.int32, (256, 256), 0)
    odd = jnp.where(odd < 128, 2 * odd, 2 * odd - 255)
    select = (lax.broadcasted_iota(jnp.int32, (256, 256), 1) == odd).astype(f32).astype(bf16)

    def part_weights(i):
        rows = at(i, CH)
        x = nn(select, r.cross_kv_v[rows].reshape(2 * CH, HL)).astype(bf16)
        r.wkv_v[0, rows, :] = x[:CH]
        r.wkv_v[1, rows, :] = x[CH:]

    def pair_rows(i):
        rows = at(i, CH)
        x = r.memory_v[rows, :]
        for j in range(HL // 256):
            cols = pl.ds(j * 256, 256)
            key[rows, cols] = nn(x, r.wkv_v[0, :, cols]).astype(bf16)
            val = (nn(x, r.wkv_v[1, :, cols]) + r.cross_qv_bias_v[1:2, cols]).astype(bf16)
            value[rows, cols] = val

    def turn(src):
        def step(i):
            rows = at(i, CH)
            for j in range(HL // 128):
                turned[pl.ds(j * 128, 128), rows] = src[rows, pl.ds(j * 128, 128)].astype(f32).T.astype(bf16)

        loop(ML // CH, step, 2)

    def memory_pair():
        load(r.cross_kv).wait()
        loop(D // CH, part_weights, 2)
        loop(ML // CH, pair_rows, 2)
        turn(value)

    def turn_memory(i):
        rows = at(i, CH)

        def block(b):
            t = r.memory_v[rows, at(b, 128)].astype(f32).T.astype(bf16)
            side, zlow, zhigh = lax.rem(b, 2), lax.rem(b // 2, 2), b // 4
            for half in range(2):
                to = half * 512 + side * 256 + zlow * 128 + zhigh * 64
                r.memory_t[pl.ds(pl.multiple_of(to, 64), 64), rows] = t[half * 64 : (half + 1) * 64]

        loop(D // 128, block, 4)

    def normalize(v, k):
        mean = jnp.mean(v, axis=-1, keepdims=True)
        centred = v - mean
        inv = lax.rsqrt(jnp.mean(centred * centred, axis=-1, keepdims=True) + epsilon)
        unit = centred * inv
        return unit * gain[k : k + 1, :] + shift[k : k + 1, :], unit, inv

    def norm_back(g, unit, inv, k):
        w = g * gain[k : k + 1, :]
        return inv * (w - jnp.mean(w, axis=-1, keepdims=True) - unit * jnp.mean(w * unit, axis=-1, keepdims=True))

    def norm_rows(k, half, base, unit_ref):
        exchange_copy(k, half).wait()
        for i in range(HALF // 16):
            rows = pl.ds(half * HALF + i * 16, 16)
            v = base[rows, :].astype(f32) + (exchanged(k, rows) + out_bias[k : k + 1, :])
            norm, unit, inv = normalize(v, k)
            r.norm[rows, :] = norm
            unit_ref[rows, :] = unit
            r.inv[k, rows, :] = jnp.broadcast_to(inv, (16, 128))
            low[rows, :] = norm.astype(bf16)

    def first_norm(half):
        norm_rows(0, half, r.tokens_v, r.unit0)

    probs_ref = r.probs
    dp_ref = r.dp
    low_probs = r.low_probs
    mem_row = lax.broadcasted_iota(jnp.int32, (CH, 2 * T), 0)
    chunks = ML // CH

    def fold(x, op):
        total = x[0:8]
        for i in range(1, x.shape[0] // 8):
            total = op(total, x[8 * i : 8 * i + 8])
        return total

    def cross_quad(half, g):
        cols, rows_q, index = pl.ds(g * 256, 256), pl.ds(half * HALF, HALF), half * (HL // 256) + g
        q = stacked_quad(r.query[rows_q, cols])
        top = jnp.full((8, 2 * T), -1e30, f32)
        for i in range(chunks):
            rows = at(i, CH)
            s = nt(key[rows, cols], q) * (scale * LOG2E)
            s = jnp.where(mem_row < r.mem_len_v[0] - i * CH, s, -1e30)
            probs_ref[index, rows, :] = s
            top = jnp.maximum(top, fold(s, jnp.maximum))
        top = jnp.max(top, axis=0, keepdims=True)
        total = jnp.zeros((8, 2 * T), f32)
        for i in range(chunks):
            rows = at(i, CH)
            w = jnp.exp2(probs_ref[index, rows, :] - top)
            probs_ref[index, rows, :] = w
            low_probs[g, rows, :] = w.astype(bf16)
            total = total + fold(w, jnp.add)
        part = 1.0 / jnp.sum(total, axis=0, keepdims=True)
        r.part[index] = jnp.broadcast_to(part, (8, 2 * T))
        mixed = nn(turned[cols, :], low_probs[g]) * part
        ycat[CROSS_OUT, rows_q, cols] = unstacked_quad(mixed).astype(bf16)

    def cross_attention(half):
        if half == 0:
            load(r.cross_q).wait()
        rows = pl.ds(half * HALF, HALF)
        for j in range(HL // 256):
            cols = pl.ds(j * 256, 256)
            x = nn(low[rows, :], r.cross_q_v[:, cols]) + r.cross_qv_bias_v[0:1, cols]
            r.query[rows, cols] = x.astype(bf16)
        for g in range(HL // 256):
            cross_quad(half, g)

    def send_second(half):
        if half == 0:
            load(r.cross_out).wait()
        exchange_half(1, half, lambda rows, cols: nn(ycat[CROSS_OUT, rows, :], r.cross_out_v[:, cols]))
        if half == 1:
            copy_y(CROSS_OUT).start()

    def second_norm(half):
        norm_rows(1, half, r.norm, r.unit1)

    def hidden_units(half):
        if half == 0:
            load(r.fc_in).wait()
        rows = pl.ds(half * HALF, HALF)

        def unit(b):
            for part in range(2):
                j = 2 * b + part
                cols = at(j, 256)
                h = nn(low[rows, :], r.fc_in_v[:, cols]) + r.fc_in_bias_v[:, cols]
                phi = 0.5 * (1.0 + lax.erf(h * 0.7071067811865476))
                slope = phi + h * jnp.exp(-0.5 * h * h) * 0.3989422804014327
                dp_ref[1, pl.ds(pl.multiple_of(j * T + half * HALF, HALF), HALF), :] = slope
                ycat[FC_OUT + b, rows, pl.ds(part * 256, 256)] = (h * phi).astype(bf16)
            copy_y_half(FC_OUT + b, half).start()

        loop(FL // W, unit)

    def ffn_term(rows, cols):
        total = nn(ycat[FC_OUT, rows, :], r.fc_out_v[pl.ds(0, W), cols])
        for b in range(1, FL // W):
            total = total + nn(ycat[FC_OUT + b, rows, :], r.fc_out_v[pl.ds(b * W, W), cols])
        return total

    def send_third(half):
        if half == 0:
            load(r.fc_out).wait()
        exchange_half(2, half, ffn_term)

    row16 = lax.broadcasted_iota(jnp.int32, (16, D), 0)
    zero8 = jnp.zeros((8, D), f32)

    def sums_of(body, k):
        def step(i, carry):
            g, unit, rounded = body(i)
            return (
                carry[0] + fold(rounded, jnp.add),
                carry[1] + fold(g * unit, jnp.add),
                carry[2] + fold(g, jnp.add),
            )

        carry = (zero8, zero8, zero8)
        for i in range(T // 16):
            carry = step(i, carry)
        bias, gains, shifts = carry
        sm[k : k + 1, :] = col_sum(bias)
        sm[3 + k : 4 + k, :] = col_sum(gains)
        sm[6 + k : 7 + k, :] = col_sum(shifts)

    def output_rows(i):
        rows = at(i, 16)
        v = r.norm[rows, :] + (exchanged(2, rows) + out_bias[2:3, :])
        norm, unit, inv = normalize(v, 2)
        r.layer_v[rows, :] = norm.astype(bf16)
        g = jnp.where(row16 + i * 16 < r.dec_len_v[0], r.cotangent_v[rows, :].astype(f32), 0.0)
        grad = norm_back(g, unit, inv, 2)
        r.grad[rows, :] = grad
        rounded = grad.astype(bf16)
        low[rows, :] = rounded
        return g, unit, rounded.astype(f32)

    def layer_copy():
        return local("layer", r.layer_v, r.layer_out)

    def output_norm():
        load(r.cotangent).wait()
        for half in range(2):
            exchange_copy(2, half).wait()
        sums_of(output_rows, 2)
        layer_copy().start()

    def hidden_grad(j):
        cols = at(j, 256)
        g = nt(low[...], r.fc_out_v[at(j, 256), :]) * dp_ref[1, at(j, T), :]
        rounded = g.astype(bf16)
        ycat[FC_IN + j // 2, 0:T, at(j % 2, 256)] = rounded
        sm[pl.ds(11 + j // 4, 1), at(j % 4, 256)] = col_sum(rounded.astype(f32))

    def hidden_grads():
        for b in range(FL // W):
            hidden_grad(2 * b)
            hidden_grad(2 * b + 1)
            copy_y(FC_IN + b).start()

    def hidden_term(j):
        rows = at(j, 256)
        total = nt(ycat[FC_IN, 0:T, :], r.fc_in_v[rows, pl.ds(0, W)])
        for b in range(1, FL // W):
            total = total + nt(ycat[FC_IN + b, 0:T, :], r.fc_in_v[rows, pl.ds(b * W, W)])
        return total

    def send_fourth():
        exchange_start(3, hidden_term)

    def grad_rows(k, e, unit_ref):
        def body(i):
            rows = at(i, 16)
            g = r.grad[rows, :] + exchanged(e, rows)
            unit = unit_ref[rows, :]
            grad = norm_back(g, unit, r.inv[k, rows, 0:1], k)
            r.grad[rows, :] = grad
            rounded = grad.astype(bf16)
            low[rows, :] = rounded
            return g, unit, rounded.astype(f32)

        exchange_wait(e)
        sums_of(body, k)

    mixed_grad = r.mixed_grad

    def second_back():
        grad_rows(1, 3, r.unit1)

    def mixed_from(weights):
        for j in range(HL // 256):
            mixed_grad[:, at(j, 256)] = nt(low[...], weights[at(j, 256), :]).astype(bf16)

    def cross_mixed_grad():
        mixed_from(r.cross_out_v)

    def cross_back(g):
        cols = pl.ds(g * 256, 256)
        halves = [pl.ds(half * HALF, HALF) for half in range(2)]
        index = [half * (HL // 256) + g for half in range(2)]
        gs = [stacked_quad(mixed_grad[rows, cols]) for rows in halves]
        part = [r.part[i, 0:1, :] for i in index]
        total = [jnp.zeros((8, 2 * T), f32)] * 2
        both = jnp.concatenate(gs, axis=0)
        for i in range(chunks):
            rows = at(i, CH)
            v = value[rows, cols]
            lows = []
            for half in range(2):
                probs = probs_ref[index[half], rows, :] * part[half]
                dprobs = nt(v, gs[half])
                dp_ref[half, rows, :] = dprobs
                probs_ref[index[half], rows, :] = probs
                total[half] = total[half] + fold(probs * dprobs, jnp.add)
                lows.append(probs.astype(bf16))
            value[rows, cols] = nn(jnp.concatenate(lows, axis=1), both).astype(bf16)
        total = [jnp.sum(x, axis=0, keepdims=True) for x in total]
        both = jnp.concatenate([stacked_quad(r.query[rows, cols]) for rows in halves], axis=0)
        for i in range(chunks):
            rows = at(i, CH)
            lows = []
            for half in range(2):
                ds = (probs_ref[index[half], rows, :] * (dp_ref[half, rows, :] - total[half])).astype(bf16)
                low_probs[half, rows, :] = ds
                lows.append(ds)
            key[rows, cols] = (nn(jnp.concatenate(lows, axis=1), both) * scale).astype(bf16)
        for half in range(2):
            dq = nn(turned[cols, :], low_probs[half])
            ycat[CROSS_Q, halves[half], cols] = (unstacked_quad(dq) * scale).astype(bf16)

    def send_fifth():
        exchange_start(4, lambda j: nt(ycat[CROSS_Q, 0:T, :], r.cross_q_v[at(j, 256), :]))
        copy_y(CROSS_Q).start()
        sm[10:11, 0:HL] = col_sum(ycat[CROSS_Q, 0:T, :].astype(f32))
        sm[10:11, HL : 2 * HL] = col_sum(value[...].astype(f32))

    def gm_copy(i):
        return remote("gm", i, 4, r.gm_out.at[i], r.gm_in.at[i], to_mp)

    def memory_term(i):
        for half, to in (((1 - m) * 4 + i, r.gm_out), (m * 4 + i, r.gm_own)):
            rows = at(half, CH)
            for j in range(D // 256):
                cols = pl.ds(j * 256, 256)
                x = nt(key[rows, :], r.wkv_v[0, cols, :]) + nt(value[rows, :], r.wkv_v[1, cols, :])
                to[i, :, cols] = x.astype(bf16)
        gm_copy(i).start()

    def gm_store(i):
        return local("gm_store", r.gm_own.at[i], r.grad_memory.at[at(i, CH), :], i, 4)

    def memory_sum(i):
        gm_copy(i).wait()
        r.gm_own[i] = (r.gm_own[i].astype(f32) + r.gm_in[i].astype(f32)).astype(bf16)
        gm_store(i).start()

    def pair_product(v):
        pair = key if v == 0 else value
        for h in range(2):
            cols = pl.ds(h * 256, 256)

            def step(b, cols=cols, h=h):
                rows = at(b, 128)
                other, own = r.memory_t[at((1 - c) * 4 + b, 128), :], r.memory_t[at(c * 4 + b, 128), :]
                r.kvc_out[v, rows, cols] = nn(other, pair[:, cols]).astype(bf16)
                r.memory_v[rows, pl.ds(v * W + h * 256, 256)] = nn(own, pair[:, cols]).astype(bf16)

            loop(4, step)
        kvc_copy(v).start()

    def pair_halve(v):
        kvc_copy(v).wait_recv()
        rows = at(1 - y, 256)
        mine = r.memory_v[rows, pl.ds(v * W, W)].astype(f32)
        r.kvy_out[v] = (mine + r.kvc_in[v, rows, :].astype(f32)).astype(bf16)
        kvy_copy(v).start()

    def first_back():
        grad_rows(0, 4, r.unit0)

    def self_back(p):
        cols = at(p, 128)
        q, k, v = (r.packed[i, :, cols] for i in range(3))
        probs = r.self_probs[p]
        g = stacked(mixed_grad[:, cols])
        dprobs = nt(v, g)
        ycat[QKV + 2, 0:T, cols] = nn(probs.astype(bf16), g).astype(bf16)
        ds = (probs * (dprobs - jnp.sum(probs * dprobs, axis=0, keepdims=True))).astype(bf16)
        ycat[QKV + 1, 0:T, cols] = (nn(ds, stacked(q)) * scale).astype(bf16)
        dq = nn(k.astype(f32).T.astype(bf16), ds)
        ycat[QKV, 0:T, cols] = (unstacked(dq) * scale).astype(bf16)

    def self_grads():
        mixed_from(r.self_out_v)
        loop(PAIRS, self_back, 4)
        for b in range(3):
            copy_y(QKV + b).start()
        sm[9:10, 0:HL] = col_sum(ycat[QKV, 0:T, :].astype(f32))
        sm[9:10, HL : 2 * HL] = col_sum(ycat[QKV + 2, 0:T, :].astype(f32))
        sm[13:16, :] = jnp.zeros((3, D), f32)

    def packed_term(j):
        rows = at(j, 256)
        total = nt(ycat[QKV, 0:T, :], r.wqkv_v[0, rows, :])
        for b in range(1, 3):
            total = total + nt(ycat[QKV + b, 0:T, :], r.wqkv_v[b, rows, :])
        return total

    def send_sixth():
        exchange_start(5, packed_term)

    def token_copy():
        return local("tokens_g", r.tokens_g, r.grad_tokens)

    def token_grads():
        def body(i):
            rows = at(i, 16)
            r.tokens_g[rows, :] = (r.grad[rows, :] + exchanged(5, rows)).astype(bf16)

        exchange_wait(5)
        loop(T // 16, body, 2)
        token_copy().start()

    doubling = (to_c, to_y, to_z1, to_z2)

    def small_copy(k):
        return remote("small", k, 4, r.sm_out.at[k], r.sm_in.at[k], doubling[k])

    def sums_copy():
        return local("sums", sm, r.sums)

    def small_step(k):
        if k > 0:
            small_copy(k - 1).wait()
            sm[...] = r.sm_out[k - 1].astype(f32) + r.sm_in[k - 1].astype(f32)
        if k < 4:
            r.sm_out[k] = sm[...].astype(bf16)
            small_copy(k).start()
        else:
            sums_copy().start()

    def each(step, *indices):
        for i in indices:
            step(i)

    project()
    self_attention()
    send_first()
    memory_pair()
    first_norm(0)
    cross_attention(0)
    send_second(0)
    first_norm(1)
    cross_attention(1)
    send_second(1)
    send_x(X_FIRST, low)
    each(turn_memory, 6)
    turn(key)
    second_norm(0)
    hidden_units(0)
    send_third(0)
    second_norm(1)
    hidden_units(1)
    send_third(1)
    send_x(X_SECOND, low)
    output_norm()
    hidden_grads()
    send_fourth()
    send_x(X_FFN, low)
    each(product, 4)
    send_x(X_TOKENS, r.tokens_v)
    each(halve, 4)
    each(product, 5)
    share_x(X_FFN)
    second_back()
    each(halve, 5)
    cross_mixed_grad()
    each(product, 6)
    send_x(X_CROSS, low)
    each(product, 0)
    each(halve_last, 4)
    each(cross_back, 0)
    each(halve, 6, 0)
    each(cross_back, 1)
    each(halve_last, 5)
    send_fifth()
    share_x(X_CROSS)
    each(product, 7, 3)
    each(turn_memory, 5, 0)
    each(halve, 7)
    each(product, 1)
    each(turn_memory, 3)
    each(halve_last, 0)
    each(turn_memory, 7)
    each(product, 2)
    each(turn_memory, 4)
    each(halve_last, 6)
    each(halve, 3)
    each(product, 9)
    first_back()
    self_grads()
    each(halve, 2)
    send_x(X_SELF, low)
    each(halve, 1)
    each(turn_memory, 2)
    each(memory_term, 3)
    each(halve, 9)
    each(turn_memory, 1)
    each(halve_last, 7)
    each(product, 8)
    each(halve_last, 3)
    each(product, 11)
    each(pair_product, 0)
    each(product, 12)
    share_x(X_SELF)
    each(total, 6)
    each(small_step, 0)
    each(halve, 11)
    each(product, 13)
    each(halve_last, 9)
    each(memory_term, 1)
    each(pair_halve, 0)
    each(halve, 12)
    each(product, 10)
    each(memory_sum, 3)
    each(memory_term, 0)
    each(halve_last, 11)
    each(halve, 8, 13)
    each(small_step, 1)
    each(pair_product, 1)
    each(total, 9)
    each(memory_term, 2)
    each(halve_last, 1, 12)
    send_sixth()
    each(memory_sum, 1)
    each(total, 7, 4, 3)
    each(pair_halve, 1)
    each(halve, 10, 14)
    each(halve_last, 8, 2, 13)
    each(memory_sum, 2)
    each(small_step, 2)
    each(halve, 15)
    each(memory_sum, 0)
    each(total, 5)
    each(halve_last, 10, 14)
    each(total, 12)
    each(small_step, 3)
    each(total, 10, 2)
    each(halve_last, 15)
    token_grads()
    each(total, 8, 1, 13)
    each(small_step, 4)
    each(total, 0, 11, 14, 15)
    for w in range(6):
        copy_x(w).wait_send()
        if x_axis(w) == AXIS_Z:
            copy_shared(w, m).wait_send()
    for u in range(UNITS):
        if u < KV:
            for copy in gathers(u):
                copy.wait_send()
            copy_core(u).wait_send()
        copy_half(u).wait_send()
        copy_last(u).wait_send()
        out_copy(u).wait()
    for v in range(2):
        kvc_copy(v).wait_send()
        kvy_copy(v).wait_send()
    for i in range(4):
        gm_store(i).wait()
    layer_copy().wait()
    token_copy().wait()
    sums_copy().wait()
    refs_at.update(remote=sum(n for _, n in given.values()), local=sum(n for _, n in local_given.values()))


REMOTE_SEMS = 160
LOCAL_SEMS = 64


def layer(tokens, memory, mem_len, dec_len, cotangent, wqkv, self_qv_bias, self_out, cross_q, cross_kv, cross_qv_bias, cross_out, fc_in, fc_in_bias, fc_out, out_bias, norm_gain, norm_bias):
    T, D = tokens.shape
    ML = memory.shape[0]
    HL = self_out.shape[0]
    FL = fc_out.shape[0]
    R = D // GROUP
    W = 512
    PAIRS = HL // 128
    anywhere = pl.BlockSpec(memory_space=pl.ANY)
    big = dict(tokens=tokens, memory=memory, cotangent=cotangent, wqkv=wqkv, self_out=self_out, cross_q=cross_q, cross_kv=cross_kv,
               cross_out=cross_out, fc_in=fc_in, fc_out=fc_out)
    small = dict(self_qv_bias=self_qv_bias, cross_qv_bias=cross_qv_bias, fc_in_bias=fc_in_bias, out_bias=out_bias,
                 norm_gain=norm_gain, norm_bias=norm_bias)
    scalars = dict(mem_len=mem_len, dec_len=dec_len)
    outs = dict(
        layer_out=((T, D), bf16),
        grad_tokens=((T, D), bf16),
        grad_memory=((ML // 2, D), bf16),
        g_qkv=((3, R, HL), f32),
        g_self_out=((R, HL), f32),
        g_cross_q=((R, HL), f32),
        g_kv=((2, R, HL), f32),
        g_cross_out=((R, HL), f32),
        g_fc_in=((R, FL), f32),
        g_fc_out=((R, FL), f32),
        sums=((16, D), f32),
    )
    scratch = {name + "_v": (x.shape, x.dtype) for name, x in (big | small).items()}
    scratch |= dict(
        wkv_v=((2, D, HL), bf16),
        packed=((3, T, HL), bf16),
        self_probs=((PAIRS, T, 2 * T), f32),
        low=((T, D), bf16),
        ycat=((KV, 2 * T, W), bf16),
        xcat=((6, 512, 256), bf16),
        xsend=((6, 512, 128), bf16),
        ex_out=((2, T, D), bf16),
        ex_in=((2, T, D), bf16),
        norm=((T, D), f32),
        unit0=((T, D), f32),
        unit1=((T, D), f32),
        inv=((2, T, 128), f32),
        grad=((T, D), f32),
        key=((ML, HL), bf16),
        value=((ML, HL), bf16),
        turned=((HL, ML), bf16),
        query=((T, HL), bf16),
        mixed_grad=((T, HL), bf16),
        probs=((PAIRS, ML, 2 * T), f32),
        part=((PAIRS, 8, 2 * T), f32),
        low_probs=((2, ML, 2 * T), bf16),
        dp=((2, ML, 2 * T), f32),
        memory_t=((D, ML), bf16),
        layer_v=((T, D), bf16),
        tokens_g=((T, D), bf16),
        gm_out=((4, 128, D), bf16),
        gm_own=((4, 128, D), bf16),
        gm_in=((4, 128, D), bf16),
        core_in=((KV, 256, W), bf16),
        kvc_out=((2, 512, W), bf16),
        kvc_in=((2, 512, W), bf16),
        kvy_out=((2, 256, W), bf16),
        kvy_in=((2, 256, W), bf16),
        half_out=((UNITS, 128, W), bf16),
        half_in=((UNITS, 128, W), bf16),
        last_out=((UNITS, 64, W), bf16),
        last_in=((UNITS, 64, W), bf16),
        fin=((UNITS, 64, W), f32),
        sm=((16, D), f32),
        sm_out=((4, 16, D), bf16),
        sm_in=((4, 16, D), bf16),
    )
    sems = dict(send_sem=REMOTE_SEMS, recv_sem=REMOTE_SEMS, local_sem=LOCAL_SEMS)
    lengths = {name + "_v": pltpu.SMEM((1,), jnp.int32) for name in scalars}
    names = [*big, *small, *scalars, *outs, *scratch, *lengths, *sems]
    got = {}
    out = pl.pallas_call(
        functools.partial(kernel, names, got),
        out_shape=[jax.ShapeDtypeStruct(s, t) for s, t in outs.values()],
        in_specs=[anywhere] * (len(big) + len(small) + len(scalars)),
        out_specs=[anywhere] * len(outs),
        scratch_shapes=[pltpu.VMEM(s, t) for s, t in scratch.values()]
        + [*lengths.values()]
        + [pltpu.SemaphoreType.DMA((count,)) for count in sems.values()],
        compiler_params=pltpu.CompilerParams(
            collective_id=0, has_side_effects=True, vmem_limit_bytes=63 * 2**20
        ),
        name="layer",
    )(*big.values(), *small.values(), *scalars.values())
    assert got["remote"] <= REMOTE_SEMS and got["local"] <= LOCAL_SEMS, got
    return types.SimpleNamespace(**dict(zip(outs, out)))


def finish_kernel(count, small, *refs):
    ins, outs, scratch = refs[: count + 2], refs[count + 2 : 2 * count + 3 + small], refs[2 * count + 3 + small :]
    held, turned, made, (in_sem, out_sem) = scratch[: count + 2], scratch[count + 2], scratch[count + 3 : -2], scratch[-2:]
    loads = [pltpu.make_async_copy(a, b, in_sem.at[i]) for i, (a, b) in enumerate(zip(ins, held))]
    stores = [
        pltpu.make_async_copy(a, b, out_sem.at[i]) for i, (a, b) in enumerate(zip((*held[:count], turned, *made), outs))
    ]
    for load in loads[::-1]:
        load.start()
    loads[count + 1].wait()
    sums = held[count + 1]
    self_bias, cross_bias, hidden_bias, out_bias, gains, shifts = made
    width = self_bias.shape[1]
    for row, to in ((9, self_bias), (10, cross_bias)):
        for part in range(2):
            to[part : part + 1, :] = sums[row : row + 1, part * width : (part + 1) * width]
    features = sums.shape[1]
    for part in range(hidden_bias.shape[1] // features):
        hidden_bias[:, part * features : (part + 1) * features] = sums[11 + part : 12 + part, :]
    for first, to in ((0, out_bias), (3, gains), (6, shifts)):
        to[...] = sums[first : first + 3, :]
    for i in range(small):
        stores[count + 1 + i].start()
    loads[count].wait()
    for part in range(2):
        turned[:, part, :] = held[count][part]
    stores[count].start()
    for i in range(count):
        loads[i].wait()
        stores[i].start()
    for store in stores:
        store.wait()


def finish(whole, kv, sums):
    R, HL = kv.shape[1:]
    D = sums.shape[1]
    anywhere = pl.BlockSpec(memory_space=pl.ANY)
    small = [(2, HL), (2, HL), (1, 4 * HL), (3, D), (3, D), (3, D)]
    return pl.pallas_call(
        functools.partial(finish_kernel, len(whole), len(small)),
        out_shape=[jax.ShapeDtypeStruct(x.shape, x.dtype) for x in whole]
        + [jax.ShapeDtypeStruct((R, 2, HL), f32)]
        + [jax.ShapeDtypeStruct(shape, f32) for shape in small],
        in_specs=[anywhere] * (len(whole) + 2),
        out_specs=[anywhere] * (len(whole) + 1 + len(small)),
        scratch_shapes=[pltpu.VMEM(x.shape, x.dtype) for x in (*whole, kv, sums)]
        + [pltpu.VMEM(shape, f32) for shape in [(R, 2, HL), *small]]
        + [pltpu.SemaphoreType.DMA((len(whole) + 2,)), pltpu.SemaphoreType.DMA((len(whole) + 1 + len(small),))],
        compiler_params=pltpu.CompilerParams(vmem_limit_bytes=63 * 2**20),
        name="finish",
    )(*whole, kv, sums)


def per_device(tokens, memory, mem_len, dec_len, cotangent, self_qkv, self_qv_bias, self_out, cross_q, cross_kv, cross_qv_bias, cross_out, fc_in, fc_in_bias, fc_out, out_bias, norm_gain, norm_bias):
    D = tokens.shape[1]
    devices = lax.axis_size("dp")
    outer = devices // GROUP

    def regroup(x, axis, there):
        if outer == 1:
            return x
        sizes = (outer, GROUP) if there else (GROUP, outer)
        shape = x.shape
        x = x.reshape(shape[:axis] + sizes + (D // devices,) + shape[axis + 1 :])
        return jnp.swapaxes(x, axis, axis + 1).reshape(shape)

    tokens, memory, cotangent, self_out, cross_out, fc_out, out_bias, norm_gain, norm_bias = (
        regroup(x, 1, True)
        for x in (tokens, memory, cotangent, self_out, cross_out, fc_out, out_bias, norm_gain, norm_bias)
    )
    self_qkv, cross_q, cross_kv, fc_in = (regroup(x, 0, True) for x in (self_qkv, cross_q, cross_kv, fc_in))
    got = layer(
        tokens, memory, mem_len, dec_len, cotangent, self_qkv.transpose(1, 0, 2), self_qv_bias, self_out, cross_q,
        cross_kv, cross_qv_bias, cross_out, fc_in, fc_in_bias.reshape(1, -1), fc_out, out_bias,
        norm_gain, norm_bias,
    )
    groups = [[o * GROUP + i for o in range(outer)] for i in range(GROUP)]

    def spread(x, axis):
        if outer == 1:
            return x
        return lax.psum_scatter(x, "dp", scatter_dimension=axis, axis_index_groups=groups, tiled=True)

    sums = got.sums
    if outer > 1:
        sums = lax.psum(sums, "dp", axis_index_groups=groups)
    (
        layer_out, grad_tokens, grad_memory, qkv, self_out, cross_q, cross_out, fc_in, fc_out, kv,
        self_bias, cross_bias, hidden_bias, out_bias, gains, shifts,
    ) = finish(
        (
            got.layer_out, got.grad_tokens, got.grad_memory, got.g_qkv, got.g_self_out, got.g_cross_q, got.g_cross_out,
            got.g_fc_in, got.g_fc_out,
        ),
        got.g_kv,
        sums,
    )
    return (
        regroup(layer_out, 1, False),
        regroup(grad_tokens, 1, False),
        regroup(grad_memory, 1, False),
        spread(qkv, 1).transpose(1, 0, 2),
        self_bias,
        spread(self_out, 0).T,
        spread(cross_q, 0),
        spread(kv, 0),
        cross_bias,
        spread(cross_out, 0).T,
        spread(fc_in, 0),
        hidden_bias.reshape(-1),
        spread(fc_out, 0).T,
        regroup(out_bias, 1, False),
        regroup(gains, 1, False),
        regroup(shifts, 1, False),
    )


def solution(mesh):
    placed = (
        P("dp", None),
        P("dp", None),
        P("dp"),
        P("dp"),
        P("dp", None),
        P(None, None, "mp"),
        P(None, "mp"),
        P("mp", None),
        P(None, "mp"),
        P(None, None, "mp"),
        P(None, "mp"),
        P("mp", None),
        P(None, "mp"),
        P("mp"),
        P("mp", None),
        P(),
        P(),
        P(),
    )
    return jax.shard_map(
        per_device,
        mesh=mesh,
        in_specs=placed,
        out_specs=(
            P("dp", None),
            P("dp", None),
            P(("dp", "mp"), None),
            P("dp", None, "mp"),
            P(None, "mp"),
            P("mp", "dp"),
            P("dp", "mp"),
            P("dp", None, "mp"),
            P(None, "mp"),
            P("mp", "dp"),
            P("dp", "mp"),
            P("mp"),
            P("mp", "dp"),
            P(),
            P(),
            P(),
        ),
        check_vma=False,
    )
```

```python
import functools
import types

import jax
import jax.numpy as jnp
from jax import lax
from jax.experimental import pallas as pl
from jax.experimental.pallas import tpu as pltpu
from jax.sharding import PartitionSpec as P

HEAD = 64
LOG2E = 1.4426950408889634
GROUP = 16
epsilon = 1e-05
MESH = pl.DeviceIdType.MESH
f32, bf16 = jnp.float32, jnp.bfloat16

FC_OUT, FC_IN, CROSS_OUT, CROSS_Q, SELF_OUT, QKV, KV = 0, 4, 8, 9, 10, 11, 14
UNITS = 16
X_TOKENS, X_FIRST, X_SECOND, X_FFN, X_CROSS, X_SELF = range(6)


AXIS_Y, AXIS_Z = 0, 1


def axis_of(unit):
    return AXIS_Z if unit < FC_IN or unit in (CROSS_OUT, SELF_OUT) else AXIS_Y


def x_axis(x):
    return AXIS_Z if x in (X_FFN, X_CROSS, X_SELF) else AXIS_Y


def x_of(unit):
    return ((X_FFN,) * 4 + (X_SECOND,) * 4 + (X_CROSS, X_FIRST, X_SELF) + (X_TOKENS,) * 3)[unit]


def nn(a, b):
    return lax.dot_general(a, b, (((1,), (0,)), ((), ())), preferred_element_type=f32)


def nt(a, b):
    return lax.dot_general(a, b, (((1,), (1,)), ((), ())), preferred_element_type=f32)


def loop(count, body, unroll=1):
    def step(i, carry):
        for j in range(unroll):
            body(i * unroll + j)
        return carry

    if unroll == count:
        step(0, 0)
    else:
        lax.fori_loop(0, count // unroll, step, 0)


def at(index, size):
    return pl.ds(index * size if isinstance(index, int) else pl.multiple_of(index * size, size), size)


def kernel(names, refs_at, *refs):
    r = types.SimpleNamespace(**dict(zip(names, refs)))
    T, D = r.tokens.shape
    ML = r.memory.shape[0]
    HL = r.self_out.shape[0]
    FL = r.fc_out.shape[0]
    W = 512
    PAIRS = HL // 128
    CH = 128
    scale = HEAD**-0.5

    d, m = lax.axis_index("dp"), lax.axis_index("mp")
    c, y = lax.rem(d, 2), lax.rem(d // 2, 2)
    zl, zh = lax.rem(d // 4, 2), lax.rem(d // 8, 2)
    to_mp = (d, 1 - m)
    to_c = (d + 1 - 2 * c, m)
    to_y = (d + 2 - 4 * y, m)
    to_z1 = (d + 4 - 8 * zl, m)
    to_z2 = (d + 8 - 16 * zh, m)

    bits, partners_of = (y, zl), (to_y, to_z1)

    barrier = pltpu.get_barrier_semaphore()
    for partner in (to_mp, to_c, to_y, to_z1, to_z2):
        pl.semaphore_signal(barrier, inc=1, device_id=partner, device_id_type=MESH)

    given = {}
    local_given = {}

    def slot(key, count=1):
        if key not in given:
            given[key] = sum(n for _, n in given.values()), count
        return given[key][0]

    def remote(key, index, count, src, dst, partner):
        base = slot(key, count) + index
        return pltpu.make_async_remote_copy(
            src_ref=src,
            dst_ref=dst,
            send_sem=r.send_sem.at[base],
            recv_sem=r.recv_sem.at[base],
            device_id=partner,
            device_id_type=MESH,
        )

    def local(key, src, dst, index=0, count=1):
        if key not in local_given:
            local_given[key] = sum(n for _, n in local_given.values()), count
        return pltpu.make_async_copy(src, dst, r.local_sem.at[local_given[key][0] + index])

    def load(src):
        name = next(k for k, v in vars(r).items() if v is src)
        return local(name, src, getattr(r, name + "_v"))

    def load_qkv(part):
        return local("qkv", r.wqkv.at[part], r.wqkv_v.at[part], part, 3)

    first = (r.dec_len, r.mem_len, r.self_qv_bias, r.cross_qv_bias, r.fc_in_bias, r.out_bias, r.norm_gain, r.norm_bias)
    load(r.tokens).start()
    load_qkv(0).start()
    for src in first:
        load(src).start()
    load_qkv(1).start()
    load_qkv(2).start()
    for src in (r.self_out, r.memory, r.cross_kv, r.cross_q, r.cross_out, r.fc_in, r.fc_out, r.cotangent):
        load(src).start()

    gain, shift, out_bias = r.norm_gain_v, r.norm_bias_v, r.out_bias_v
    sm = r.sm
    ycat, xcat, xsend = r.ycat, r.xcat, r.xsend
    low = r.low
    lane_low = lax.broadcasted_iota(jnp.int32, (T, 128), 1) < HEAD

    def stacked(pair):
        wide = pair.astype(f32)
        return jnp.concatenate(
            [jnp.where(lane_low, wide, 0.0).astype(bf16), jnp.where(lane_low, 0.0, wide).astype(bf16)], axis=0
        )

    def unstacked(wide):
        return jnp.concatenate([wide[:HEAD, :T], wide[HEAD:, T:]], axis=0).T

    quad_lane = lax.broadcasted_iota(jnp.int32, (T // 2, 256), 1) // HEAD

    def stacked_quad(quad):
        wide = quad.astype(f32)
        return jnp.concatenate([jnp.where(quad_lane == h, wide, 0.0).astype(bf16) for h in range(4)], axis=0)

    def unstacked_quad(wide):
        parts = []
        for b in range(2):
            span = slice(b * 128, (b + 1) * 128)
            t = wide[span, span].T
            parts.append(jnp.where(lane_low[: T // 2], t[: T // 2], t[T // 2 :]))
        return jnp.concatenate(parts, axis=1)

    def col_sum(x):
        return jnp.sum(x, axis=0, keepdims=True)

    def send_x(w, src):
        g = x_axis(w)

        def block(q):
            high, o = q // 2, lax.rem(q, 2)
            row = o * 128 + high * 64
            for own in (True, False):
                side = bits[g] if own else 1 - bits[g]
                from_block = high * 4 + (o * 2 + side if g == AXIS_Y else side * 2 + o)
                t = src[:, at(from_block, 128)].astype(f32).T.astype(bf16)
                for half in range(2):
                    rows = pl.ds(pl.multiple_of(half * 256 + row, 64), 64)
                    piece = t[half * 64 : (half + 1) * 64]
                    if own:
                        xcat[w, rows, 0:128] = piece
                    else:
                        xsend[w, rows, :] = piece

        loop(4, block, 2)
        copy_x(w).start()

    def copy_x(w):
        rows = pl.ds(0, 512) if x_axis(w) == AXIS_Y else at(m, 256)
        return remote(
            ("x", w), 0, 1, xsend.at[w, rows, :], xcat.at[w, rows, pl.ds(128, 128)], partners_of[x_axis(w)]
        )

    def copy_shared(w, side):
        held = xcat.at[w, at(side, 256), pl.ds(128, 128)]
        return remote(("shared", w), 0, 1, held, held, to_mp)

    def share_x(w):
        copy_x(w).wait_recv()
        copy_shared(w, m).start()

    def copy_y_half(u, half):
        rows, there = pl.ds(half * (T // 2), T // 2), pl.ds(T + half * (T // 2), T // 2)
        return remote(("half", half), u, 4, ycat.at[u, rows, :], ycat.at[u, there, :], partners_of[axis_of(FC_OUT)])

    def gathers(u):
        return [copy_y_half(u, half) for half in range(2)] if u < FC_IN else [copy_y(u)]

    def copy_y(u):
        to = partners_of[axis_of(u)]
        return remote("gather", u, KV, ycat.at[u, pl.ds(0, T), :], ycat.at[u, pl.ds(T, T), :], to)

    HALF = T // 2

    def exchange_part(k, j):
        return (at(j, HALF), pl.ds(0, D)) if k < 3 else (pl.ds(0, T), at(j, 256))

    def exchange_copy(k, j):
        rows, cols = exchange_part(k, j)
        return remote(
            ("ex", k), j, 4, r.ex_out.at[k % 2, rows, cols], r.ex_in.at[k % 2, rows, cols], to_mp
        )

    def exchange_half(k, half, term):
        for j in range(D // 256):
            cols = pl.ds(j * 256, 256)
            r.ex_out[k % 2, at(half, HALF), cols] = term(at(half, HALF), cols).astype(bf16)
        exchange_copy(k, half).start()

    def exchange_start(k, term):
        for j in range(D // 256):
            r.ex_out[k % 2, :, pl.ds(j * 256, 256)] = term(j).astype(bf16)
            exchange_copy(k, j).start()

    def exchange_wait(k):
        for j in range(4):
            exchange_copy(k, j).wait()

    def exchanged(k, rows):
        return r.ex_out[k % 2, rows, :].astype(f32) + r.ex_in[k % 2, rows, :].astype(f32)

    def kept(u):
        return r.fc_out_v.at[at(u % 8, 256), at(u // 8, W)]

    def core_out(u):
        return r.fc_in_v.at[at(u % 4, 256), at(u // 4, W)]

    def copy_core(u):
        return remote("core", u, KV, core_out(u), r.core_in.at[u], to_c)

    def copy_half(u):
        return remote("half", u, UNITS, r.half_out.at[u], r.half_in.at[u], partners_of[1 - axis_of(u)])

    def copy_last(u):
        return remote("last", u, UNITS, r.last_out.at[u], r.last_in.at[u], to_z2)

    def kvc_copy(v):
        return remote("kvc", v, 2, r.kvc_out.at[v], r.kvc_in.at[v], to_c)

    def kvy_copy(v):
        return remote("kvy", v, 2, r.kvy_out.at[v], r.kvy_in.at[v], to_y)

    arrived = set()

    def product(u):
        w = x_of(u)
        if w not in arrived:
            arrived.add(w)
            (copy_x(w) if x_axis(w) == AXIS_Y else copy_shared(w, 1 - m)).wait_recv()
        for copy in gathers(u):
            copy.wait_recv()
        for h in range(W // 256):
            cols = pl.ds(h * 256, 256)
            rhs = ycat[u, :, cols]
            core_out(u)[:, cols] = nn(xcat[w, at(1 - c, 256), :], rhs).astype(bf16)
            kept(u)[:, cols] = nn(xcat[w, at(c, 256), :], rhs).astype(bf16)
        copy_core(u).start()

    def local_sum(u, rows):
        if u < KV:
            return kept(u)[rows, :].astype(f32) + r.core_in[u, rows, :].astype(f32)
        v = u - KV
        wide = pl.ds(pl.multiple_of(y * 256 + rows.start, 64), rows.size)
        mine = r.memory_v[wide, pl.ds(v * W, W)].astype(f32) + r.kvc_in[v, wide, :].astype(f32)
        return mine + r.kvy_in[v, rows, :].astype(f32)

    def halve(u):
        if u < KV:
            copy_core(u).wait_recv()
        else:
            kvy_copy(u - KV).wait_recv()
        r.half_out[u] = local_sum(u, at(1 - bits[1 - axis_of(u)], 128)).astype(bf16)
        copy_half(u).start()

    def part_rows(u, high):
        return pl.ds(pl.multiple_of(bits[1 - axis_of(u)] * 128 + high * 64, 64), 64)

    def halve_last(u):
        copy_half(u).wait_recv()
        got = r.half_in[u, at(1 - zh, 64), :].astype(f32)
        r.last_out[u] = (local_sum(u, part_rows(u, 1 - zh)) + got).astype(bf16)
        copy_last(u).start()

    def total(u):
        copy_last(u).wait_recv()
        got = r.half_in[u, at(zh, 64), :].astype(f32) + r.last_in[u].astype(f32)
        x = local_sum(u, part_rows(u, zh)) + got
        if u < FC_IN:
            r.g_fc_out[:, at(u, W)] = x
        elif u < CROSS_OUT:
            r.g_fc_in[:, at(u - FC_IN, W)] = x
        elif u < QKV:
            (r.g_cross_out, r.g_cross_q, r.g_self_out)[u - CROSS_OUT][...] = x
        elif u < KV:
            r.g_qkv[u - QKV] = x
        else:
            r.g_kv[u - KV] = x

    def project():
        load(r.tokens).wait()
        for part in range(3):
            load_qkv(part).wait()
            if part == 0:
                for src in first:
                    load(src).wait()

            def packed(j, part=part):
                cols = at(j, 256)
                x = nn(r.tokens_v[...], r.wqkv_v[part, :, cols])
                if part == 0:
                    x = x + r.self_qv_bias_v[0:1, cols]
                if part == 2:
                    x = x + r.self_qv_bias_v[1:2, cols]
                r.packed[part, :, cols] = x.astype(bf16)

            loop(HL // 256, packed, 2)

    key_row = lax.broadcasted_iota(jnp.int32, (T, 2 * T), 0)
    query_row = lax.rem(lax.broadcasted_iota(jnp.int32, (T, 2 * T), 1), T)

    def self_pair(p):
        cols = at(p, 128)
        q, k, v = (r.packed[i, :, cols] for i in range(3))
        s = nt(k, stacked(q)) * scale
        s = jnp.where((key_row <= query_row) & (key_row < r.dec_len_v[0]), s, -1e30)
        w = jnp.exp(s - jnp.max(s, axis=0, keepdims=True))
        probs = w / jnp.sum(w, axis=0, keepdims=True)
        r.self_probs[p] = probs
        mixed = nn(v.astype(f32).T.astype(bf16), probs.astype(bf16))
        ycat[SELF_OUT, 0:T, cols] = unstacked(mixed).astype(bf16)

    def self_attention():
        loop(PAIRS, self_pair, 4)

    def send_first():
        load(r.self_out).wait()
        pl.semaphore_wait(barrier, 5)
        for half in range(2):
            exchange_half(0, half, lambda rows, cols: nn(ycat[SELF_OUT, rows, :], r.self_out_v[:, cols]))
        copy_y(SELF_OUT).start()
        load(r.memory).wait()

    key, value, turned = r.key, r.value, r.turned
    odd = lax.broadcasted_iota(jnp.int32, (256, 256), 0)
    odd = jnp.where(odd < 128, 2 * odd, 2 * odd - 255)
    select = (lax.broadcasted_iota(jnp.int32, (256, 256), 1) == odd).astype(f32).astype(bf16)

    def part_weights(i):
        rows = at(i, CH)
        x = nn(select, r.cross_kv_v[rows].reshape(2 * CH, HL)).astype(bf16)
        r.wkv_v[0, rows, :] = x[:CH]
        r.wkv_v[1, rows, :] = x[CH:]

    BIG = 512

    def pair_rows(i):
        rows = at(i, BIG)
        for j in range(HL // 256):
            cols = pl.ds(j * 256, 256)
            key[rows, cols] = nn(r.memory_v[rows, :], r.wkv_v[0, :, cols]).astype(bf16)
            x = nn(r.memory_v[rows, :], r.wkv_v[1, :, cols]) + r.cross_qv_bias_v[1:2, cols]
            value[rows, cols] = x.astype(bf16)
            for b in range(BIG // 128):
                for h in range(2):
                    block = x[b * 128 : (b + 1) * 128, h * 128 : (h + 1) * 128].T
                    turned[pl.ds(j * 256 + h * 128, 128), pl.ds(pl.multiple_of(i * BIG + b * 128, 128), 128)] = block.astype(bf16)

    def turn(src):
        def step(i):
            rows = at(i, CH)
            for j in range(HL // 128):
                turned[pl.ds(j * 128, 128), rows] = src[rows, pl.ds(j * 128, 128)].astype(f32).T.astype(bf16)

        loop(ML // CH, step, 2)

    def memory_pair():
        load(r.cross_kv).wait()
        loop(D // CH, part_weights, 2)
        loop(ML // BIG, pair_rows)

    def turn_memory(i):
        rows = at(i, CH)

        def block(b):
            t = r.memory_v[rows, at(b, 128)].astype(f32).T.astype(bf16)
            side, zlow, zhigh = lax.rem(b, 2), lax.rem(b // 2, 2), b // 4
            for half in range(2):
                to = half * 512 + side * 256 + zlow * 128 + zhigh * 64
                r.memory_t[pl.ds(pl.multiple_of(to, 64), 64), rows] = t[half * 64 : (half + 1) * 64]

        loop(D // 128, block, 4)

    def normalize(v, k):
        mean = jnp.mean(v, axis=-1, keepdims=True)
        centred = v - mean
        inv = lax.rsqrt(jnp.mean(centred * centred, axis=-1, keepdims=True) + epsilon)
        unit = centred * inv
        return unit * gain[k : k + 1, :] + shift[k : k + 1, :], unit, inv

    def norm_back(g, unit, inv, k):
        w = g * gain[k : k + 1, :]
        return inv * (w - jnp.mean(w, axis=-1, keepdims=True) - unit * jnp.mean(w * unit, axis=-1, keepdims=True))

    def norm_rows(k, half, base, unit_ref):
        exchange_copy(k, half).wait()
        for i in range(HALF // 16):
            rows = pl.ds(half * HALF + i * 16, 16)
            v = base[rows, :].astype(f32) + (exchanged(k, rows) + out_bias[k : k + 1, :])
            norm, unit, inv = normalize(v, k)
            r.norm[rows, :] = norm
            unit_ref[rows, :] = unit
            r.inv[k, rows, :] = jnp.broadcast_to(inv, (16, 128))
            low[rows, :] = norm.astype(bf16)

    def first_norm(half):
        norm_rows(0, half, r.tokens_v, r.unit0)

    probs_ref = r.probs
    dp_ref = r.dp
    low_probs = r.low_probs
    mem_row = lax.broadcasted_iota(jnp.int32, (CH, 2 * T), 0)
    chunks = ML // CH

    def fold(x, op):
        total = x[0:8]
        for i in range(1, x.shape[0] // 8):
            total = op(total, x[8 * i : 8 * i + 8])
        return total

    def cross_quad(half, g):
        cols, rows_q, index = pl.ds(g * 256, 256), pl.ds(half * HALF, HALF), half * (HL // 256) + g
        q = stacked_quad(r.query[rows_q, cols])
        top = jnp.full((8, 2 * T), -1e30, f32)
        for b in range(ML // BIG):
            scores = nt(key[pl.ds(b * BIG, BIG), cols], q)
            for i in range(BIG // CH):
                first = b * BIG + i * CH
                s = scores[i * CH : (i + 1) * CH] * (scale * LOG2E)
                s = jnp.where(mem_row < r.mem_len_v[0] - first, s, -1e30)
                probs_ref[index, pl.ds(first, CH), :] = s
                top = jnp.maximum(top, fold(s, jnp.maximum))
        top = jnp.max(top, axis=0, keepdims=True)
        total = jnp.zeros((8, 2 * T), f32)
        for i in range(chunks):
            rows = at(i, CH)
            w = jnp.exp2(probs_ref[index, rows, :] - top)
            probs_ref[index, rows, :] = w
            low_probs[rows, cols] = w.astype(bf16)
            total = total + fold(w, jnp.add)
        part = 1.0 / jnp.sum(total, axis=0, keepdims=True)
        r.part[index] = jnp.broadcast_to(part, (8, 2 * T))
        mixed = nn(turned[cols, :], low_probs[:, cols]) * part
        ycat[CROSS_OUT, rows_q, cols] = unstacked_quad(mixed).astype(bf16)

    def cross_attention(half):
        if half == 0:
            load(r.cross_q).wait()
        rows = pl.ds(half * HALF, HALF)
        for j in range(HL // 256):
            cols = pl.ds(j * 256, 256)
            x = nn(low[rows, :], r.cross_q_v[:, cols]) + r.cross_qv_bias_v[0:1, cols]
            r.query[rows, cols] = x.astype(bf16)
        for g in range(HL // 256):
            cross_quad(half, g)

    def send_second(half):
        if half == 0:
            load(r.cross_out).wait()
        exchange_half(1, half, lambda rows, cols: nn(ycat[CROSS_OUT, rows, :], r.cross_out_v[:, cols]))
        if half == 1:
            copy_y(CROSS_OUT).start()

    def second_norm(half):
        norm_rows(1, half, r.norm, r.unit1)

    def normal_share(h):
        return 0.5 * (1.0 + lax.erf(h * 0.7071067811865476))

    def hidden_units(half):
        if half == 0:
            load(r.fc_in).wait()
        rows = pl.ds(half * HALF, HALF)

        def unit(b):
            for part in range(2):
                j = 2 * b + part
                cols = at(j, 256)
                h = nn(low[rows, :], r.fc_in_v[:, cols]) + r.fc_in_bias_v[:, cols]
                dp_ref[1, pl.ds(j * T + half * HALF, HALF), :] = h
                ycat[FC_OUT + b, rows, pl.ds(part * 256, 256)] = (h * normal_share(h)).astype(bf16)
            copy_y_half(FC_OUT + b, half).start()

        for b in range(FL // W):
            unit(b)

    def slopes(j):
        h = dp_ref[1, at(j, T), :]
        dp_ref[1, at(j, T), :] = normal_share(h) + h * jnp.exp(-0.5 * h * h) * 0.3989422804014327

    def ffn_term(rows, cols):
        total = nn(ycat[FC_OUT, rows, :], r.fc_out_v[pl.ds(0, W), cols])
        for b in range(1, FL // W):
            total = total + nn(ycat[FC_OUT + b, rows, :], r.fc_out_v[pl.ds(b * W, W), cols])
        return total

    def send_third(half):
        if half == 0:
            load(r.fc_out).wait()
        exchange_half(2, half, ffn_term)

    row16 = lax.broadcasted_iota(jnp.int32, (16, D), 0)
    zero8 = jnp.zeros((8, D), f32)

    def sums_of(body, k):
        def step(i, carry):
            g, unit, rounded = body(i)
            return (
                carry[0] + fold(rounded, jnp.add),
                carry[1] + fold(g * unit, jnp.add),
                carry[2] + fold(g, jnp.add),
            )

        carry = (zero8, zero8, zero8)
        for i in range(T // 16):
            carry = step(i, carry)
        bias, gains, shifts = carry
        sm[k : k + 1, :] = col_sum(bias)
        sm[3 + k : 4 + k, :] = col_sum(gains)
        sm[6 + k : 7 + k, :] = col_sum(shifts)

    def output_rows(i):
        rows = at(i, 16)
        v = r.norm[rows, :] + (exchanged(2, rows) + out_bias[2:3, :])
        norm, unit, inv = normalize(v, 2)
        r.layer_out[rows, :] = norm.astype(bf16)
        g = jnp.where(row16 + i * 16 < r.dec_len_v[0], r.cotangent_v[rows, :].astype(f32), 0.0)
        grad = norm_back(g, unit, inv, 2)
        r.grad[rows, :] = grad
        rounded = grad.astype(bf16)
        low[rows, :] = rounded
        return g, unit, rounded.astype(f32)

    def output_norm():
        load(r.cotangent).wait()
        for half in range(2):
            exchange_copy(2, half).wait()
        sums_of(output_rows, 2)

    def hidden_grad(j):
        cols = at(j, 256)
        g = nt(low[...], r.fc_out_v[at(j, 256), :]) * dp_ref[1, at(j, T), :]
        rounded = g.astype(bf16)
        ycat[FC_IN + j // 2, 0:T, at(j % 2, 256)] = rounded
        sm[pl.ds(11 + j // 4, 1), at(j % 4, 256)] = col_sum(rounded.astype(f32))

    def hidden_grads():
        for b in range(FL // W):
            hidden_grad(2 * b)
            hidden_grad(2 * b + 1)
            copy_y(FC_IN + b).start()

    def hidden_term(j):
        rows = at(j, 256)
        total = nt(ycat[FC_IN, 0:T, :], r.fc_in_v[rows, pl.ds(0, W)])
        for b in range(1, FL // W):
            total = total + nt(ycat[FC_IN + b, 0:T, :], r.fc_in_v[rows, pl.ds(b * W, W)])
        return total

    def send_fourth():
        exchange_start(3, hidden_term)

    def grad_rows(k, e, unit_ref):
        def body(i):
            rows = at(i, 16)
            g = r.grad[rows, :] + exchanged(e, rows)
            unit = unit_ref[rows, :]
            grad = norm_back(g, unit, r.inv[k, rows, 0:1], k)
            r.grad[rows, :] = grad
            rounded = grad.astype(bf16)
            low[rows, :] = rounded
            return g, unit, rounded.astype(f32)

        exchange_wait(e)
        sums_of(body, k)

    mixed_grad = r.mixed_grad

    def second_back():
        grad_rows(1, 3, r.unit1)

    def mixed_from(weights):
        for j in range(HL // 256):
            mixed_grad[:, at(j, 256)] = nt(low[...], weights[at(j, 256), :]).astype(bf16)

    def cross_mixed_grad():
        mixed_from(r.cross_out_v)

    def cross_back(g):
        cols = pl.ds(g * 256, 256)
        halves = [pl.ds(half * HALF, HALF) for half in range(2)]
        index = [half * (HL // 256) + g for half in range(2)]
        gs = [stacked_quad(mixed_grad[rows, cols]) for rows in halves]
        part = [r.part[i, 0:1, :] for i in index]
        total = [jnp.zeros((8, 2 * T), f32)] * 2
        both = jnp.concatenate(gs, axis=0)
        lanes = [pl.ds(half * 2 * T, 2 * T) for half in range(2)]
        for b in range(ML // BIG):
            big = pl.ds(b * BIG, BIG)
            for half in range(2):
                dbig = nt(value[big, cols], gs[half])
                for i in range(BIG // CH):
                    rows = pl.ds(b * BIG + i * CH, CH)
                    probs = probs_ref[index[half], rows, :] * part[half]
                    dprobs = dbig[i * CH : (i + 1) * CH]
                    dp_ref[half, rows, :] = dprobs
                    probs_ref[index[half], rows, :] = probs
                    total[half] = total[half] + fold(probs * dprobs, jnp.add)
                    low_probs[rows, lanes[half]] = probs.astype(bf16)
            value[big, cols] = nn(low_probs[big, :], both).astype(bf16)
        total = [jnp.sum(x, axis=0, keepdims=True) for x in total]
        both = jnp.concatenate([stacked_quad(r.query[rows, cols]) for rows in halves], axis=0)
        for b in range(ML // BIG):
            big = pl.ds(b * BIG, BIG)
            for half in range(2):
                for i in range(BIG // CH):
                    rows = pl.ds(b * BIG + i * CH, CH)
                    ds = probs_ref[index[half], rows, :] * (dp_ref[half, rows, :] - total[half])
                    low_probs[rows, lanes[half]] = ds.astype(bf16)
            key[big, cols] = (nn(low_probs[big, :], both) * scale).astype(bf16)
        for half in range(2):
            dq = nn(turned[cols, :], low_probs[:, lanes[half]])
            ycat[CROSS_Q, halves[half], cols] = (unstacked_quad(dq) * scale).astype(bf16)

    def send_fifth():
        exchange_start(4, lambda j: nt(ycat[CROSS_Q, 0:T, :], r.cross_q_v[at(j, 256), :]))
        copy_y(CROSS_Q).start()
        sm[10:11, 0:HL] = col_sum(ycat[CROSS_Q, 0:T, :].astype(f32))
        sm[10:11, HL : 2 * HL] = col_sum(value[...].astype(f32))

    def gm_copy(i):
        cols = at(i, 256)
        return remote("gm", i, 4, r.gm_out.at[:, cols], r.gm_in.at[:, cols], to_mp)

    def memory_term(i):
        cols = pl.ds(i * 256, 256)
        for half, to in ((1 - m, r.gm_out), (m, r.grad_memory)):
            rows = at(half, ML // 2)
            x = nt(key[rows, :], r.wkv_v[0, cols, :]) + nt(value[rows, :], r.wkv_v[1, cols, :])
            to[:, cols] = x.astype(bf16)
        gm_copy(i).start()

    def memory_sum(i):
        gm_copy(i).wait()
        cols = pl.ds(i * 256, 256)
        r.grad_memory[:, cols] = (r.grad_memory[:, cols].astype(f32) + r.gm_in[:, cols].astype(f32)).astype(bf16)

    def pair_product(v):
        pair = key if v == 0 else value
        for h in range(2):
            cols = pl.ds(h * 256, 256)
            rhs = pair[:, cols]
            r.kvc_out[v, :, cols] = nn(r.memory_t[at(1 - c, D // 2), :], rhs).astype(bf16)
            r.memory_v[0 : D // 2, pl.ds(v * W + h * 256, 256)] = nn(r.memory_t[at(c, D // 2), :], rhs).astype(bf16)
        kvc_copy(v).start()

    def pair_halve(v):
        kvc_copy(v).wait_recv()
        rows = at(1 - y, 256)
        mine = r.memory_v[rows, pl.ds(v * W, W)].astype(f32)
        r.kvy_out[v] = (mine + r.kvc_in[v, rows, :].astype(f32)).astype(bf16)
        kvy_copy(v).start()

    def first_back():
        grad_rows(0, 4, r.unit0)

    def self_back(p):
        cols = at(p, 128)
        q, k, v = (r.packed[i, :, cols] for i in range(3))
        probs = r.self_probs[p]
        g = stacked(mixed_grad[:, cols])
        dprobs = nt(v, g)
        ycat[QKV + 2, 0:T, cols] = nn(probs.astype(bf16), g).astype(bf16)
        ds = (probs * (dprobs - jnp.sum(probs * dprobs, axis=0, keepdims=True))).astype(bf16)
        ycat[QKV + 1, 0:T, cols] = (nn(ds, stacked(q)) * scale).astype(bf16)
        dq = nn(k.astype(f32).T.astype(bf16), ds)
        ycat[QKV, 0:T, cols] = (unstacked(dq) * scale).astype(bf16)

    def self_grads():
        mixed_from(r.self_out_v)
        loop(PAIRS, self_back, 4)
        for b in range(3):
            copy_y(QKV + b).start()
        sm[9:10, 0:HL] = col_sum(ycat[QKV, 0:T, :].astype(f32))
        sm[9:10, HL : 2 * HL] = col_sum(ycat[QKV + 2, 0:T, :].astype(f32))
        sm[13:16, :] = jnp.zeros((3, D), f32)

    def packed_term(j):
        rows = at(j, 256)
        total = nt(ycat[QKV, 0:T, :], r.wqkv_v[0, rows, :])
        for b in range(1, 3):
            total = total + nt(ycat[QKV + b, 0:T, :], r.wqkv_v[b, rows, :])
        return total

    def send_sixth():
        exchange_start(5, packed_term)

    def token_grads():
        def body(i):
            rows = at(i, 16)
            r.grad_tokens[rows, :] = (r.grad[rows, :] + exchanged(5, rows)).astype(bf16)

        exchange_wait(5)
        loop(T // 16, body, 2)

    doubling = (to_c, to_y, to_z1, to_z2)

    def small_copy(k):
        return remote("small", k, 4, r.sm_out.at[k], r.sm_in.at[k], doubling[k])

    def small_step(k):
        if k > 0:
            small_copy(k - 1).wait()
            (sm if k < 4 else r.sums)[...] = r.sm_out[k - 1].astype(f32) + r.sm_in[k - 1].astype(f32)
        if k < 4:
            r.sm_out[k] = sm[...].astype(bf16)
            small_copy(k).start()

    def each(step, *indices):
        for i in indices:
            step(i)

    project()
    self_attention()
    send_first()
    memory_pair()
    first_norm(0)
    cross_attention(0)
    send_second(0)
    each(turn_memory, 0)
    first_norm(1)
    cross_attention(1)
    send_second(1)
    send_x(X_FIRST, low)
    second_norm(0)
    hidden_units(0)
    send_third(0)
    second_norm(1)
    hidden_units(1)
    send_third(1)
    turn(key)
    each(slopes, 7)
    send_x(X_SECOND, low)
    each(turn_memory, 7)
    each(slopes, 3)
    each(turn_memory, 3)
    each(slopes, 4, 0, 6, 5, 2, 1)
    output_norm()
    hidden_grads()
    send_x(X_FFN, low)
    send_fourth()
    each(product, 4)
    send_x(X_TOKENS, r.tokens_v)
    share_x(X_FFN)
    each(halve, 4)
    each(product, 5)
    second_back()
    cross_mixed_grad()
    send_x(X_CROSS, low)
    each(product, 2)
    each(turn_memory, 6)
    each(halve, 5)
    each(cross_back, 0)
    each(product, 7)
    each(halve_last, 4)
    each(halve, 2)
    each(cross_back, 1)
    send_fifth()
    each(halve, 7)
    each(product, 6, 3, 1)
    share_x(X_CROSS)
    each(halve_last, 5)
    each(halve, 3)
    each(halve_last, 2)
    each(turn_memory, 4)
    each(halve, 6)
    each(product, 0)
    each(memory_term, 3)
    each(halve, 1)
    each(turn_memory, 2)
    first_back()
    self_grads()
    each(halve_last, 7)
    each(total, 5)
    each(halve, 0)
    each(small_step, 0)
    each(product, 9)
    each(halve_last, 3)
    each(turn_memory, 5)
    each(product, 8)
    each(memory_term, 2)
    send_x(X_SELF, low)
    each(halve, 9)
    each(small_step, 1)
    each(product, 11)
    each(turn_memory, 1)
    each(halve_last, 1, 6)
    each(memory_sum, 2)
    each(total, 3)
    each(halve, 11)
    each(total, 4)
    each(pair_product, 1, 0)
    each(product, 12)
    each(halve_last, 9)
    share_x(X_SELF)
    each(memory_term, 1)
    each(product, 13)
    each(halve, 8)
    each(halve_last, 0)
    each(pair_halve, 1)
    each(halve, 12, 13)
    send_sixth()
    each(small_step, 2)
    each(pair_halve, 0)
    each(product, 10)
    each(halve_last, 8, 11)
    each(total, 2, 1, 6)
    each(halve, 10, 15)
    token_grads()
    each(memory_term, 0)
    each(halve_last, 13, 12)
    each(total, 7)
    each(halve, 14)
    each(halve_last, 10)
    each(total, 8)
    each(small_step, 3)
    each(halve_last, 15)
    each(memory_sum, 1)
    each(total, 10, 13, 9)
    each(halve_last, 14)
    each(memory_sum, 0)
    each(total, 15, 11)
    each(small_step, 4)
    each(total, 12, 0)
    each(memory_sum, 3)
    each(total, 14)
    for w in range(6):
        copy_x(w).wait_send()
        if x_axis(w) == AXIS_Z:
            copy_shared(w, m).wait_send()
    for u in range(UNITS):
        if u < KV:
            for copy in gathers(u):
                copy.wait_send()
            copy_core(u).wait_send()
        copy_half(u).wait_send()
        copy_last(u).wait_send()
    for v in range(2):
        kvc_copy(v).wait_send()
        kvy_copy(v).wait_send()
    refs_at.update(remote=sum(n for _, n in given.values()), local=sum(n for _, n in local_given.values()))


REMOTE_SEMS = 160
LAYER_VMEM = 59 * 2**20
LOCAL_SEMS = 64


def layer(tokens, memory, mem_len, dec_len, cotangent, wqkv, self_qv_bias, self_out, cross_q, cross_kv, cross_qv_bias, cross_out, fc_in, fc_in_bias, fc_out, out_bias, norm_gain, norm_bias):
    T, D = tokens.shape
    ML = memory.shape[0]
    HL = self_out.shape[0]
    FL = fc_out.shape[0]
    R = D // GROUP
    W = 512
    PAIRS = HL // 128
    anywhere = pl.BlockSpec(memory_space=pl.ANY)
    big = dict(tokens=tokens, memory=memory, cotangent=cotangent, wqkv=wqkv, self_out=self_out, cross_q=cross_q, cross_kv=cross_kv,
               cross_out=cross_out, fc_in=fc_in, fc_out=fc_out)
    small = dict(self_qv_bias=self_qv_bias, cross_qv_bias=cross_qv_bias, fc_in_bias=fc_in_bias, out_bias=out_bias,
                 norm_gain=norm_gain, norm_bias=norm_bias)
    scalars = dict(mem_len=mem_len, dec_len=dec_len)
    outs = dict(
        layer_out=((T, D), bf16),
        grad_tokens=((T, D), bf16),
        grad_memory=((ML // 2, D), bf16),
        g_qkv=((3, R, HL), f32),
        g_self_out=((R, HL), f32),
        g_cross_q=((R, HL), f32),
        g_kv=((2, R, HL), f32),
        g_cross_out=((R, HL), f32),
        g_fc_in=((R, FL), f32),
        g_fc_out=((R, FL), f32),
        sums=((16, D), f32),
    )
    scratch = {name + "_v": (x.shape, x.dtype) for name, x in (big | small).items()}
    scratch |= dict(
        wkv_v=((2, D, HL), bf16),
        packed=((3, T, HL), bf16),
        self_probs=((PAIRS, T, 2 * T), f32),
        low=((T, D), bf16),
        ycat=((KV, 2 * T, W), bf16),
        xcat=((6, 512, 256), bf16),
        xsend=((6, 512, 128), bf16),
        ex_out=((2, T, D), bf16),
        ex_in=((2, T, D), bf16),
        norm=((T, D), f32),
        unit0=((T, D), f32),
        unit1=((T, D), f32),
        inv=((2, T, 128), f32),
        grad=((T, D), f32),
        key=((ML, HL), bf16),
        value=((ML, HL), bf16),
        turned=((HL, ML), bf16),
        query=((T, HL), bf16),
        mixed_grad=((T, HL), bf16),
        probs=((PAIRS, ML, 2 * T), f32),
        part=((PAIRS, 8, 2 * T), f32),
        low_probs=((ML, 4 * T), bf16),
        dp=((2, ML, 2 * T), f32),
        memory_t=((D, ML), bf16),
        gm_out=((ML // 2, D), bf16),
        gm_in=((ML // 2, D), bf16),
        core_in=((KV, 256, W), bf16),
        kvc_out=((2, 512, W), bf16),
        kvc_in=((2, 512, W), bf16),
        kvy_out=((2, 256, W), bf16),
        kvy_in=((2, 256, W), bf16),
        half_out=((UNITS, 128, W), bf16),
        half_in=((UNITS, 128, W), bf16),
        last_out=((UNITS, 64, W), bf16),
        last_in=((UNITS, 64, W), bf16),
        sm=((16, D), f32),
        sm_out=((4, 16, D), bf16),
        sm_in=((4, 16, D), bf16),
    )
    sems = dict(send_sem=REMOTE_SEMS, recv_sem=REMOTE_SEMS, local_sem=LOCAL_SEMS)
    lengths = {name + "_v": pltpu.SMEM((1,), jnp.int32) for name in scalars}
    names = [*big, *small, *scalars, *outs, *scratch, *lengths, *sems]
    got = {}
    out = pl.pallas_call(
        functools.partial(kernel, names, got),
        out_shape=[pltpu.VMEM(s, t) for s, t in outs.values()],
        in_specs=[anywhere] * (len(big) + len(small) + len(scalars)),
        out_specs=[pl.BlockSpec(memory_space=pltpu.VMEM)] * len(outs),
        scratch_shapes=[pltpu.VMEM(s, t) for s, t in scratch.values()]
        + [*lengths.values()]
        + [pltpu.SemaphoreType.DMA((count,)) for count in sems.values()],
        compiler_params=pltpu.CompilerParams(
            collective_id=0, has_side_effects=True, vmem_limit_bytes=LAYER_VMEM
        ),
        name="layer",
    )(*big.values(), *small.values(), *scalars.values())
    assert got["remote"] <= REMOTE_SEMS and got["local"] <= LOCAL_SEMS, got
    return types.SimpleNamespace(**dict(zip(outs, out)))


def finish_kernel(count, small, *refs):
    ins, outs, scratch = refs[: count + 2], refs[count + 2 : 2 * count + 3 + small], refs[2 * count + 3 + small :]
    turned, made, sem = scratch[0], scratch[1:-1], scratch[-1]
    stores = [
        pltpu.make_async_copy(a, b, sem.at[i]) for i, (a, b) in enumerate(zip((*ins[:count], turned, *made), outs))
    ]
    for i in range(count):
        stores[i].start()
    kv, sums = ins[count:]
    for part in range(2):
        turned[:, part, :] = kv[part]
    stores[count].start()
    self_bias, cross_bias, hidden_bias, out_bias, gains, shifts = made
    width = self_bias.shape[1]
    for row, to in ((9, self_bias), (10, cross_bias)):
        for part in range(2):
            to[part : part + 1, :] = sums[row : row + 1, part * width : (part + 1) * width]
    features = sums.shape[1]
    for part in range(hidden_bias.shape[1] // features):
        hidden_bias[:, part * features : (part + 1) * features] = sums[11 + part : 12 + part, :]
    for first, to in ((0, out_bias), (3, gains), (6, shifts)):
        to[...] = sums[first : first + 3, :]
    for i in range(small):
        stores[count + 1 + i].start()
    for store in stores:
        store.wait()


def finish(whole, kv, sums):
    R, HL = kv.shape[1:]
    D = sums.shape[1]
    anywhere = pl.BlockSpec(memory_space=pl.ANY)
    in_vmem = pl.BlockSpec(memory_space=pltpu.VMEM)
    small = [(2, HL), (2, HL), (1, 4 * HL), (3, D), (3, D), (3, D)]
    return pl.pallas_call(
        functools.partial(finish_kernel, len(whole), len(small)),
        out_shape=[jax.ShapeDtypeStruct(x.shape, x.dtype) for x in whole]
        + [jax.ShapeDtypeStruct((R, 2, HL), f32)]
        + [jax.ShapeDtypeStruct(shape, f32) for shape in small],
        in_specs=[in_vmem] * (len(whole) + 2),
        out_specs=[anywhere] * (len(whole) + 1 + len(small)),
        scratch_shapes=[pltpu.VMEM(shape, f32) for shape in [(R, 2, HL), *small]]
        + [pltpu.SemaphoreType.DMA((len(whole) + 1 + len(small),))],
        compiler_params=pltpu.CompilerParams(vmem_limit_bytes=8 * 2**20),
        name="finish",
    )(*whole, kv, sums)


def per_device(tokens, memory, mem_len, dec_len, cotangent, self_qkv, self_qv_bias, self_out, cross_q, cross_kv, cross_qv_bias, cross_out, fc_in, fc_in_bias, fc_out, out_bias, norm_gain, norm_bias):
    D = tokens.shape[1]
    devices = lax.axis_size("dp")
    outer = devices // GROUP

    def regroup(x, axis, there):
        if outer == 1:
            return x
        sizes = (outer, GROUP) if there else (GROUP, outer)
        shape = x.shape
        x = x.reshape(shape[:axis] + sizes + (D // devices,) + shape[axis + 1 :])
        return jnp.swapaxes(x, axis, axis + 1).reshape(shape)

    tokens, memory, cotangent, self_out, cross_out, fc_out, out_bias, norm_gain, norm_bias = (
        regroup(x, 1, True)
        for x in (tokens, memory, cotangent, self_out, cross_out, fc_out, out_bias, norm_gain, norm_bias)
    )
    self_qkv, cross_q, cross_kv, fc_in = (regroup(x, 0, True) for x in (self_qkv, cross_q, cross_kv, fc_in))
    got = layer(
        tokens, memory, mem_len, dec_len, cotangent, self_qkv.transpose(1, 0, 2), self_qv_bias, self_out, cross_q,
        cross_kv, cross_qv_bias, cross_out, fc_in, fc_in_bias.reshape(1, -1), fc_out, out_bias,
        norm_gain, norm_bias,
    )
    groups = [[o * GROUP + i for o in range(outer)] for i in range(GROUP)]

    def spread(x, axis):
        if outer == 1:
            return x
        return lax.psum_scatter(x, "dp", scatter_dimension=axis, axis_index_groups=groups, tiled=True)

    (
        layer_out, grad_tokens, grad_memory, qkv, self_out, cross_q, cross_out, fc_in, fc_out, kv,
        self_bias, cross_bias, hidden_bias, out_bias, gains, shifts,
    ) = finish(
        (
            got.layer_out, got.grad_tokens, got.grad_memory, got.g_qkv, got.g_self_out, got.g_cross_q, got.g_cross_out,
            got.g_fc_in, got.g_fc_out,
        ),
        got.g_kv,
        got.sums,
    )
    small = (self_bias, cross_bias, hidden_bias, out_bias, gains, shifts)
    if outer > 1:
        small = lax.psum(small, "dp", axis_index_groups=groups)
    self_bias, cross_bias, hidden_bias, out_bias, gains, shifts = small
    return (
        regroup(layer_out, 1, False),
        regroup(grad_tokens, 1, False),
        regroup(grad_memory, 1, False),
        spread(qkv, 1).transpose(1, 0, 2),
        self_bias,
        spread(self_out, 0).T,
        spread(cross_q, 0),
        spread(kv, 0),
        cross_bias,
        spread(cross_out, 0).T,
        spread(fc_in, 0),
        hidden_bias.reshape(-1),
        spread(fc_out, 0).T,
        regroup(out_bias, 1, False),
        regroup(gains, 1, False),
        regroup(shifts, 1, False),
    )


def solution(mesh):
    placed = (
        P("dp", None),
        P("dp", None),
        P("dp"),
        P("dp"),
        P("dp", None),
        P(None, None, "mp"),
        P(None, "mp"),
        P("mp", None),
        P(None, "mp"),
        P(None, None, "mp"),
        P(None, "mp"),
        P("mp", None),
        P(None, "mp"),
        P("mp"),
        P("mp", None),
        P(),
        P(),
        P(),
    )
    return jax.shard_map(
        per_device,
        mesh=mesh,
        in_specs=placed,
        out_specs=(
            P("dp", None),
            P("dp", None),
            P(("dp", "mp"), None),
            P("dp", None, "mp"),
            P(None, "mp"),
            P("mp", "dp"),
            P("dp", "mp"),
            P("dp", None, "mp"),
            P(None, "mp"),
            P("mp", "dp"),
            P("dp", "mp"),
            P("mp"),
            P("mp", "dp"),
            P(),
            P(),
            P(),
        ),
        check_vma=False,
    )
```

```python
import functools
import types

import jax
import jax.numpy as jnp
from jax import lax
from jax.experimental import pallas as pl
from jax.experimental.pallas import tpu as pltpu
from jax.sharding import PartitionSpec as P

HEAD = 64
LOG2E = 1.4426950408889634
GROUP = 16
epsilon = 1e-05
MESH = pl.DeviceIdType.MESH
f32, bf16 = jnp.float32, jnp.bfloat16

FC_OUT, FC_IN, CROSS_OUT, CROSS_Q, SELF_OUT, QKV, KV = 0, 4, 8, 9, 10, 11, 14
UNITS = 16
X_TOKENS, X_FIRST, X_SECOND, X_FFN, X_CROSS, X_SELF = range(6)


AXIS_Y, AXIS_Z = 0, 1


def axis_of(unit):
    return AXIS_Z if unit < FC_IN or unit in (CROSS_OUT, SELF_OUT) else AXIS_Y


def x_axis(x):
    return AXIS_Z if x in (X_FFN, X_CROSS, X_SELF) else AXIS_Y


def x_of(unit):
    return ((X_FFN,) * 4 + (X_SECOND,) * 4 + (X_CROSS, X_FIRST, X_SELF) + (X_TOKENS,) * 3)[unit]


def nn(a, b):
    return lax.dot_general(a, b, (((1,), (0,)), ((), ())), preferred_element_type=f32)


def nt(a, b):
    return lax.dot_general(a, b, (((1,), (1,)), ((), ())), preferred_element_type=f32)


def loop(count, body, unroll=1):
    def step(i, carry):
        for j in range(unroll):
            body(i * unroll + j)
        return carry

    if unroll == count:
        step(0, 0)
    else:
        lax.fori_loop(0, count // unroll, step, 0)


def at(index, size):
    return pl.ds(index * size if isinstance(index, int) else pl.multiple_of(index * size, size), size)


def kernel(names, refs_at, *refs):
    r = types.SimpleNamespace(**dict(zip(names, refs)))
    T, D = r.tokens.shape
    ML = r.memory.shape[0]
    HL = r.self_out.shape[0]
    FL = r.fc_out.shape[0]
    W = 512
    PAIRS = HL // 128
    CH = 128
    scale = HEAD**-0.5

    d, m = lax.axis_index("dp"), lax.axis_index("mp")
    c, y = lax.rem(d, 2), lax.rem(d // 2, 2)
    zl, zh = lax.rem(d // 4, 2), lax.rem(d // 8, 2)
    to_mp = (d, 1 - m)
    to_c = (d + 1 - 2 * c, m)
    to_y = (d + 2 - 4 * y, m)
    to_z1 = (d + 4 - 8 * zl, m)
    to_z2 = (d + 8 - 16 * zh, m)

    bits, partners_of = (y, zl), (to_y, to_z1)

    barrier = pltpu.get_barrier_semaphore()
    for partner in (to_mp, to_c, to_y, to_z1, to_z2):
        pl.semaphore_signal(barrier, inc=1, device_id=partner, device_id_type=MESH)

    given = {}
    local_given = {}

    def slot(key, count=1):
        if key not in given:
            given[key] = sum(n for _, n in given.values()), count
        return given[key][0]

    def remote(key, index, count, src, dst, partner):
        base = slot(key, count) + index
        return pltpu.make_async_remote_copy(
            src_ref=src,
            dst_ref=dst,
            send_sem=r.send_sem.at[base],
            recv_sem=r.recv_sem.at[base],
            device_id=partner,
            device_id_type=MESH,
        )

    def local(key, src, dst, index=0, count=1):
        if key not in local_given:
            local_given[key] = sum(n for _, n in local_given.values()), count
        return pltpu.make_async_copy(src, dst, r.local_sem.at[local_given[key][0] + index])

    def load(src):
        name = next(k for k, v in vars(r).items() if v is src)
        return local(name, src, getattr(r, name + "_v"))

    def load_qkv(part):
        return local("qkv", r.wqkv.at[part], r.wqkv_v.at[part], part, 3)

    first = (r.dec_len, r.mem_len, r.self_qv_bias, r.cross_qv_bias, r.fc_in_bias, r.out_bias, r.norm_gain, r.norm_bias)
    load(r.tokens).start()
    load_qkv(0).start()
    for src in first:
        load(src).start()
    load_qkv(1).start()
    load_qkv(2).start()
    for src in (r.self_out, r.memory, r.cross_kv, r.cross_q, r.cross_out, r.fc_in, r.fc_out, r.cotangent):
        load(src).start()

    gain, shift, out_bias = r.norm_gain_v, r.norm_bias_v, r.out_bias_v
    sm = r.sm
    ycat, xcat, xsend = r.ycat, r.xcat, r.xsend
    low = r.low
    lane_low = lax.broadcasted_iota(jnp.int32, (T, 128), 1) < HEAD

    def stacked(pair):
        wide = pair.astype(f32)
        return jnp.concatenate(
            [jnp.where(lane_low, wide, 0.0).astype(bf16), jnp.where(lane_low, 0.0, wide).astype(bf16)], axis=0
        )

    def unstacked(wide):
        return jnp.concatenate([wide[:HEAD, :T], wide[HEAD:, T:]], axis=0).T

    quad_lane = lax.broadcasted_iota(jnp.int32, (T // 2, 256), 1) // HEAD

    def stacked_quad(quad):
        wide = quad.astype(f32)
        return jnp.concatenate([jnp.where(quad_lane == h, wide, 0.0).astype(bf16) for h in range(4)], axis=0)

    def unstacked_quad(wide):
        parts = []
        for b in range(2):
            span = slice(b * 128, (b + 1) * 128)
            t = wide[span, span].T
            parts.append(jnp.where(lane_low[: T // 2], t[: T // 2], t[T // 2 :]))
        return jnp.concatenate(parts, axis=1)

    def col_sum(x):
        return jnp.sum(x, axis=0, keepdims=True)

    def send_x(w, src):
        g = x_axis(w)

        def block(q):
            high, o = q // 2, lax.rem(q, 2)
            row = o * 128 + high * 64
            for own in (True, False):
                side = bits[g] if own else 1 - bits[g]
                from_block = high * 4 + (o * 2 + side if g == AXIS_Y else side * 2 + o)
                t = src[:, at(from_block, 128)].astype(f32).T.astype(bf16)
                for half in range(2):
                    rows = pl.ds(pl.multiple_of(half * 256 + row, 64), 64)
                    piece = t[half * 64 : (half + 1) * 64]
                    if own:
                        xcat[w, rows, 0:128] = piece
                    else:
                        xsend[w, rows, :] = piece

        loop(4, block, 2)
        copy_x(w).start()

    def copy_x(w):
        rows = pl.ds(0, 512) if x_axis(w) == AXIS_Y else at(m, 256)
        return remote(
            ("x", w), 0, 1, xsend.at[w, rows, :], xcat.at[w, rows, pl.ds(128, 128)], partners_of[x_axis(w)]
        )

    def copy_shared(w, side):
        held = xcat.at[w, at(side, 256), pl.ds(128, 128)]
        return remote(("shared", w), 0, 1, held, held, to_mp)

    def share_x(w):
        copy_x(w).wait_recv()
        copy_shared(w, m).start()

    def copy_y_half(u, half):
        rows, there = pl.ds(half * (T // 2), T // 2), pl.ds(T + half * (T // 2), T // 2)
        return remote(("half", half), u, 4, ycat.at[u, rows, :], ycat.at[u, there, :], partners_of[axis_of(FC_OUT)])

    def gathers(u):
        return [copy_y_half(u, half) for half in range(2)] if u < FC_IN else [copy_y(u)]

    def copy_y(u):
        to = partners_of[axis_of(u)]
        return remote("gather", u, KV, ycat.at[u, pl.ds(0, T), :], ycat.at[u, pl.ds(T, T), :], to)

    HALF = T // 2

    def exchange_part(k, j):
        return (at(j // 2, HALF), at(j % 2, D // 2)) if k < 3 else (pl.ds(0, T), at(j, 256))

    def exchange_copy(k, j):
        rows, cols = exchange_part(k, j)
        return remote(
            ("ex", k), j, 4, r.ex_out.at[k % 2, rows, cols], r.ex_in.at[k % 2, rows, cols], to_mp
        )

    def exchange_half(k, half, term):
        for j in range(D // 256):
            cols = pl.ds(j * 256, 256)
            r.ex_out[k % 2, at(half, HALF), cols] = term(at(half, HALF), cols).astype(bf16)
            if j % 2:
                exchange_copy(k, 2 * half + j // 2).start()

    def half_wait(k, half):
        for j in range(2):
            exchange_copy(k, 2 * half + j).wait()

    def exchange_start(k, term):
        for j in range(D // 256):
            r.ex_out[k % 2, :, pl.ds(j * 256, 256)] = term(j).astype(bf16)
            exchange_copy(k, j).start()

    def exchange_wait(k):
        for j in range(4):
            exchange_copy(k, j).wait()

    def exchanged(k, rows):
        return r.ex_out[k % 2, rows, :].astype(f32) + r.ex_in[k % 2, rows, :].astype(f32)

    def kept(u):
        return r.fc_out_v.at[at(u % 8, 256), at(u // 8, W)]

    def core_out(u):
        return r.fc_in_v.at[at(u % 4, 256), at(u // 4, W)]

    def copy_core(u):
        return remote("core", u, KV, core_out(u), r.core_in.at[u], to_c)

    def copy_half(u):
        return remote("half", u, UNITS, r.half_out.at[u], r.half_in.at[u], partners_of[1 - axis_of(u)])

    def copy_last(u):
        return remote("last", u, UNITS, r.last_out.at[u], r.last_in.at[u], to_z2)

    def kvc_copy(v):
        return remote("kvc", v, 2, r.kvc_out.at[v], r.kvc_in.at[v], to_c)

    def kvy_copy(v):
        return remote("kvy", v, 2, r.kvy_out.at[v], r.kvy_in.at[v], to_y)

    arrived = set()

    def product(u):
        w = x_of(u)
        if w not in arrived:
            arrived.add(w)
            (copy_x(w) if x_axis(w) == AXIS_Y else copy_shared(w, 1 - m)).wait_recv()
        for copy in gathers(u):
            copy.wait_recv()
        for h in range(W // 256):
            cols = pl.ds(h * 256, 256)
            rhs = ycat[u, :, cols]
            core_out(u)[:, cols] = nn(xcat[w, at(1 - c, 256), :], rhs).astype(bf16)
            kept(u)[:, cols] = nn(xcat[w, at(c, 256), :], rhs).astype(bf16)
        copy_core(u).start()

    def local_sum(u, rows):
        if u < KV:
            return kept(u)[rows, :].astype(f32) + r.core_in[u, rows, :].astype(f32)
        v = u - KV
        wide = pl.ds(pl.multiple_of(y * 256 + rows.start, 64), rows.size)
        mine = r.memory_v[wide, pl.ds(v * W, W)].astype(f32) + r.kvc_in[v, wide, :].astype(f32)
        return mine + r.kvy_in[v, rows, :].astype(f32)

    def halve(u):
        if u < KV:
            copy_core(u).wait_recv()
        else:
            kvy_copy(u - KV).wait_recv()
        r.half_out[u] = local_sum(u, at(1 - bits[1 - axis_of(u)], 128)).astype(bf16)
        copy_half(u).start()

    def part_rows(u, high):
        return pl.ds(pl.multiple_of(bits[1 - axis_of(u)] * 128 + high * 64, 64), 64)

    def halve_last(u):
        copy_half(u).wait_recv()
        got = r.half_in[u, at(1 - zh, 64), :].astype(f32)
        r.last_out[u] = (local_sum(u, part_rows(u, 1 - zh)) + got).astype(bf16)
        copy_last(u).start()

    def total(u):
        copy_last(u).wait_recv()
        got = r.half_in[u, at(zh, 64), :].astype(f32) + r.last_in[u].astype(f32)
        x = local_sum(u, part_rows(u, zh)) + got
        if u < FC_IN:
            r.g_fc_out[:, at(u, W)] = x
        elif u < CROSS_OUT:
            r.g_fc_in[:, at(u - FC_IN, W)] = x
        elif u < QKV:
            (r.g_cross_out, r.g_cross_q, r.g_self_out)[u - CROSS_OUT][...] = x
        elif u < KV:
            r.g_qkv[u - QKV] = x
        else:
            r.g_kv[u - KV] = x

    def project():
        load(r.tokens).wait()
        for part in range(3):
            load_qkv(part).wait()
            if part == 0:
                for src in first:
                    load(src).wait()

            def packed(j, part=part):
                cols = at(j, 256)
                x = nn(r.tokens_v[...], r.wqkv_v[part, :, cols])
                if part == 0:
                    x = x + r.self_qv_bias_v[0:1, cols]
                if part == 2:
                    x = x + r.self_qv_bias_v[1:2, cols]
                r.packed[part, :, cols] = x.astype(bf16)

            loop(HL // 256, packed, 2)

    key_row = lax.broadcasted_iota(jnp.int32, (T, 2 * T), 0)
    query_row = lax.rem(lax.broadcasted_iota(jnp.int32, (T, 2 * T), 1), T)

    def self_pair(p):
        cols = at(p, 128)
        q, k, v = (r.packed[i, :, cols] for i in range(3))
        s = nt(k, stacked(q)) * scale
        s = jnp.where((key_row <= query_row) & (key_row < r.dec_len_v[0]), s, -1e30)
        w = jnp.exp(s - jnp.max(s, axis=0, keepdims=True))
        probs = w / jnp.sum(w, axis=0, keepdims=True)
        r.self_probs[p] = probs
        mixed = nn(v.astype(f32).T.astype(bf16), probs.astype(bf16))
        ycat[SELF_OUT, 0:T, cols] = unstacked(mixed).astype(bf16)

    def self_attention():
        loop(PAIRS, self_pair, 4)

    def send_first():
        load(r.self_out).wait()
        pl.semaphore_wait(barrier, 5)
        for half in range(2):
            exchange_half(0, half, lambda rows, cols: nn(ycat[SELF_OUT, rows, :], r.self_out_v[:, cols]))
        copy_y(SELF_OUT).start()
        load(r.memory).wait()

    key, value, turned = r.key, r.value, r.turned
    odd = lax.broadcasted_iota(jnp.int32, (256, 256), 0)
    odd = jnp.where(odd < 128, 2 * odd, 2 * odd - 255)
    select = (lax.broadcasted_iota(jnp.int32, (256, 256), 1) == odd).astype(f32).astype(bf16)

    def part_weights(i):
        rows = at(i, CH)
        x = nn(select, r.cross_kv_v[rows].reshape(2 * CH, HL)).astype(bf16)
        r.wkv_v[0, rows, :] = x[:CH]
        r.wkv_v[1, rows, :] = x[CH:]

    BIG = 512

    def pair_rows(i):
        rows = at(i, BIG)
        for j in range(HL // 256):
            cols = pl.ds(j * 256, 256)
            key[rows, cols] = nn(r.memory_v[rows, :], r.wkv_v[0, :, cols]).astype(bf16)
            x = nn(r.memory_v[rows, :], r.wkv_v[1, :, cols]) + r.cross_qv_bias_v[1:2, cols]
            value[rows, cols] = x.astype(bf16)
            for b in range(BIG // 128):
                for h in range(2):
                    block = x[b * 128 : (b + 1) * 128, h * 128 : (h + 1) * 128].T
                    turned[pl.ds(j * 256 + h * 128, 128), pl.ds(pl.multiple_of(i * BIG + b * 128, 128), 128)] = block.astype(bf16)

    def turn(src):
        def step(i):
            rows = at(i, CH)
            for j in range(HL // 128):
                turned[pl.ds(j * 128, 128), rows] = src[rows, pl.ds(j * 128, 128)].astype(f32).T.astype(bf16)

        loop(ML // CH, step, 2)

    def memory_pair():
        load(r.cross_kv).wait()
        loop(D // CH, part_weights, 2)
        loop(ML // BIG, pair_rows)

    def turn_memory(i):
        rows = at(i, CH)

        def block(b):
            t = r.memory_v[rows, at(b, 128)].astype(f32).T.astype(bf16)
            side, zlow, zhigh = lax.rem(b, 2), lax.rem(b // 2, 2), b // 4
            for half in range(2):
                to = half * 512 + side * 256 + zlow * 128 + zhigh * 64
                r.memory_t[pl.ds(pl.multiple_of(to, 64), 64), rows] = t[half * 64 : (half + 1) * 64]

        loop(D // 128, block, 4)

    def normalize(v, k):
        mean = jnp.mean(v, axis=-1, keepdims=True)
        centred = v - mean
        inv = lax.rsqrt(jnp.mean(centred * centred, axis=-1, keepdims=True) + epsilon)
        unit = centred * inv
        return unit * gain[k : k + 1, :] + shift[k : k + 1, :], unit, inv

    def norm_back(g, unit, inv, k):
        w = g * gain[k : k + 1, :]
        return inv * (w - jnp.mean(w, axis=-1, keepdims=True) - unit * jnp.mean(w * unit, axis=-1, keepdims=True))

    def norm_rows(k, half, base, unit_ref):
        half_wait(k, half)
        for i in range(HALF // 16):
            rows = pl.ds(half * HALF + i * 16, 16)
            v = base[rows, :].astype(f32) + (exchanged(k, rows) + out_bias[k : k + 1, :])
            norm, unit, inv = normalize(v, k)
            r.norm[rows, :] = norm
            unit_ref[rows, :] = unit
            r.inv[k, rows, :] = jnp.broadcast_to(inv, (16, 128))
            low[rows, :] = norm.astype(bf16)

    def first_norm(half):
        norm_rows(0, half, r.tokens_v, r.unit0)

    probs_ref = r.probs
    dp_ref = r.dp
    low_probs = r.low_probs
    mem_row = lax.broadcasted_iota(jnp.int32, (CH, 2 * T), 0)
    chunks = ML // CH

    def fold(x, op):
        total = x[0:8]
        for i in range(1, x.shape[0] // 8):
            total = op(total, x[8 * i : 8 * i + 8])
        return total

    def cross_quad(half, g):
        cols, rows_q, index = pl.ds(g * 256, 256), pl.ds(half * HALF, HALF), half * (HL // 256) + g
        q = stacked_quad(r.query[rows_q, cols])
        top = jnp.full((8, 2 * T), -1e30, f32)
        for b in range(ML // BIG):
            scores = nt(key[pl.ds(b * BIG, BIG), cols], q)
            for i in range(BIG // CH):
                first = b * BIG + i * CH
                s = scores[i * CH : (i + 1) * CH] * (scale * LOG2E)
                s = jnp.where(mem_row < r.mem_len_v[0] - first, s, -1e30)
                probs_ref[index, pl.ds(first, CH), :] = s
                top = jnp.maximum(top, fold(s, jnp.maximum))
        top = jnp.max(top, axis=0, keepdims=True)
        total = jnp.zeros((8, 2 * T), f32)
        for i in range(chunks):
            rows = at(i, CH)
            w = jnp.exp2(probs_ref[index, rows, :] - top)
            probs_ref[index, rows, :] = w
            low_probs[rows, cols] = w.astype(bf16)
            total = total + fold(w, jnp.add)
        part = 1.0 / jnp.sum(total, axis=0, keepdims=True)
        r.part[index] = jnp.broadcast_to(part, (8, 2 * T))
        mixed = nn(turned[cols, :], low_probs[:, cols]) * part
        ycat[CROSS_OUT, rows_q, cols] = unstacked_quad(mixed).astype(bf16)

    def cross_attention(half):
        if half == 0:
            load(r.cross_q).wait()
        rows = pl.ds(half * HALF, HALF)
        for j in range(HL // 256):
            cols = pl.ds(j * 256, 256)
            x = nn(low[rows, :], r.cross_q_v[:, cols]) + r.cross_qv_bias_v[0:1, cols]
            r.query[rows, cols] = x.astype(bf16)
        for g in range(HL // 256):
            cross_quad(half, g)

    def send_second(half):
        if half == 0:
            load(r.cross_out).wait()
        exchange_half(1, half, lambda rows, cols: nn(ycat[CROSS_OUT, rows, :], r.cross_out_v[:, cols]))
        if half == 1:
            copy_y(CROSS_OUT).start()

    def second_norm(half):
        norm_rows(1, half, r.norm, r.unit1)

    def normal_share(h):
        return 0.5 * (1.0 + lax.erf(h * 0.7071067811865476))

    def hidden_units(half):
        if half == 0:
            load(r.fc_in).wait()
        rows = pl.ds(half * HALF, HALF)

        def unit(b):
            for part in range(2):
                j = 2 * b + part
                cols = at(j, 256)
                h = nn(low[rows, :], r.fc_in_v[:, cols]) + r.fc_in_bias_v[:, cols]
                dp_ref[1, pl.ds(j * T + half * HALF, HALF), :] = h
                ycat[FC_OUT + b, rows, pl.ds(part * 256, 256)] = (h * normal_share(h)).astype(bf16)
            copy_y_half(FC_OUT + b, half).start()

        for b in range(FL // W):
            unit(b)

    def slopes(j):
        h = dp_ref[1, at(j, T), :]
        dp_ref[1, at(j, T), :] = normal_share(h) + h * jnp.exp(-0.5 * h * h) * 0.3989422804014327

    def ffn_term(rows, cols):
        total = nn(ycat[FC_OUT, rows, :], r.fc_out_v[pl.ds(0, W), cols])
        for b in range(1, FL // W):
            total = total + nn(ycat[FC_OUT + b, rows, :], r.fc_out_v[pl.ds(b * W, W), cols])
        return total

    def send_third(half):
        if half == 0:
            load(r.fc_out).wait()
        exchange_half(2, half, ffn_term)

    row16 = lax.broadcasted_iota(jnp.int32, (16, D), 0)
    zero8 = jnp.zeros((8, D), f32)

    def sums_of(body, k):
        def step(i, carry):
            g, unit, rounded = body(i)
            return (
                carry[0] + fold(rounded, jnp.add),
                carry[1] + fold(g * unit, jnp.add),
                carry[2] + fold(g, jnp.add),
            )

        carry = (zero8, zero8, zero8)
        for i in range(T // 16):
            carry = step(i, carry)
        bias, gains, shifts = carry
        sm[k : k + 1, :] = col_sum(bias)
        sm[3 + k : 4 + k, :] = col_sum(gains)
        sm[6 + k : 7 + k, :] = col_sum(shifts)

    def output_rows(i):
        if i % (HALF // 16) == 0:
            half_wait(2, i // (HALF // 16))
        rows = at(i, 16)
        v = r.norm[rows, :] + (exchanged(2, rows) + out_bias[2:3, :])
        norm, unit, inv = normalize(v, 2)
        r.layer_out[rows, :] = norm.astype(bf16)
        g = jnp.where(row16 + i * 16 < r.dec_len_v[0], r.cotangent_v[rows, :].astype(f32), 0.0)
        grad = norm_back(g, unit, inv, 2)
        r.grad[rows, :] = grad
        rounded = grad.astype(bf16)
        low[rows, :] = rounded
        return g, unit, rounded.astype(f32)

    def output_norm():
        load(r.cotangent).wait()
        sums_of(output_rows, 2)

    def hidden_grad(j):
        cols = at(j, 256)
        g = nt(low[...], r.fc_out_v[at(j, 256), :]) * dp_ref[1, at(j, T), :]
        rounded = g.astype(bf16)
        ycat[FC_IN + j // 2, 0:T, at(j % 2, 256)] = rounded
        sm[pl.ds(11 + j // 4, 1), at(j % 4, 256)] = col_sum(rounded.astype(f32))

    def hidden_grads():
        for b in range(FL // W):
            hidden_grad(2 * b)
            hidden_grad(2 * b + 1)
            copy_y(FC_IN + b).start()

    def hidden_term(j):
        rows = at(j, 256)
        total = nt(ycat[FC_IN, 0:T, :], r.fc_in_v[rows, pl.ds(0, W)])
        for b in range(1, FL // W):
            total = total + nt(ycat[FC_IN + b, 0:T, :], r.fc_in_v[rows, pl.ds(b * W, W)])
        return total

    def send_fourth():
        exchange_start(3, hidden_term)

    def grad_rows(k, e, unit_ref):
        def body(i):
            rows = at(i, 16)
            g = r.grad[rows, :] + exchanged(e, rows)
            unit = unit_ref[rows, :]
            grad = norm_back(g, unit, r.inv[k, rows, 0:1], k)
            r.grad[rows, :] = grad
            rounded = grad.astype(bf16)
            low[rows, :] = rounded
            return g, unit, rounded.astype(f32)

        exchange_wait(e)
        sums_of(body, k)

    mixed_grad = r.mixed_grad

    def second_back():
        grad_rows(1, 3, r.unit1)

    def mixed_from(weights):
        for j in range(HL // 256):
            mixed_grad[:, at(j, 256)] = nt(low[...], weights[at(j, 256), :]).astype(bf16)

    def cross_mixed_grad():
        mixed_from(r.cross_out_v)

    def cross_back(g):
        cols = pl.ds(g * 256, 256)
        halves = [pl.ds(half * HALF, HALF) for half in range(2)]
        index = [half * (HL // 256) + g for half in range(2)]
        gs = [stacked_quad(mixed_grad[rows, cols]) for rows in halves]
        part = [r.part[i, 0:1, :] for i in index]
        total = [jnp.zeros((8, 2 * T), f32)] * 2
        both = jnp.concatenate(gs, axis=0)
        lanes = [pl.ds(half * 2 * T, 2 * T) for half in range(2)]
        for b in range(ML // BIG):
            big = pl.ds(b * BIG, BIG)
            for half in range(2):
                dbig = nt(value[big, cols], gs[half])
                for i in range(BIG // CH):
                    rows = pl.ds(b * BIG + i * CH, CH)
                    probs = probs_ref[index[half], rows, :] * part[half]
                    dprobs = dbig[i * CH : (i + 1) * CH]
                    dp_ref[half, rows, :] = dprobs
                    probs_ref[index[half], rows, :] = probs
                    total[half] = total[half] + fold(probs * dprobs, jnp.add)
                    low_probs[rows, lanes[half]] = probs.astype(bf16)
            value[big, cols] = nn(low_probs[big, :], both).astype(bf16)
        total = [jnp.sum(x, axis=0, keepdims=True) for x in total]
        both = jnp.concatenate([stacked_quad(r.query[rows, cols]) for rows in halves], axis=0)
        for b in range(ML // BIG):
            big = pl.ds(b * BIG, BIG)
            for half in range(2):
                for i in range(BIG // CH):
                    rows = pl.ds(b * BIG + i * CH, CH)
                    ds = probs_ref[index[half], rows, :] * (dp_ref[half, rows, :] - total[half])
                    low_probs[rows, lanes[half]] = ds.astype(bf16)
            key[big, cols] = (nn(low_probs[big, :], both) * scale).astype(bf16)
        for half in range(2):
            dq = nn(turned[cols, :], low_probs[:, lanes[half]])
            ycat[CROSS_Q, halves[half], cols] = (unstacked_quad(dq) * scale).astype(bf16)

    def send_fifth():
        exchange_start(4, lambda j: nt(ycat[CROSS_Q, 0:T, :], r.cross_q_v[at(j, 256), :]))
        copy_y(CROSS_Q).start()
        sm[10:11, 0:HL] = col_sum(ycat[CROSS_Q, 0:T, :].astype(f32))
        sm[10:11, HL : 2 * HL] = col_sum(value[...].astype(f32))

    def gm_copy(i):
        cols = at(i, 256)
        return remote("gm", i, 4, r.gm_out.at[:, cols], r.gm_in.at[:, cols], to_mp)

    def memory_term(i):
        cols = pl.ds(i * 256, 256)
        for half, to in ((1 - m, r.gm_out), (m, r.grad_memory)):
            rows = at(half, ML // 2)
            x = nt(key[rows, :], r.wkv_v[0, cols, :]) + nt(value[rows, :], r.wkv_v[1, cols, :])
            to[:, cols] = x.astype(bf16)
        gm_copy(i).start()

    def memory_sum(i):
        gm_copy(i).wait()
        cols = pl.ds(i * 256, 256)
        r.grad_memory[:, cols] = (r.grad_memory[:, cols].astype(f32) + r.gm_in[:, cols].astype(f32)).astype(bf16)

    def pair_product(v):
        pair = key if v == 0 else value
        for h in range(2):
            cols = pl.ds(h * 256, 256)
            rhs = pair[:, cols]
            r.kvc_out[v, :, cols] = nn(r.memory_t[at(1 - c, D // 2), :], rhs).astype(bf16)
            r.memory_v[0 : D // 2, pl.ds(v * W + h * 256, 256)] = nn(r.memory_t[at(c, D // 2), :], rhs).astype(bf16)
        kvc_copy(v).start()

    def pair_halve(v):
        kvc_copy(v).wait_recv()
        rows = at(1 - y, 256)
        mine = r.memory_v[rows, pl.ds(v * W, W)].astype(f32)
        r.kvy_out[v] = (mine + r.kvc_in[v, rows, :].astype(f32)).astype(bf16)
        kvy_copy(v).start()

    def first_back():
        grad_rows(0, 4, r.unit0)

    def self_back(p):
        cols = at(p, 128)
        q, k, v = (r.packed[i, :, cols] for i in range(3))
        probs = r.self_probs[p]
        g = stacked(mixed_grad[:, cols])
        dprobs = nt(v, g)
        ycat[QKV + 2, 0:T, cols] = nn(probs.astype(bf16), g).astype(bf16)
        ds = (probs * (dprobs - jnp.sum(probs * dprobs, axis=0, keepdims=True))).astype(bf16)
        ycat[QKV + 1, 0:T, cols] = (nn(ds, stacked(q)) * scale).astype(bf16)
        dq = nn(k.astype(f32).T.astype(bf16), ds)
        ycat[QKV, 0:T, cols] = (unstacked(dq) * scale).astype(bf16)

    def self_grads():
        mixed_from(r.self_out_v)
        loop(PAIRS, self_back, 4)
        for b in range(3):
            copy_y(QKV + b).start()
        sm[9:10, 0:HL] = col_sum(ycat[QKV, 0:T, :].astype(f32))
        sm[9:10, HL : 2 * HL] = col_sum(ycat[QKV + 2, 0:T, :].astype(f32))
        sm[13:16, :] = jnp.zeros((3, D), f32)

    def packed_term(j):
        rows = at(j, 256)
        total = nt(ycat[QKV, 0:T, :], r.wqkv_v[0, rows, :])
        for b in range(1, 3):
            total = total + nt(ycat[QKV + b, 0:T, :], r.wqkv_v[b, rows, :])
        return total

    def send_sixth():
        exchange_start(5, packed_term)

    def token_grads():
        def body(i):
            rows = at(i, 16)
            r.grad_tokens[rows, :] = (r.grad[rows, :] + exchanged(5, rows)).astype(bf16)

        exchange_wait(5)
        loop(T // 16, body, 2)

    doubling = (to_c, to_y, to_z1, to_z2)

    def small_copy(k):
        return remote("small", k, 4, r.sm_out.at[k], r.sm_in.at[k], doubling[k])

    def small_step(k):
        if k > 0:
            small_copy(k - 1).wait()
            (sm if k < 4 else r.sums)[...] = r.sm_out[k - 1].astype(f32) + r.sm_in[k - 1].astype(f32)
        if k < 4:
            r.sm_out[k] = sm[...].astype(bf16)
            small_copy(k).start()

    def each(step, *indices):
        for i in indices:
            step(i)

    project()
    self_attention()
    send_first()
    memory_pair()
    first_norm(0)
    cross_attention(0)
    send_second(0)
    each(turn_memory, 0)
    first_norm(1)
    cross_attention(1)
    send_second(1)
    send_x(X_FIRST, low)
    second_norm(0)
    hidden_units(0)
    send_third(0)
    second_norm(1)
    hidden_units(1)
    send_third(1)
    turn(key)
    each(slopes, 7)
    send_x(X_SECOND, low)
    each(turn_memory, 7)
    each(slopes, 3)
    each(turn_memory, 3)
    each(slopes, 4, 0, 6, 5, 2, 1)
    output_norm()
    hidden_grads()
    send_x(X_FFN, low)
    send_fourth()
    each(product, 4)
    send_x(X_TOKENS, r.tokens_v)
    share_x(X_FFN)
    each(halve, 4)
    each(product, 5)
    second_back()
    cross_mixed_grad()
    send_x(X_CROSS, low)
    each(product, 2)
    each(turn_memory, 6)
    each(halve, 5)
    each(cross_back, 0)
    each(product, 7)
    each(halve_last, 4)
    each(halve, 2)
    each(cross_back, 1)
    send_fifth()
    each(halve, 7)
    each(product, 6, 3, 1)
    share_x(X_CROSS)
    each(halve_last, 5)
    each(halve, 3)
    each(halve_last, 2)
    each(turn_memory, 4)
    each(halve, 6)
    each(product, 0)
    each(memory_term, 3)
    each(halve, 1)
    each(turn_memory, 2)
    first_back()
    self_grads()
    each(halve_last, 7)
    each(total, 5)
    each(halve, 0)
    each(small_step, 0)
    each(product, 9)
    each(halve_last, 3)
    each(turn_memory, 5)
    each(product, 8)
    each(memory_term, 2)
    send_x(X_SELF, low)
    each(halve, 9)
    each(small_step, 1)
    each(product, 11)
    each(turn_memory, 1)
    each(halve_last, 1, 6)
    each(memory_sum, 2)
    each(total, 3)
    each(halve, 11)
    each(total, 4)
    each(pair_product, 1, 0)
    each(product, 12)
    each(halve_last, 9)
    share_x(X_SELF)
    each(memory_term, 1)
    each(product, 13)
    each(halve, 8)
    each(halve_last, 0)
    each(pair_halve, 1)
    each(halve, 12, 13)
    send_sixth()
    each(small_step, 2)
    each(pair_halve, 0)
    each(product, 10)
    each(halve_last, 8, 11)
    each(total, 2, 1, 6)
    each(halve, 10, 15)
    token_grads()
    each(memory_term, 0)
    each(halve_last, 13, 12)
    each(total, 7)
    each(halve, 14)
    each(halve_last, 10)
    each(total, 8)
    each(small_step, 3)
    each(halve_last, 15)
    each(memory_sum, 1)
    each(total, 10, 13, 9)
    each(halve_last, 14)
    each(memory_sum, 0)
    each(total, 15, 11)
    each(small_step, 4)
    each(total, 12, 0)
    each(memory_sum, 3)
    each(total, 14)
    for w in range(6):
        copy_x(w).wait_send()
        if x_axis(w) == AXIS_Z:
            copy_shared(w, m).wait_send()
    for u in range(UNITS):
        if u < KV:
            for copy in gathers(u):
                copy.wait_send()
            copy_core(u).wait_send()
        copy_half(u).wait_send()
        copy_last(u).wait_send()
    for v in range(2):
        kvc_copy(v).wait_send()
        kvy_copy(v).wait_send()
    refs_at.update(remote=sum(n for _, n in given.values()), local=sum(n for _, n in local_given.values()))


REMOTE_SEMS = 160
LAYER_VMEM = 59 * 2**20
LOCAL_SEMS = 64


def layer(tokens, memory, mem_len, dec_len, cotangent, wqkv, self_qv_bias, self_out, cross_q, cross_kv, cross_qv_bias, cross_out, fc_in, fc_in_bias, fc_out, out_bias, norm_gain, norm_bias):
    T, D = tokens.shape
    ML = memory.shape[0]
    HL = self_out.shape[0]
    FL = fc_out.shape[0]
    R = D // GROUP
    W = 512
    PAIRS = HL // 128
    anywhere = pl.BlockSpec(memory_space=pl.ANY)
    big = dict(tokens=tokens, memory=memory, cotangent=cotangent, wqkv=wqkv, self_out=self_out, cross_q=cross_q, cross_kv=cross_kv,
               cross_out=cross_out, fc_in=fc_in, fc_out=fc_out)
    small = dict(self_qv_bias=self_qv_bias, cross_qv_bias=cross_qv_bias, fc_in_bias=fc_in_bias, out_bias=out_bias,
                 norm_gain=norm_gain, norm_bias=norm_bias)
    scalars = dict(mem_len=mem_len, dec_len=dec_len)
    outs = dict(
        layer_out=((T, D), bf16),
        grad_tokens=((T, D), bf16),
        grad_memory=((ML // 2, D), bf16),
        g_qkv=((3, R, HL), f32),
        g_self_out=((R, HL), f32),
        g_cross_q=((R, HL), f32),
        g_kv=((2, R, HL), f32),
        g_cross_out=((R, HL), f32),
        g_fc_in=((R, FL), f32),
        g_fc_out=((R, FL), f32),
        sums=((16, D), f32),
    )
    scratch = {name + "_v": (x.shape, x.dtype) for name, x in (big | small).items()}
    scratch |= dict(
        wkv_v=((2, D, HL), bf16),
        packed=((3, T, HL), bf16),
        self_probs=((PAIRS, T, 2 * T), f32),
        low=((T, D), bf16),
        ycat=((KV, 2 * T, W), bf16),
        xcat=((6, 512, 256), bf16),
        xsend=((6, 512, 128), bf16),
        ex_out=((2, T, D), bf16),
        ex_in=((2, T, D), bf16),
        norm=((T, D), f32),
        unit0=((T, D), f32),
        unit1=((T, D), f32),
        inv=((2, T, 128), f32),
        grad=((T, D), f32),
        key=((ML, HL), bf16),
        value=((ML, HL), bf16),
        turned=((HL, ML), bf16),
        query=((T, HL), bf16),
        mixed_grad=((T, HL), bf16),
        probs=((PAIRS, ML, 2 * T), f32),
        part=((PAIRS, 8, 2 * T), f32),
        low_probs=((ML, 4 * T), bf16),
        dp=((2, ML, 2 * T), f32),
        memory_t=((D, ML), bf16),
        gm_out=((ML // 2, D), bf16),
        gm_in=((ML // 2, D), bf16),
        core_in=((KV, 256, W), bf16),
        kvc_out=((2, 512, W), bf16),
        kvc_in=((2, 512, W), bf16),
        kvy_out=((2, 256, W), bf16),
        kvy_in=((2, 256, W), bf16),
        half_out=((UNITS, 128, W), bf16),
        half_in=((UNITS, 128, W), bf16),
        last_out=((UNITS, 64, W), bf16),
        last_in=((UNITS, 64, W), bf16),
        sm=((16, D), f32),
        sm_out=((4, 16, D), bf16),
        sm_in=((4, 16, D), bf16),
    )
    sems = dict(send_sem=REMOTE_SEMS, recv_sem=REMOTE_SEMS, local_sem=LOCAL_SEMS)
    lengths = {name + "_v": pltpu.SMEM((1,), jnp.int32) for name in scalars}
    names = [*big, *small, *scalars, *outs, *scratch, *lengths, *sems]
    got = {}
    out = pl.pallas_call(
        functools.partial(kernel, names, got),
        out_shape=[pltpu.VMEM(s, t) for s, t in outs.values()],
        in_specs=[anywhere] * (len(big) + len(small) + len(scalars)),
        out_specs=[pl.BlockSpec(memory_space=pltpu.VMEM)] * len(outs),
        scratch_shapes=[pltpu.VMEM(s, t) for s, t in scratch.values()]
        + [*lengths.values()]
        + [pltpu.SemaphoreType.DMA((count,)) for count in sems.values()],
        compiler_params=pltpu.CompilerParams(
            collective_id=0, has_side_effects=True, vmem_limit_bytes=LAYER_VMEM
        ),
        name="layer",
    )(*big.values(), *small.values(), *scalars.values())
    assert got["remote"] <= REMOTE_SEMS and got["local"] <= LOCAL_SEMS, got
    return types.SimpleNamespace(**dict(zip(outs, out)))


def finish_kernel(count, small, *refs):
    ins, outs, scratch = refs[: count + 2], refs[count + 2 : 2 * count + 3 + small], refs[2 * count + 3 + small :]
    turned, made, sem = scratch[0], scratch[1:-1], scratch[-1]
    stores = [
        pltpu.make_async_copy(a, b, sem.at[i]) for i, (a, b) in enumerate(zip((*ins[:count], turned, *made), outs))
    ]
    for i in range(count):
        stores[i].start()
    kv, sums = ins[count:]
    for part in range(2):
        turned[:, part, :] = kv[part]
    stores[count].start()
    self_bias, cross_bias, hidden_bias, out_bias, gains, shifts = made
    width = self_bias.shape[1]
    for row, to in ((9, self_bias), (10, cross_bias)):
        for part in range(2):
            to[part : part + 1, :] = sums[row : row + 1, part * width : (part + 1) * width]
    features = sums.shape[1]
    for part in range(hidden_bias.shape[1] // features):
        hidden_bias[:, part * features : (part + 1) * features] = sums[11 + part : 12 + part, :]
    for first, to in ((0, out_bias), (3, gains), (6, shifts)):
        to[...] = sums[first : first + 3, :]
    for i in range(small):
        stores[count + 1 + i].start()
    for store in stores:
        store.wait()


def finish(whole, kv, sums):
    R, HL = kv.shape[1:]
    D = sums.shape[1]
    anywhere = pl.BlockSpec(memory_space=pl.ANY)
    in_vmem = pl.BlockSpec(memory_space=pltpu.VMEM)
    small = [(2, HL), (2, HL), (1, 4 * HL), (3, D), (3, D), (3, D)]
    return pl.pallas_call(
        functools.partial(finish_kernel, len(whole), len(small)),
        out_shape=[jax.ShapeDtypeStruct(x.shape, x.dtype) for x in whole]
        + [jax.ShapeDtypeStruct((R, 2, HL), f32)]
        + [jax.ShapeDtypeStruct(shape, f32) for shape in small],
        in_specs=[in_vmem] * (len(whole) + 2),
        out_specs=[anywhere] * (len(whole) + 1 + len(small)),
        scratch_shapes=[pltpu.VMEM(shape, f32) for shape in [(R, 2, HL), *small]]
        + [pltpu.SemaphoreType.DMA((len(whole) + 1 + len(small),))],
        compiler_params=pltpu.CompilerParams(vmem_limit_bytes=8 * 2**20),
        name="finish",
    )(*whole, kv, sums)


def per_device(tokens, memory, mem_len, dec_len, cotangent, self_qkv, self_qv_bias, self_out, cross_q, cross_kv, cross_qv_bias, cross_out, fc_in, fc_in_bias, fc_out, out_bias, norm_gain, norm_bias):
    D = tokens.shape[1]
    devices = lax.axis_size("dp")
    outer = devices // GROUP

    def regroup(x, axis, there):
        if outer == 1:
            return x
        sizes = (outer, GROUP) if there else (GROUP, outer)
        shape = x.shape
        x = x.reshape(shape[:axis] + sizes + (D // devices,) + shape[axis + 1 :])
        return jnp.swapaxes(x, axis, axis + 1).reshape(shape)

    tokens, memory, cotangent, self_out, cross_out, fc_out, out_bias, norm_gain, norm_bias = (
        regroup(x, 1, True)
        for x in (tokens, memory, cotangent, self_out, cross_out, fc_out, out_bias, norm_gain, norm_bias)
    )
    self_qkv, cross_q, cross_kv, fc_in = (regroup(x, 0, True) for x in (self_qkv, cross_q, cross_kv, fc_in))
    got = layer(
        tokens, memory, mem_len, dec_len, cotangent, self_qkv.transpose(1, 0, 2), self_qv_bias, self_out, cross_q,
        cross_kv, cross_qv_bias, cross_out, fc_in, fc_in_bias.reshape(1, -1), fc_out, out_bias,
        norm_gain, norm_bias,
    )
    groups = [[o * GROUP + i for o in range(outer)] for i in range(GROUP)]

    def spread(x, axis):
        if outer == 1:
            return x
        return lax.psum_scatter(x, "dp", scatter_dimension=axis, axis_index_groups=groups, tiled=True)

    (
        layer_out, grad_tokens, grad_memory, qkv, self_out, cross_q, cross_out, fc_in, fc_out, kv,
        self_bias, cross_bias, hidden_bias, out_bias, gains, shifts,
    ) = finish(
        (
            got.layer_out, got.grad_tokens, got.grad_memory, got.g_qkv, got.g_self_out, got.g_cross_q, got.g_cross_out,
            got.g_fc_in, got.g_fc_out,
        ),
        got.g_kv,
        got.sums,
    )
    small = (self_bias, cross_bias, hidden_bias, out_bias, gains, shifts)
    if outer > 1:
        small = lax.psum(small, "dp", axis_index_groups=groups)
    self_bias, cross_bias, hidden_bias, out_bias, gains, shifts = small
    return (
        regroup(layer_out, 1, False),
        regroup(grad_tokens, 1, False),
        regroup(grad_memory, 1, False),
        spread(qkv, 1).transpose(1, 0, 2),
        self_bias,
        spread(self_out, 0).T,
        spread(cross_q, 0),
        spread(kv, 0),
        cross_bias,
        spread(cross_out, 0).T,
        spread(fc_in, 0),
        hidden_bias.reshape(-1),
        spread(fc_out, 0).T,
        regroup(out_bias, 1, False),
        regroup(gains, 1, False),
        regroup(shifts, 1, False),
    )


def solution(mesh):
    placed = (
        P("dp", None),
        P("dp", None),
        P("dp"),
        P("dp"),
        P("dp", None),
        P(None, None, "mp"),
        P(None, "mp"),
        P("mp", None),
        P(None, "mp"),
        P(None, None, "mp"),
        P(None, "mp"),
        P("mp", None),
        P(None, "mp"),
        P("mp"),
        P("mp", None),
        P(),
        P(),
        P(),
    )
    return jax.shard_map(
        per_device,
        mesh=mesh,
        in_specs=placed,
        out_specs=(
            P("dp", None),
            P("dp", None),
            P(("dp", "mp"), None),
            P("dp", None, "mp"),
            P(None, "mp"),
            P("mp", "dp"),
            P("dp", "mp"),
            P("dp", None, "mp"),
            P(None, "mp"),
            P("mp", "dp"),
            P("dp", "mp"),
            P("mp"),
            P("mp", "dp"),
            P(),
            P(),
            P(),
        ),
        check_vma=False,
    )
```

```python
import functools
import types

import jax
import jax.numpy as jnp
from jax import lax
from jax.experimental import pallas as pl
from jax.experimental.pallas import tpu as pltpu
from jax.sharding import PartitionSpec as P

HEAD = 64
LOG2E = 1.4426950408889634
GROUP = 16
epsilon = 1e-05
MESH = pl.DeviceIdType.MESH
f32, bf16 = jnp.float32, jnp.bfloat16

FC_OUT, FC_IN, CROSS_OUT, CROSS_Q, SELF_OUT, QKV, KV = 0, 4, 8, 9, 10, 11, 14
UNITS = 16
X_TOKENS, X_FIRST, X_SECOND, X_FFN, X_CROSS, X_SELF = range(6)


AXIS_Y, AXIS_Z = 0, 1


def axis_of(unit):
    return AXIS_Z if unit < FC_IN or unit in (CROSS_OUT, SELF_OUT) else AXIS_Y


def x_axis(x):
    return AXIS_Z if x in (X_FFN, X_CROSS, X_SELF) else AXIS_Y


def x_of(unit):
    return ((X_FFN,) * 4 + (X_SECOND,) * 4 + (X_CROSS, X_FIRST, X_SELF) + (X_TOKENS,) * 3)[unit]


def nn(a, b):
    return lax.dot_general(a, b, (((1,), (0,)), ((), ())), preferred_element_type=f32)


def nt(a, b):
    return lax.dot_general(a, b, (((1,), (1,)), ((), ())), preferred_element_type=f32)


def loop(count, body, unroll=1):
    def step(i, carry):
        for j in range(unroll):
            body(i * unroll + j)
        return carry

    if unroll == count:
        step(0, 0)
    else:
        lax.fori_loop(0, count // unroll, step, 0)


def at(index, size):
    return pl.ds(index * size if isinstance(index, int) else pl.multiple_of(index * size, size), size)


def kernel(names, refs_at, *refs):
    r = types.SimpleNamespace(**dict(zip(names, refs)))
    T, D = r.tokens.shape
    ML = r.memory.shape[0]
    HL = r.self_out.shape[0]
    FL = r.fc_out.shape[0]
    W = 512
    PAIRS = HL // 128
    CH = 128
    scale = HEAD**-0.5

    d, m = lax.axis_index("dp"), lax.axis_index("mp")
    c, y = lax.rem(d, 2), lax.rem(d // 2, 2)
    zl, zh = lax.rem(d // 4, 2), lax.rem(d // 8, 2)
    to_mp = (d, 1 - m)
    to_c = (d + 1 - 2 * c, m)
    to_y = (d + 2 - 4 * y, m)
    to_z1 = (d + 4 - 8 * zl, m)
    to_z2 = (d + 8 - 16 * zh, m)

    bits, partners_of = (y, zl), (to_y, to_z1)

    barrier = pltpu.get_barrier_semaphore()
    for partner in (to_mp, to_c, to_y, to_z1, to_z2):
        pl.semaphore_signal(barrier, inc=1, device_id=partner, device_id_type=MESH)

    given = {}
    local_given = {}

    def slot(key, count=1):
        if key not in given:
            given[key] = sum(n for _, n in given.values()), count
        return given[key][0]

    def remote(key, index, count, src, dst, partner):
        base = slot(key, count) + index
        return pltpu.make_async_remote_copy(
            src_ref=src,
            dst_ref=dst,
            send_sem=r.send_sem.at[base],
            recv_sem=r.recv_sem.at[base],
            device_id=partner,
            device_id_type=MESH,
        )

    def local(key, src, dst, index=0, count=1):
        if key not in local_given:
            local_given[key] = sum(n for _, n in local_given.values()), count
        return pltpu.make_async_copy(src, dst, r.local_sem.at[local_given[key][0] + index])

    def load(src):
        name = next(k for k, v in vars(r).items() if v is src)
        return local(name, src, getattr(r, name + "_v"))

    def load_qkv(part):
        return local("qkv", r.wqkv.at[part], r.wqkv_v.at[part], part, 3)

    first = (r.dec_len, r.mem_len, r.self_qv_bias, r.cross_qv_bias, r.fc_in_bias, r.out_bias, r.norm_gain, r.norm_bias)
    load(r.tokens).start()
    load_qkv(0).start()
    for src in first:
        load(src).start()
    load_qkv(1).start()
    load_qkv(2).start()
    for src in (r.self_out, r.memory, r.cross_kv, r.cross_q, r.cross_out, r.fc_in, r.fc_out, r.cotangent):
        load(src).start()

    gain, shift, out_bias = r.norm_gain_v, r.norm_bias_v, r.out_bias_v
    sm = r.sm
    ycat, xcat, xsend = r.ycat, r.xcat, r.xsend
    low = r.low
    lane_low = lax.broadcasted_iota(jnp.int32, (T, 128), 1) < HEAD

    def stacked(pair):
        wide = pair.astype(f32)
        return jnp.concatenate(
            [jnp.where(lane_low, wide, 0.0).astype(bf16), jnp.where(lane_low, 0.0, wide).astype(bf16)], axis=0
        )

    def unstacked(wide):
        return jnp.concatenate([wide[:HEAD, :T], wide[HEAD:, T:]], axis=0).T

    quad_lane = lax.broadcasted_iota(jnp.int32, (T // 2, 256), 1) // HEAD

    def stacked_quad(quad):
        wide = quad.astype(f32)
        return jnp.concatenate([jnp.where(quad_lane == h, wide, 0.0).astype(bf16) for h in range(4)], axis=0)

    def unstacked_quad(wide):
        parts = []
        for b in range(2):
            span = slice(b * 128, (b + 1) * 128)
            t = wide[span, span].T
            parts.append(jnp.where(lane_low[: T // 2], t[: T // 2], t[T // 2 :]))
        return jnp.concatenate(parts, axis=1)

    def col_sum(x):
        return jnp.sum(x, axis=0, keepdims=True)

    def send_x(w, src):
        g = x_axis(w)

        def block(q):
            high, o = q // 2, lax.rem(q, 2)
            row = o * 128 + high * 64
            for own in (True, False):
                side = bits[g] if own else 1 - bits[g]
                from_block = high * 4 + (o * 2 + side if g == AXIS_Y else side * 2 + o)
                t = src[:, at(from_block, 128)].astype(f32).T.astype(bf16)
                for half in range(2):
                    rows = pl.ds(pl.multiple_of(half * 256 + row, 64), 64)
                    piece = t[half * 64 : (half + 1) * 64]
                    if own:
                        xcat[w, rows, 0:128] = piece
                    else:
                        xsend[w, rows, :] = piece

        loop(4, block, 2)
        copy_x(w).start()

    def copy_x(w):
        rows = pl.ds(0, 512) if x_axis(w) == AXIS_Y else at(m, 256)
        return remote(
            ("x", w), 0, 1, xsend.at[w, rows, :], xcat.at[w, rows, pl.ds(128, 128)], partners_of[x_axis(w)]
        )

    def copy_shared(w, side):
        held = xcat.at[w, at(side, 256), pl.ds(128, 128)]
        return remote(("shared", w), 0, 1, held, held, to_mp)

    def share_x(w):
        copy_x(w).wait_recv()
        copy_shared(w, m).start()

    def copy_y_half(u, half):
        rows, there = pl.ds(half * (T // 2), T // 2), pl.ds(T + half * (T // 2), T // 2)
        return remote(("half", half), u, 4, ycat.at[u, rows, :], ycat.at[u, there, :], partners_of[axis_of(FC_OUT)])

    def gathers(u):
        return [copy_y_half(u, half) for half in range(2)] if u < FC_IN else [copy_y(u)]

    def copy_y(u):
        to = partners_of[axis_of(u)]
        return remote("gather", u, KV, ycat.at[u, pl.ds(0, T), :], ycat.at[u, pl.ds(T, T), :], to)

    HALF = T // 2

    def exchange_part(k, j):
        return (at(j // 2, HALF), at(j % 2, D // 2)) if k < 3 else (pl.ds(0, T), at(j, 256))

    def exchange_copy(k, j):
        rows, cols = exchange_part(k, j)
        return remote(
            ("ex", k), j, 4, r.ex_out.at[k % 2, rows, cols], r.ex_in.at[k % 2, rows, cols], to_mp
        )

    def exchange_half(k, half, term):
        for j in range(D // 256):
            cols = pl.ds(j * 256, 256)
            r.ex_out[k % 2, at(half, HALF), cols] = term(at(half, HALF), cols).astype(bf16)
            if j % 2:
                exchange_copy(k, 2 * half + j // 2).start()

    def half_wait(k, half):
        for j in range(2):
            exchange_copy(k, 2 * half + j).wait()

    def exchange_start(k, term):
        for j in range(D // 256):
            r.ex_out[k % 2, :, pl.ds(j * 256, 256)] = term(j).astype(bf16)
            exchange_copy(k, j).start()

    def exchange_wait(k):
        for j in range(4):
            exchange_copy(k, j).wait()

    def exchanged(k, rows):
        return r.ex_out[k % 2, rows, :].astype(f32) + r.ex_in[k % 2, rows, :].astype(f32)

    def kept(u):
        return r.fc_out_v.at[at(u % 8, 256), at(u // 8, W)]

    def core_out(u):
        return r.fc_in_v.at[at(u % 4, 256), at(u // 4, W)]

    def copy_core(u):
        return remote("core", u, KV, core_out(u), r.core_in.at[u], to_c)

    def copy_half(u):
        return remote("half", u, UNITS, r.half_out.at[u], r.half_in.at[u], partners_of[1 - axis_of(u)])

    def copy_last(u):
        return remote("last", u, UNITS, r.last_out.at[u], r.last_in.at[u], to_z2)

    def kvc_copy(v):
        return remote("kvc", v, 2, r.kvc_out.at[v], r.kvc_in.at[v], to_c)

    def kvy_copy(v):
        return remote("kvy", v, 2, r.kvy_out.at[v], r.kvy_in.at[v], to_y)

    arrived = set()

    def product(u):
        w = x_of(u)
        if w not in arrived:
            arrived.add(w)
            (copy_x(w) if x_axis(w) == AXIS_Y else copy_shared(w, 1 - m)).wait_recv()
        for copy in gathers(u):
            copy.wait_recv()
        for h in range(W // 256):
            cols = pl.ds(h * 256, 256)
            core_out(u)[:, cols] = nn(xcat[w, at(1 - c, 256), :], ycat[u, :, cols]).astype(bf16)
        copy_core(u).start()
        for h in range(W // 256):
            cols = pl.ds(h * 256, 256)
            kept(u)[:, cols] = nn(xcat[w, at(c, 256), :], ycat[u, :, cols]).astype(bf16)

    def local_sum(u, rows):
        if u < KV:
            return kept(u)[rows, :].astype(f32) + r.core_in[u, rows, :].astype(f32)
        v = u - KV
        wide = pl.ds(pl.multiple_of(y * 256 + rows.start, 64), rows.size)
        mine = r.memory_v[wide, pl.ds(v * W, W)].astype(f32) + r.kvc_in[v, wide, :].astype(f32)
        return mine + r.kvy_in[v, rows, :].astype(f32)

    def halve(u):
        if u < KV:
            copy_core(u).wait_recv()
        else:
            kvy_copy(u - KV).wait_recv()
        r.half_out[u] = local_sum(u, at(1 - bits[1 - axis_of(u)], 128)).astype(bf16)
        copy_half(u).start()

    def part_rows(u, high):
        return pl.ds(pl.multiple_of(bits[1 - axis_of(u)] * 128 + high * 64, 64), 64)

    def halve_last(u):
        copy_half(u).wait_recv()
        got = r.half_in[u, at(1 - zh, 64), :].astype(f32)
        r.last_out[u] = (local_sum(u, part_rows(u, 1 - zh)) + got).astype(bf16)
        copy_last(u).start()

    def total(u):
        copy_last(u).wait_recv()
        got = r.half_in[u, at(zh, 64), :].astype(f32) + r.last_in[u].astype(f32)
        x = local_sum(u, part_rows(u, zh)) + got
        if u < FC_IN:
            r.g_fc_out[:, at(u, W)] = x
        elif u < CROSS_OUT:
            r.g_fc_in[:, at(u - FC_IN, W)] = x
        elif u < QKV:
            (r.g_cross_out, r.g_cross_q, r.g_self_out)[u - CROSS_OUT][...] = x
        elif u < KV:
            r.g_qkv[u - QKV] = x
        else:
            r.g_kv[u - KV] = x

    def project():
        load(r.tokens).wait()
        for part in range(3):
            load_qkv(part).wait()
            if part == 0:
                for src in first:
                    load(src).wait()

            def packed(j, part=part):
                cols = at(j, 256)
                x = nn(r.tokens_v[...], r.wqkv_v[part, :, cols])
                if part == 0:
                    x = x + r.self_qv_bias_v[0:1, cols]
                if part == 2:
                    x = x + r.self_qv_bias_v[1:2, cols]
                r.packed[part, :, cols] = x.astype(bf16)

            loop(HL // 256, packed, 2)

    key_row = lax.broadcasted_iota(jnp.int32, (T, 2 * T), 0)
    query_row = lax.rem(lax.broadcasted_iota(jnp.int32, (T, 2 * T), 1), T)

    def self_pair(p):
        cols = at(p, 128)
        q, k, v = (r.packed[i, :, cols] for i in range(3))
        s = nt(k, stacked(q)) * scale
        s = jnp.where((key_row <= query_row) & (key_row < r.dec_len_v[0]), s, -1e30)
        w = jnp.exp(s - jnp.max(s, axis=0, keepdims=True))
        probs = w / jnp.sum(w, axis=0, keepdims=True)
        r.self_probs[p] = probs
        mixed = nn(v.astype(f32).T.astype(bf16), probs.astype(bf16))
        ycat[SELF_OUT, 0:T, cols] = unstacked(mixed).astype(bf16)

    def self_attention():
        loop(PAIRS, self_pair, 4)

    def send_first():
        load(r.self_out).wait()
        pl.semaphore_wait(barrier, 5)
        for half in range(2):
            exchange_half(0, half, lambda rows, cols: nn(ycat[SELF_OUT, rows, :], r.self_out_v[:, cols]))
        copy_y(SELF_OUT).start()
        load(r.memory).wait()

    key, value, turned = r.key, r.value, r.turned
    odd = lax.broadcasted_iota(jnp.int32, (256, 256), 0)
    odd = jnp.where(odd < 128, 2 * odd, 2 * odd - 255)
    select = (lax.broadcasted_iota(jnp.int32, (256, 256), 1) == odd).astype(f32).astype(bf16)

    def part_weights(i):
        rows = at(i, CH)
        x = nn(select, r.cross_kv_v[rows].reshape(2 * CH, HL)).astype(bf16)
        r.wkv_v[0, rows, :] = x[:CH]
        r.wkv_v[1, rows, :] = x[CH:]

    BIG = 512

    def pair_rows(i):
        rows = at(i, BIG)
        for j in range(HL // 256):
            cols = pl.ds(j * 256, 256)
            key[rows, cols] = nn(r.memory_v[rows, :], r.wkv_v[0, :, cols]).astype(bf16)
            x = nn(r.memory_v[rows, :], r.wkv_v[1, :, cols]) + r.cross_qv_bias_v[1:2, cols]
            value[rows, cols] = x.astype(bf16)
            for b in range(BIG // 128):
                for h in range(2):
                    block = x[b * 128 : (b + 1) * 128, h * 128 : (h + 1) * 128].T
                    turned[pl.ds(j * 256 + h * 128, 128), pl.ds(pl.multiple_of(i * BIG + b * 128, 128), 128)] = block.astype(bf16)

    def turn(src):
        def step(i):
            rows = at(i, CH)
            for j in range(HL // 128):
                turned[pl.ds(j * 128, 128), rows] = src[rows, pl.ds(j * 128, 128)].astype(f32).T.astype(bf16)

        loop(ML // CH, step, 2)

    def memory_pair():
        load(r.cross_kv).wait()
        loop(D // CH, part_weights, 2)
        loop(ML // BIG, pair_rows)

    def turn_memory(i):
        rows = at(i, CH)

        def block(b):
            t = r.memory_v[rows, at(b, 128)].astype(f32).T.astype(bf16)
            side, zlow, zhigh = lax.rem(b, 2), lax.rem(b // 2, 2), b // 4
            for half in range(2):
                to = half * 512 + side * 256 + zlow * 128 + zhigh * 64
                r.memory_t[pl.ds(pl.multiple_of(to, 64), 64), rows] = t[half * 64 : (half + 1) * 64]

        loop(D // 128, block, 4)

    def normalize(v, k):
        mean = jnp.mean(v, axis=-1, keepdims=True)
        centred = v - mean
        inv = lax.rsqrt(jnp.mean(centred * centred, axis=-1, keepdims=True) + epsilon)
        unit = centred * inv
        return unit * gain[k : k + 1, :] + shift[k : k + 1, :], unit, inv

    def norm_back(g, unit, inv, k):
        w = g * gain[k : k + 1, :]
        return inv * (w - jnp.mean(w, axis=-1, keepdims=True) - unit * jnp.mean(w * unit, axis=-1, keepdims=True))

    def norm_rows(k, half, base, unit_ref):
        half_wait(k, half)
        for i in range(HALF // 16):
            rows = pl.ds(half * HALF + i * 16, 16)
            v = base[rows, :].astype(f32) + (exchanged(k, rows) + out_bias[k : k + 1, :])
            norm, unit, inv = normalize(v, k)
            r.norm[rows, :] = norm
            unit_ref[rows, :] = unit
            r.inv[k, rows, :] = jnp.broadcast_to(inv, (16, 128))
            low[rows, :] = norm.astype(bf16)

    def first_norm(half):
        norm_rows(0, half, r.tokens_v, r.unit0)

    probs_ref = r.probs
    dp_ref = r.dp
    low_probs = r.low_probs
    mem_row = lax.broadcasted_iota(jnp.int32, (CH, 2 * T), 0)
    chunks = ML // CH

    def fold(x, op):
        total = x[0:8]
        for i in range(1, x.shape[0] // 8):
            total = op(total, x[8 * i : 8 * i + 8])
        return total

    def cross_quad(half, g):
        cols, rows_q, index = pl.ds(g * 256, 256), pl.ds(half * HALF, HALF), half * (HL // 256) + g
        q = stacked_quad(r.query[rows_q, cols])
        top = jnp.full((8, 2 * T), -1e30, f32)
        for b in range(ML // BIG):
            scores = nt(key[pl.ds(b * BIG, BIG), cols], q)
            for i in range(BIG // CH):
                first = b * BIG + i * CH
                s = scores[i * CH : (i + 1) * CH] * (scale * LOG2E)
                s = jnp.where(mem_row < r.mem_len_v[0] - first, s, -1e30)
                probs_ref[index, pl.ds(first, CH), :] = s
                top = jnp.maximum(top, fold(s, jnp.maximum))
        top = jnp.max(top, axis=0, keepdims=True)
        total = jnp.zeros((8, 2 * T), f32)
        for i in range(chunks):
            rows = at(i, CH)
            w = jnp.exp2(probs_ref[index, rows, :] - top)
            probs_ref[index, rows, :] = w
            low_probs[rows, cols] = w.astype(bf16)
            total = total + fold(w, jnp.add)
        part = 1.0 / jnp.sum(total, axis=0, keepdims=True)
        r.part[index] = jnp.broadcast_to(part, (8, 2 * T))
        mixed = nn(turned[cols, :], low_probs[:, cols]) * part
        ycat[CROSS_OUT, rows_q, cols] = unstacked_quad(mixed).astype(bf16)

    def cross_attention(half):
        if half == 0:
            load(r.cross_q).wait()
        rows = pl.ds(half * HALF, HALF)
        for j in range(HL // 256):
            cols = pl.ds(j * 256, 256)
            x = nn(low[rows, :], r.cross_q_v[:, cols]) + r.cross_qv_bias_v[0:1, cols]
            r.query[rows, cols] = x.astype(bf16)
        for g in range(HL // 256):
            cross_quad(half, g)

    def send_second(half):
        if half == 0:
            load(r.cross_out).wait()
        exchange_half(1, half, lambda rows, cols: nn(ycat[CROSS_OUT, rows, :], r.cross_out_v[:, cols]))
        if half == 1:
            copy_y(CROSS_OUT).start()

    def second_norm(half):
        norm_rows(1, half, r.norm, r.unit1)

    def normal_share(h):
        return 0.5 * (1.0 + lax.erf(h * 0.7071067811865476))

    def hidden_units(half):
        if half == 0:
            load(r.fc_in).wait()
        rows = pl.ds(half * HALF, HALF)

        def unit(b):
            for part in range(2):
                j = 2 * b + part
                cols = at(j, 256)
                h = nn(low[rows, :], r.fc_in_v[:, cols]) + r.fc_in_bias_v[:, cols]
                dp_ref[1, pl.ds(j * T + half * HALF, HALF), :] = h
                ycat[FC_OUT + b, rows, pl.ds(part * 256, 256)] = (h * normal_share(h)).astype(bf16)
            copy_y_half(FC_OUT + b, half).start()

        for b in range(FL // W):
            unit(b)

    def slopes(j):
        h = dp_ref[1, at(j, T), :]
        dp_ref[1, at(j, T), :] = normal_share(h) + h * jnp.exp(-0.5 * h * h) * 0.3989422804014327

    def ffn_term(rows, cols):
        total = nn(ycat[FC_OUT, rows, :], r.fc_out_v[pl.ds(0, W), cols])
        for b in range(1, FL // W):
            total = total + nn(ycat[FC_OUT + b, rows, :], r.fc_out_v[pl.ds(b * W, W), cols])
        return total

    def send_third(half):
        if half == 0:
            load(r.fc_out).wait()
        exchange_half(2, half, ffn_term)

    row16 = lax.broadcasted_iota(jnp.int32, (16, D), 0)
    zero8 = jnp.zeros((8, D), f32)

    def sums_of(body, k):
        def step(i, carry):
            g, unit, rounded = body(i)
            return (
                carry[0] + fold(rounded, jnp.add),
                carry[1] + fold(g * unit, jnp.add),
                carry[2] + fold(g, jnp.add),
            )

        carry = (zero8, zero8, zero8)
        for i in range(T // 16):
            carry = step(i, carry)
        bias, gains, shifts = carry
        sm[k : k + 1, :] = col_sum(bias)
        sm[3 + k : 4 + k, :] = col_sum(gains)
        sm[6 + k : 7 + k, :] = col_sum(shifts)

    def output_rows(i):
        if i % (HALF // 16) == 0:
            half_wait(2, i // (HALF // 16))
        rows = at(i, 16)
        v = r.norm[rows, :] + (exchanged(2, rows) + out_bias[2:3, :])
        norm, unit, inv = normalize(v, 2)
        r.layer_out[rows, :] = norm.astype(bf16)
        g = jnp.where(row16 + i * 16 < r.dec_len_v[0], r.cotangent_v[rows, :].astype(f32), 0.0)
        grad = norm_back(g, unit, inv, 2)
        r.grad[rows, :] = grad
        rounded = grad.astype(bf16)
        low[rows, :] = rounded
        return g, unit, rounded.astype(f32)

    def output_norm():
        load(r.cotangent).wait()
        sums_of(output_rows, 2)

    def hidden_grad(j):
        cols = at(j, 256)
        g = nt(low[...], r.fc_out_v[at(j, 256), :]) * dp_ref[1, at(j, T), :]
        rounded = g.astype(bf16)
        ycat[FC_IN + j // 2, 0:T, at(j % 2, 256)] = rounded
        sm[pl.ds(11 + j // 4, 1), at(j % 4, 256)] = col_sum(rounded.astype(f32))

    def hidden_grads():
        for b in range(FL // W):
            hidden_grad(2 * b)
            hidden_grad(2 * b + 1)
            copy_y(FC_IN + b).start()

    def hidden_term(j):
        rows = at(j, 256)
        total = nt(ycat[FC_IN, 0:T, :], r.fc_in_v[rows, pl.ds(0, W)])
        for b in range(1, FL // W):
            total = total + nt(ycat[FC_IN + b, 0:T, :], r.fc_in_v[rows, pl.ds(b * W, W)])
        return total

    def send_fourth():
        exchange_start(3, hidden_term)

    def grad_rows(k, e, unit_ref):
        def body(i):
            rows = at(i, 16)
            g = r.grad[rows, :] + exchanged(e, rows)
            unit = unit_ref[rows, :]
            grad = norm_back(g, unit, r.inv[k, rows, 0:1], k)
            r.grad[rows, :] = grad
            rounded = grad.astype(bf16)
            low[rows, :] = rounded
            return g, unit, rounded.astype(f32)

        exchange_wait(e)
        sums_of(body, k)

    mixed_grad = r.mixed_grad

    def second_back():
        grad_rows(1, 3, r.unit1)

    def mixed_from(weights):
        for j in range(HL // 256):
            mixed_grad[:, at(j, 256)] = nt(low[...], weights[at(j, 256), :]).astype(bf16)

    def cross_mixed_grad():
        mixed_from(r.cross_out_v)

    def cross_back(g):
        cols = pl.ds(g * 256, 256)
        halves = [pl.ds(half * HALF, HALF) for half in range(2)]
        index = [half * (HL // 256) + g for half in range(2)]
        gs = [stacked_quad(mixed_grad[rows, cols]) for rows in halves]
        part = [r.part[i, 0:1, :] for i in index]
        total = [jnp.zeros((8, 2 * T), f32)] * 2
        both = jnp.concatenate(gs, axis=0)
        lanes = [pl.ds(half * 2 * T, 2 * T) for half in range(2)]
        for b in range(ML // BIG):
            big = pl.ds(b * BIG, BIG)
            for half in range(2):
                dbig = nt(value[big, cols], gs[half])
                for i in range(BIG // CH):
                    rows = pl.ds(b * BIG + i * CH, CH)
                    probs = probs_ref[index[half], rows, :] * part[half]
                    dprobs = dbig[i * CH : (i + 1) * CH]
                    dp_ref[half, rows, :] = dprobs
                    probs_ref[index[half], rows, :] = probs
                    total[half] = total[half] + fold(probs * dprobs, jnp.add)
                    low_probs[rows, lanes[half]] = probs.astype(bf16)
            value[big, cols] = nn(low_probs[big, :], both).astype(bf16)
        total = [jnp.sum(x, axis=0, keepdims=True) for x in total]
        both = jnp.concatenate([stacked_quad(r.query[rows, cols]) for rows in halves], axis=0)
        for b in range(ML // BIG):
            big = pl.ds(b * BIG, BIG)
            for half in range(2):
                for i in range(BIG // CH):
                    rows = pl.ds(b * BIG + i * CH, CH)
                    ds = probs_ref[index[half], rows, :] * (dp_ref[half, rows, :] - total[half])
                    low_probs[rows, lanes[half]] = ds.astype(bf16)
            key[big, cols] = (nn(low_probs[big, :], both) * scale).astype(bf16)
        for half in range(2):
            dq = nn(turned[cols, :], low_probs[:, lanes[half]])
            ycat[CROSS_Q, halves[half], cols] = (unstacked_quad(dq) * scale).astype(bf16)

    def send_fifth():
        exchange_start(4, lambda j: nt(ycat[CROSS_Q, 0:T, :], r.cross_q_v[at(j, 256), :]))
        copy_y(CROSS_Q).start()
        sm[10:11, 0:HL] = col_sum(ycat[CROSS_Q, 0:T, :].astype(f32))
        sm[10:11, HL : 2 * HL] = col_sum(value[...].astype(f32))

    def gm_copy(i):
        cols = at(i, 256)
        return remote("gm", i, 4, r.gm_out.at[:, cols], r.gm_in.at[:, cols], to_mp)

    def memory_term(i):
        cols = pl.ds(i * 256, 256)
        for half, to in ((1 - m, r.gm_out), (m, r.grad_memory)):
            rows = at(half, ML // 2)
            x = nt(key[rows, :], r.wkv_v[0, cols, :]) + nt(value[rows, :], r.wkv_v[1, cols, :])
            to[:, cols] = x.astype(bf16)
        gm_copy(i).start()

    def memory_sum(i):
        gm_copy(i).wait()
        cols = pl.ds(i * 256, 256)
        r.grad_memory[:, cols] = (r.grad_memory[:, cols].astype(f32) + r.gm_in[:, cols].astype(f32)).astype(bf16)

    def pair_product(v):
        pair = key if v == 0 else value
        for h in range(2):
            cols = pl.ds(h * 256, 256)
            rhs = pair[:, cols]
            r.kvc_out[v, :, cols] = nn(r.memory_t[at(1 - c, D // 2), :], rhs).astype(bf16)
            r.memory_v[0 : D // 2, pl.ds(v * W + h * 256, 256)] = nn(r.memory_t[at(c, D // 2), :], rhs).astype(bf16)
        kvc_copy(v).start()

    def pair_halve(v):
        kvc_copy(v).wait_recv()
        rows = at(1 - y, 256)
        mine = r.memory_v[rows, pl.ds(v * W, W)].astype(f32)
        r.kvy_out[v] = (mine + r.kvc_in[v, rows, :].astype(f32)).astype(bf16)
        kvy_copy(v).start()

    def first_back():
        grad_rows(0, 4, r.unit0)

    def self_back(p):
        cols = at(p, 128)
        q, k, v = (r.packed[i, :, cols] for i in range(3))
        probs = r.self_probs[p]
        g = stacked(mixed_grad[:, cols])
        dprobs = nt(v, g)
        ycat[QKV + 2, 0:T, cols] = nn(probs.astype(bf16), g).astype(bf16)
        ds = (probs * (dprobs - jnp.sum(probs * dprobs, axis=0, keepdims=True))).astype(bf16)
        ycat[QKV + 1, 0:T, cols] = (nn(ds, stacked(q)) * scale).astype(bf16)
        dq = nn(k.astype(f32).T.astype(bf16), ds)
        ycat[QKV, 0:T, cols] = (unstacked(dq) * scale).astype(bf16)

    def self_grads():
        mixed_from(r.self_out_v)
        loop(PAIRS, self_back, 4)
        for b in range(3):
            copy_y(QKV + b).start()
        sm[9:10, 0:HL] = col_sum(ycat[QKV, 0:T, :].astype(f32))
        sm[9:10, HL : 2 * HL] = col_sum(ycat[QKV + 2, 0:T, :].astype(f32))
        sm[13:16, :] = jnp.zeros((3, D), f32)

    def packed_term(j):
        rows = at(j, 256)
        total = nt(ycat[QKV, 0:T, :], r.wqkv_v[0, rows, :])
        for b in range(1, 3):
            total = total + nt(ycat[QKV + b, 0:T, :], r.wqkv_v[b, rows, :])
        return total

    def send_sixth():
        exchange_start(5, packed_term)

    def token_grads():
        def body(i):
            rows = at(i, 16)
            r.grad_tokens[rows, :] = (r.grad[rows, :] + exchanged(5, rows)).astype(bf16)

        exchange_wait(5)
        loop(T // 16, body, 2)

    doubling = (to_c, to_y, to_z1, to_z2)

    def small_copy(k):
        return remote("small", k, 4, r.sm_out.at[k], r.sm_in.at[k], doubling[k])

    def small_step(k):
        if k > 0:
            small_copy(k - 1).wait()
            (sm if k < 4 else r.sums)[...] = r.sm_out[k - 1].astype(f32) + r.sm_in[k - 1].astype(f32)
        if k < 4:
            r.sm_out[k] = sm[...].astype(bf16)
            small_copy(k).start()

    def each(step, *indices):
        for i in indices:
            step(i)

    project()
    self_attention()
    send_first()
    memory_pair()
    first_norm(0)
    cross_attention(0)
    send_second(0)
    each(turn_memory, 0)
    first_norm(1)
    cross_attention(1)
    send_second(1)
    send_x(X_FIRST, low)
    second_norm(0)
    hidden_units(0)
    send_third(0)
    second_norm(1)
    hidden_units(1)
    send_third(1)
    turn(key)
    each(slopes, 7)
    send_x(X_SECOND, low)
    each(turn_memory, 7)
    each(slopes, 3)
    each(turn_memory, 3)
    each(slopes, 4, 0, 6, 5, 2, 1)
    output_norm()
    hidden_grads()
    send_x(X_FFN, low)
    send_fourth()
    each(product, 4)
    send_x(X_TOKENS, r.tokens_v)
    share_x(X_FFN)
    each(halve, 4)
    each(product, 5)
    second_back()
    cross_mixed_grad()
    send_x(X_CROSS, low)
    each(product, 2)
    each(turn_memory, 6)
    each(halve, 5)
    each(cross_back, 0)
    each(product, 7)
    each(halve_last, 4)
    each(halve, 2)
    each(cross_back, 1)
    send_fifth()
    each(halve, 7)
    each(product, 6, 3, 1)
    share_x(X_CROSS)
    each(halve_last, 5)
    each(halve, 3)
    each(halve_last, 2)
    each(turn_memory, 4)
    each(halve, 6)
    each(product, 0)
    each(memory_term, 3)
    each(halve, 1)
    each(turn_memory, 2)
    first_back()
    self_grads()
    each(halve_last, 7)
    each(total, 5)
    each(halve, 0)
    each(small_step, 0)
    each(product, 9)
    each(halve_last, 3)
    each(turn_memory, 5)
    each(product, 8)
    each(memory_term, 2)
    send_x(X_SELF, low)
    each(halve, 9)
    each(small_step, 1)
    each(product, 11)
    each(turn_memory, 1)
    each(halve_last, 1, 6)
    each(memory_sum, 2)
    each(total, 3)
    each(halve, 11)
    each(total, 4)
    each(pair_product, 1, 0)
    each(product, 12)
    each(halve_last, 9)
    share_x(X_SELF)
    each(memory_term, 1)
    each(product, 13)
    each(halve, 8)
    each(halve_last, 0)
    each(pair_halve, 1)
    each(halve, 12, 13)
    send_sixth()
    each(small_step, 2)
    each(pair_halve, 0)
    each(product, 10)
    each(halve_last, 8, 11)
    each(total, 2, 1, 6)
    each(halve, 10, 15)
    token_grads()
    each(memory_term, 0)
    each(halve_last, 13, 12)
    each(total, 7)
    each(halve, 14)
    each(halve_last, 10)
    each(total, 8)
    each(small_step, 3)
    each(halve_last, 15)
    each(memory_sum, 1)
    each(total, 10, 13, 9)
    each(halve_last, 14)
    each(memory_sum, 0)
    each(total, 15, 11)
    each(small_step, 4)
    each(total, 12, 0)
    each(memory_sum, 3)
    each(total, 14)
    for w in range(6):
        copy_x(w).wait_send()
        if x_axis(w) == AXIS_Z:
            copy_shared(w, m).wait_send()
    for u in range(UNITS):
        if u < KV:
            for copy in gathers(u):
                copy.wait_send()
            copy_core(u).wait_send()
        copy_half(u).wait_send()
        copy_last(u).wait_send()
    for v in range(2):
        kvc_copy(v).wait_send()
        kvy_copy(v).wait_send()
    refs_at.update(remote=sum(n for _, n in given.values()), local=sum(n for _, n in local_given.values()))


REMOTE_SEMS = 160
LAYER_VMEM = 59 * 2**20
LOCAL_SEMS = 64


def layer(tokens, memory, mem_len, dec_len, cotangent, wqkv, self_qv_bias, self_out, cross_q, cross_kv, cross_qv_bias, cross_out, fc_in, fc_in_bias, fc_out, out_bias, norm_gain, norm_bias):
    T, D = tokens.shape
    ML = memory.shape[0]
    HL = self_out.shape[0]
    FL = fc_out.shape[0]
    R = D // GROUP
    W = 512
    PAIRS = HL // 128
    anywhere = pl.BlockSpec(memory_space=pl.ANY)
    big = dict(tokens=tokens, memory=memory, cotangent=cotangent, wqkv=wqkv, self_out=self_out, cross_q=cross_q, cross_kv=cross_kv,
               cross_out=cross_out, fc_in=fc_in, fc_out=fc_out)
    small = dict(self_qv_bias=self_qv_bias, cross_qv_bias=cross_qv_bias, fc_in_bias=fc_in_bias, out_bias=out_bias,
                 norm_gain=norm_gain, norm_bias=norm_bias)
    scalars = dict(mem_len=mem_len, dec_len=dec_len)
    outs = dict(
        layer_out=((T, D), bf16),
        grad_tokens=((T, D), bf16),
        grad_memory=((ML // 2, D), bf16),
        g_qkv=((3, R, HL), f32),
        g_self_out=((R, HL), f32),
        g_cross_q=((R, HL), f32),
        g_kv=((2, R, HL), f32),
        g_cross_out=((R, HL), f32),
        g_fc_in=((R, FL), f32),
        g_fc_out=((R, FL), f32),
        sums=((16, D), f32),
    )
    scratch = {name + "_v": (x.shape, x.dtype) for name, x in (big | small).items()}
    scratch |= dict(
        wkv_v=((2, D, HL), bf16),
        packed=((3, T, HL), bf16),
        self_probs=((PAIRS, T, 2 * T), f32),
        low=((T, D), bf16),
        ycat=((KV, 2 * T, W), bf16),
        xcat=((6, 512, 256), bf16),
        xsend=((6, 512, 128), bf16),
        ex_out=((2, T, D), bf16),
        ex_in=((2, T, D), bf16),
        norm=((T, D), f32),
        unit0=((T, D), f32),
        unit1=((T, D), f32),
        inv=((2, T, 128), f32),
        grad=((T, D), f32),
        key=((ML, HL), bf16),
        value=((ML, HL), bf16),
        turned=((HL, ML), bf16),
        query=((T, HL), bf16),
        mixed_grad=((T, HL), bf16),
        probs=((PAIRS, ML, 2 * T), f32),
        part=((PAIRS, 8, 2 * T), f32),
        low_probs=((ML, 4 * T), bf16),
        dp=((2, ML, 2 * T), f32),
        memory_t=((D, ML), bf16),
        gm_out=((ML // 2, D), bf16),
        gm_in=((ML // 2, D), bf16),
        core_in=((KV, 256, W), bf16),
        kvc_out=((2, 512, W), bf16),
        kvc_in=((2, 512, W), bf16),
        kvy_out=((2, 256, W), bf16),
        kvy_in=((2, 256, W), bf16),
        half_out=((UNITS, 128, W), bf16),
        half_in=((UNITS, 128, W), bf16),
        last_out=((UNITS, 64, W), bf16),
        last_in=((UNITS, 64, W), bf16),
        sm=((16, D), f32),
        sm_out=((4, 16, D), bf16),
        sm_in=((4, 16, D), bf16),
    )
    sems = dict(send_sem=REMOTE_SEMS, recv_sem=REMOTE_SEMS, local_sem=LOCAL_SEMS)
    lengths = {name + "_v": pltpu.SMEM((1,), jnp.int32) for name in scalars}
    names = [*big, *small, *scalars, *outs, *scratch, *lengths, *sems]
    got = {}
    out = pl.pallas_call(
        functools.partial(kernel, names, got),
        out_shape=[pltpu.VMEM(s, t) for s, t in outs.values()],
        in_specs=[anywhere] * (len(big) + len(small) + len(scalars)),
        out_specs=[pl.BlockSpec(memory_space=pltpu.VMEM)] * len(outs),
        scratch_shapes=[pltpu.VMEM(s, t) for s, t in scratch.values()]
        + [*lengths.values()]
        + [pltpu.SemaphoreType.DMA((count,)) for count in sems.values()],
        compiler_params=pltpu.CompilerParams(
            collective_id=0, has_side_effects=True, vmem_limit_bytes=LAYER_VMEM
        ),
        name="layer",
    )(*big.values(), *small.values(), *scalars.values())
    assert got["remote"] <= REMOTE_SEMS and got["local"] <= LOCAL_SEMS, got
    return types.SimpleNamespace(**dict(zip(outs, out)))


def finish_kernel(count, small, *refs):
    ins, outs, scratch = refs[: count + 2], refs[count + 2 : 2 * count + 3 + small], refs[2 * count + 3 + small :]
    turned, made, sem = scratch[0], scratch[1:-1], scratch[-1]
    stores = [
        pltpu.make_async_copy(a, b, sem.at[i]) for i, (a, b) in enumerate(zip((*ins[:count], turned, *made), outs))
    ]
    for i in range(count):
        stores[i].start()
    kv, sums = ins[count:]
    for part in range(2):
        turned[:, part, :] = kv[part]
    stores[count].start()
    self_bias, cross_bias, hidden_bias, out_bias, gains, shifts = made
    width = self_bias.shape[1]
    for row, to in ((9, self_bias), (10, cross_bias)):
        for part in range(2):
            to[part : part + 1, :] = sums[row : row + 1, part * width : (part + 1) * width]
    features = sums.shape[1]
    for part in range(hidden_bias.shape[1] // features):
        hidden_bias[:, part * features : (part + 1) * features] = sums[11 + part : 12 + part, :]
    for first, to in ((0, out_bias), (3, gains), (6, shifts)):
        to[...] = sums[first : first + 3, :]
    for i in range(small):
        stores[count + 1 + i].start()
    for store in stores:
        store.wait()


def finish(whole, kv, sums):
    R, HL = kv.shape[1:]
    D = sums.shape[1]
    anywhere = pl.BlockSpec(memory_space=pl.ANY)
    in_vmem = pl.BlockSpec(memory_space=pltpu.VMEM)
    small = [(2, HL), (2, HL), (1, 4 * HL), (3, D), (3, D), (3, D)]
    return pl.pallas_call(
        functools.partial(finish_kernel, len(whole), len(small)),
        out_shape=[jax.ShapeDtypeStruct(x.shape, x.dtype) for x in whole]
        + [jax.ShapeDtypeStruct((R, 2, HL), f32)]
        + [jax.ShapeDtypeStruct(shape, f32) for shape in small],
        in_specs=[in_vmem] * (len(whole) + 2),
        out_specs=[anywhere] * (len(whole) + 1 + len(small)),
        scratch_shapes=[pltpu.VMEM(shape, f32) for shape in [(R, 2, HL), *small]]
        + [pltpu.SemaphoreType.DMA((len(whole) + 1 + len(small),))],
        compiler_params=pltpu.CompilerParams(vmem_limit_bytes=8 * 2**20),
        name="finish",
    )(*whole, kv, sums)


def per_device(tokens, memory, mem_len, dec_len, cotangent, self_qkv, self_qv_bias, self_out, cross_q, cross_kv, cross_qv_bias, cross_out, fc_in, fc_in_bias, fc_out, out_bias, norm_gain, norm_bias):
    D = tokens.shape[1]
    devices = lax.axis_size("dp")
    outer = devices // GROUP

    def regroup(x, axis, there):
        if outer == 1:
            return x
        sizes = (outer, GROUP) if there else (GROUP, outer)
        shape = x.shape
        x = x.reshape(shape[:axis] + sizes + (D // devices,) + shape[axis + 1 :])
        return jnp.swapaxes(x, axis, axis + 1).reshape(shape)

    tokens, memory, cotangent, self_out, cross_out, fc_out, out_bias, norm_gain, norm_bias = (
        regroup(x, 1, True)
        for x in (tokens, memory, cotangent, self_out, cross_out, fc_out, out_bias, norm_gain, norm_bias)
    )
    self_qkv, cross_q, cross_kv, fc_in = (regroup(x, 0, True) for x in (self_qkv, cross_q, cross_kv, fc_in))
    got = layer(
        tokens, memory, mem_len, dec_len, cotangent, self_qkv.transpose(1, 0, 2), self_qv_bias, self_out, cross_q,
        cross_kv, cross_qv_bias, cross_out, fc_in, fc_in_bias.reshape(1, -1), fc_out, out_bias,
        norm_gain, norm_bias,
    )
    groups = [[o * GROUP + i for o in range(outer)] for i in range(GROUP)]

    def spread(x, axis):
        if outer == 1:
            return x
        return lax.psum_scatter(x, "dp", scatter_dimension=axis, axis_index_groups=groups, tiled=True)

    (
        layer_out, grad_tokens, grad_memory, qkv, self_out, cross_q, cross_out, fc_in, fc_out, kv,
        self_bias, cross_bias, hidden_bias, out_bias, gains, shifts,
    ) = finish(
        (
            got.layer_out, got.grad_tokens, got.grad_memory, got.g_qkv, got.g_self_out, got.g_cross_q, got.g_cross_out,
            got.g_fc_in, got.g_fc_out,
        ),
        got.g_kv,
        got.sums,
    )
    small = (self_bias, cross_bias, hidden_bias, out_bias, gains, shifts)
    if outer > 1:
        small = lax.psum(small, "dp", axis_index_groups=groups)
    self_bias, cross_bias, hidden_bias, out_bias, gains, shifts = small
    return (
        regroup(layer_out, 1, False),
        regroup(grad_tokens, 1, False),
        regroup(grad_memory, 1, False),
        spread(qkv, 1).transpose(1, 0, 2),
        self_bias,
        spread(self_out, 0).T,
        spread(cross_q, 0),
        spread(kv, 0),
        cross_bias,
        spread(cross_out, 0).T,
        spread(fc_in, 0),
        hidden_bias.reshape(-1),
        spread(fc_out, 0).T,
        regroup(out_bias, 1, False),
        regroup(gains, 1, False),
        regroup(shifts, 1, False),
    )


def solution(mesh):
    placed = (
        P("dp", None),
        P("dp", None),
        P("dp"),
        P("dp"),
        P("dp", None),
        P(None, None, "mp"),
        P(None, "mp"),
        P("mp", None),
        P(None, "mp"),
        P(None, None, "mp"),
        P(None, "mp"),
        P("mp", None),
        P(None, "mp"),
        P("mp"),
        P("mp", None),
        P(),
        P(),
        P(),
    )
    return jax.shard_map(
        per_device,
        mesh=mesh,
        in_specs=placed,
        out_specs=(
            P("dp", None),
            P("dp", None),
            P(("dp", "mp"), None),
            P("dp", None, "mp"),
            P(None, "mp"),
            P("mp", "dp"),
            P("dp", "mp"),
            P("dp", None, "mp"),
            P(None, "mp"),
            P("mp", "dp"),
            P("dp", "mp"),
            P("mp"),
            P("mp", "dp"),
            P(),
            P(),
            P(),
        ),
        check_vma=False,
    )
```
